32 devices in a mesh: seq: 4 (over x, core), rep: 8 (over z, y).
Axes of the slice: x: 2, y: 2, z: 4, core: 2. Of those that a mesh axis runs over, the one named last changes fastest.
Arguments:
- tokens: bfloat16 [8, 512, 2048], P('rep', 'seq'), may hold values from -6 to 6
- segment_ids: int32 [8, 512], P('rep', 'seq'), may hold values from 0 to 5, never falling along the last dimension, each value on 1 to 256 neighbouring positions
- cotangent: bfloat16 [8, 512, 2048], P('rep', 'seq'), may hold values from -6 to 6
- attn_gain: bfloat16 [2048], P(('seq', 'rep')), may hold values from 0.099609375 to 1.8984375
- w_qkv: bfloat16 [2048, 1920], P(('seq', 'rep')), may hold values from -0.125 to 0.125
- w_out: bfloat16 [2048, 1280], P(('seq', 'rep')), may hold values from -0.5 to 0.5
- ffn_gain: bfloat16 [2048], P(('seq', 'rep')), may hold values from 0.099609375 to 1.8984375
- w_gate: bfloat16 [2048, 3584], P(('seq', 'rep')), may hold values from -0.125 to 0.125
- w_up: bfloat16 [2048, 3584], P(('seq', 'rep')), may hold values from -0.125 to 0.125
- w_down: bfloat16 [2048, 3584], P(('seq', 'rep')), may hold values from -0.09375 to 0.09375
- q_gain: bfloat16 [64], replicated, may hold values from 0.099609375 to 1.8984375
- k_gain: bfloat16 [64], replicated, may hold values from 0.099609375 to 1.8984375
Outputs:
- activations: bfloat16 [8, 512, 2048], P('rep', 'seq')
- grad_tokens: float32 [8, 512, 2048], P('rep', 'seq')
- grad_attn_gain: float32 [2048], P(('seq', 'rep'))
- grad_qkv: float32 [2048, 1920], P(('seq', 'rep'))
- grad_out: float32 [2048, 1280], P(('seq', 'rep'))
- grad_ffn_gain: float32 [2048], P(('seq', 'rep'))
- grad_gate: float32 [2048, 3584], P(('seq', 'rep'))
- grad_up: float32 [2048, 3584], P(('seq', 'rep'))
- grad_down: float32 [2048, 3584], P(('seq', 'rep'))
- grad_q_gain: float32 [64], replicated
- grad_k_gain: float32 [64], replicated
The draws below stay inside these ranges and needn't reach their ends.
All inputs are finite; a program needn't handle non-finite values.
Results may differ from the reference program's by a relative error of at most 0.015.
Values may be sent and summed in bfloat16 or wider, within the bound.
A program may use at most 384 MiB of HBM per device.

```python
import math
import jax
import jax.numpy as jnp
import numpy as np
from jax import lax

D = 2048
QH = 20
KVG = 5
HD = 64
FF = 3584
LEN = 512
ROWS = 8
QW = 1280
KW = 320
QKVW = 1920


def steps_of(key, shape, cuts, least, high):
    loudness, own = 1.0, jax.random.fold_in(key, 6)
    for axis_at, blocks in cuts:
        draws = jnp.exp(jax.random.uniform(jax.random.fold_in(own, axis_at), (blocks,), jnp.float32, least / len(cuts), high / len(cuts)))
        loudness = loudness * jnp.repeat(draws, shape[axis_at] // blocks).reshape([-1 if axis == axis_at else 1 for axis in range(len(shape))])
    return loudness


def split_up(amount, total, most, lean):
    loads = [(1 << 20) // math.isqrt(standing ** lean) + 1 for standing in range(2, amount + 1)]
    spare, holding = total - most - (amount - 1), [1] * (amount - 1)
    while spare > 0:
        movable = [i for i in range(amount - 1) if holding[i] < most]
        mass, remaining = sum([loads[i] for i in movable]), spare
        for i in movable:
            extra = min(most - holding[i], max(1, remaining * loads[i] // mass), spare)
            holding[i] = holding[i] + extra
            spare = spare - extra
    return np.array([most] + holding)


def ragged_sizes(stream_key, amount, total, reach, slope):
    if amount == 2:
        one = jax.random.randint(stream_key, (), max(1, total - reach), min(reach, total - 1) + 1)
        return jnp.stack([one, total - one])
    tallies = jnp.asarray(split_up(amount, total, reach, slope), jnp.int32)
    twos = (amount - 1) // 2
    source_of, taker = tallies[1:1 + 2 * twos:2], tallies[2:2 + 2 * twos:2]
    margin = jnp.minimum(source_of - 1, reach - taker)
    shifted = jax.random.randint(jax.random.fold_in(stream_key, 1), (twos,), 0, 1 << 20) % (margin + 1)
    tallies = tallies.at[1:1 + 2 * twos:2].set(source_of - shifted).at[2:2 + 2 * twos:2].set(taker + shifted)
    return tallies[jax.random.permutation(jax.random.fold_in(stream_key, 2), amount)]


def centred(rng, dims, deviation, most, shards=(), held_as=jnp.bfloat16):
    values = deviation * jax.random.normal(rng, dims, jnp.float32)
    if shards:
        values = values * steps_of(rng, dims, shards, -0.22, 0.18)
    return jnp.clip(values, -most, most).astype(held_as)


def setup_inputs(seed: int = 0) -> dict:
    key_of = jax.random.split(jax.random.key(seed), 13)
    return {
        "tokens": centred(key_of[0], (ROWS, LEN, D), 1.0, 6.0, ((0, 8), (1, 4))),
        "segment_ids": jax.vmap(lambda own: jnp.searchsorted(jnp.cumsum(ragged_sizes(own, 6, LEN, LEN // 2, 2)), jnp.arange(LEN), side="right"))(jax.random.split(key_of[1], ROWS)).reshape((ROWS, LEN)).astype(jnp.int32),
        "cotangent": centred(key_of[2], (ROWS, LEN, D), 1.0, 6.0, ((0, 8), (1, 4))),
        "attn_gain": jnp.clip(1.0 + 0.18 * jax.random.normal(key_of[3], (D,), jnp.float32), 0.099609375, 1.8984375).astype(jnp.bfloat16),
        "w_qkv": centred(key_of[4], (D, QKVW), D ** -0.5, 0.125, ((0, 32),)),
        "w_out": centred(key_of[5], (D, QW), (QW * 64 // LEN) ** -0.5, 0.5, ((0, 32),)),
        "ffn_gain": jnp.clip(1.0 + 0.18 * jax.random.normal(key_of[6], (D,), jnp.float32), 0.099609375, 1.8984375).astype(jnp.bfloat16),
        "w_gate": centred(key_of[7], (D, FF), D ** -0.5, 0.125, ((0, 32),)),
        "w_up": centred(key_of[8], (D, FF), D ** -0.5, 0.125, ((0, 32),)),
        "w_down": centred(key_of[9], (D, FF), FF ** -0.5, 0.09375, ((0, 32),)),
        "q_gain": jnp.clip(1.0 + 0.18 * jax.random.normal(key_of[10], (HD,), jnp.float32), 0.099609375, 1.8984375).astype(jnp.bfloat16),
        "k_gain": jnp.clip(1.0 + 0.18 * jax.random.normal(key_of[11], (HD,), jnp.float32), 0.099609375, 1.8984375).astype(jnp.bfloat16),
    }


@jax.custom_vjp
def low(v):
    return lax.optimization_barrier(v.astype(jnp.bfloat16)).astype(jnp.float32)

@jax.custom_vjp
def low_back(v):
    return v

def low_keep(v):
    return (low(v), None)

def low_pass(kept, grad):
    return (grad,)

def back_keep(v):
    return (v, None)

def back_low(kept, grad):
    return (low(grad),)
low.defvjp(low_keep, low_pass)
low_back.defvjp(back_keep, back_low)
norm_eps = 1e-06
rope_base = 10000.0

def matmul(left, right):
    return jnp.dot(left, right, precision=lax.Precision.HIGHEST, preferred_element_type=jnp.float32)

def norm_rows(value_matrix, gain):
    return value_matrix * lax.rsqrt(lax.optimization_barrier(jnp.mean(value_matrix * value_matrix, axis=-1, keepdims=True)) + norm_eps) * gain

def rotate_heads(value_matrix, positions):
    half = value_matrix.shape[-1] // 2
    freqs = rope_base ** (-jnp.arange(half, dtype=jnp.float32) * 2.0 / value_matrix.shape[-1])
    angles = positions.astype(jnp.float32)[:, None] * freqs[None, :]
    cosine = jnp.cos(angles)[:, None, :]
    sine = jnp.sin(angles)[:, None, :]
    first = value_matrix[..., :half]
    second = value_matrix[..., half:]
    return jnp.concatenate([first * cosine - second * sine, second * cosine + first * sine], axis=-1)

def heads_prep(qkv, q_scale, k_scale, positions):
    count = qkv.shape[0]
    query = qkv[:, :QW].reshape(count, QH, HD)
    key = qkv[:, QW:QW + KW].reshape(count, KVG, HD)
    value = qkv[:, QW + KW:].reshape(count, KVG, HD)
    query = rotate_heads(norm_rows(query, q_scale), positions)
    key = rotate_heads(norm_rows(key, k_scale), positions)
    return (query, key, value)

def attend(query, key, value, seg_row):
    length = query.shape[0]
    block = min(512, length)
    per_group = QH // KVG
    score_scale = HD ** (-0.5)
    q_heads = query.transpose(1, 0, 2)
    k_heads = jnp.repeat(key.transpose(1, 0, 2), per_group, axis=0)
    v_heads = jnp.repeat(value.transpose(1, 0, 2), per_group, axis=0)
    cols = jnp.arange(length, dtype=jnp.int32)

    def one_block(start):
        query_block = lax.dynamic_slice_in_dim(q_heads, start, block, 1)
        rows = start + jnp.arange(block, dtype=jnp.int32)
        seg_blk = lax.dynamic_slice_in_dim(seg_row, start, block, 0)
        allowed = (cols[None, :] <= rows[:, None]) & (seg_row[None, :] == seg_blk[:, None])
        logit_scores = low_back(jnp.einsum('hqd,hkd->hqk', query_block, k_heads, precision=lax.Precision.HIGHEST) * score_scale)
        logit_scores = jnp.where(allowed[None], logit_scores, -1e+30)
        attention_probabilities = low(jax.nn.softmax(logit_scores, axis=-1))
        return jnp.einsum('hqk,hkd->qhd', attention_probabilities, v_heads, precision=lax.Precision.HIGHEST)
    starts = jnp.arange(0, length, block, dtype=jnp.int32)
    blocks = lax.map(jax.checkpoint(one_block), starts)
    return blocks.reshape(length, QH, HD)

def row_forward(x_row, seg_row, gain_a, qkv_w, out_w, gain_b, gate_w, up_w, down_w, q_scale, k_scale):
    length = x_row.shape[0]
    index = jnp.arange(length, dtype=jnp.int32)
    earlier = lax.optimization_barrier(jnp.sum((seg_row[None, :] < seg_row[:, None]).astype(jnp.int32), axis=1))
    positions = index - earlier
    normed = low(norm_rows(x_row, gain_a))
    qkv = low_back(matmul(normed, qkv_w))
    query, key, value = heads_prep(qkv, q_scale, k_scale, positions)
    query = low(low_back(query))
    key = low(low_back(key))
    value = low(low_back(value))
    mixed = attend(query, key, value, seg_row)
    mixed = low(low_back(mixed.reshape(length, QW)))
    hidden = x_row + low_back(matmul(mixed, out_w.T))
    normed_two = low(norm_rows(hidden, gain_b))
    gate = low_back(matmul(normed_two, gate_w))
    upward = low_back(matmul(normed_two, up_w))
    active = low(jax.nn.silu(gate) * upward)
    return hidden + low_back(matmul(active, down_w.T))

def reference(tokens, segment_ids, cotangent, attn_gain, w_qkv, w_out, ffn_gain, w_gate, w_up, w_down, q_gain, k_gain):
    params = (attn_gain.astype(jnp.float32), w_qkv.astype(jnp.float32), w_out.astype(jnp.float32), ffn_gain.astype(jnp.float32), w_gate.astype(jnp.float32), w_up.astype(jnp.float32), w_down.astype(jnp.float32), q_gain.astype(jnp.float32), k_gain.astype(jnp.float32))

    def forward(x_all, weights):

        def step(carry, item):
            x_row, seg_row = item
            out_row = jax.checkpoint(row_forward)(x_row, seg_row, weights[0], weights[1], weights[2], weights[3], weights[4], weights[5], weights[6], weights[7], weights[8])
            return (carry, out_row)
        carry, rows_out = lax.scan(step, jnp.zeros((), jnp.float32), (x_all, segment_ids))
        return rows_out
    layer_result, pullback = jax.vjp(forward, tokens.astype(jnp.float32), params)
    d_tokens, d_params = pullback(cotangent.astype(jnp.float32))
    return (layer_result.astype(jnp.bfloat16), d_tokens, d_params[0], d_params[1], d_params[2], d_params[3], d_params[4], d_params[5], d_params[6], d_params[7], d_params[8])
```

```python
import jax
import jax.numpy as jnp
from jax import lax
from jax.experimental import pallas as pl
from jax.experimental.pallas import tpu as pltpu
from jax.sharding import PartitionSpec as P

QH = 20
KVG = 5
HD = 64
QW = 1280
KW = 320


norm_eps = 1e-06
rope_base = 10000.0


def norm_rows(value_matrix, gain):
    return (
        value_matrix
        * lax.rsqrt(jnp.mean(value_matrix * value_matrix, axis=-1, keepdims=True) + norm_eps)
        * gain
    )


def rotate_heads(value_matrix, positions):
    half = value_matrix.shape[-1] // 2
    freqs = rope_base ** (-jnp.arange(half, dtype=jnp.float32) * 2.0 / value_matrix.shape[-1])
    angles = positions.astype(jnp.float32)[:, None] * freqs[None, :]
    cosine = jnp.cos(angles)[:, None, :]
    sine = jnp.sin(angles)[:, None, :]
    first = value_matrix[..., :half]
    second = value_matrix[..., half:]
    return jnp.concatenate(
        [first * cosine - second * sine, second * cosine + first * sine], axis=-1
    )


def heads_prep(qkv, q_scale, k_scale, positions):
    count = qkv.shape[0]
    query = qkv[:, :QW].reshape(count, QH, HD)
    key = qkv[:, QW : QW + KW].reshape(count, KVG, HD)
    value = qkv[:, QW + KW :].reshape(count, KVG, HD)
    query = rotate_heads(norm_rows(query, q_scale), positions)
    key = rotate_heads(norm_rows(key, k_scale), positions)
    return (query, key, value)


def times_rows(left, right):
    return lax.dot_general(
        left, right, (((1,), (1,)), ((), ())), preferred_element_type=jnp.float32
    )


def token_sum(left, right):
    return lax.dot_general(
        left, right, (((0,), (0,)), ((), ())), preferred_element_type=jnp.float32
    )


def block_scores(query_block, key_matrix, seg_row, start, score_scale):
    width = query_block.shape[1]
    length = key_matrix.shape[1]
    logit_scores = (
        jnp.einsum("zjfr,zyr->zfjy", query_block, key_matrix, preferred_element_type=jnp.float32)
        * score_scale
    )
    rows = start + jnp.arange(width, dtype=jnp.int32)
    cols = jnp.arange(length, dtype=jnp.int32)
    seg_blk = lax.dynamic_slice_in_dim(seg_row, start, width, 1)
    allowed = (cols[None, None, :] <= rows[None, :, None]) & (
        seg_row[:, None, :] == seg_blk[:, :, None]
    )
    return jnp.where(allowed[:, None], logit_scores, -1e30)


def attend_forward(query, key_matrix, value_matrix, seg_row, block):
    length = key_matrix.shape[1]
    score_scale = HD ** (-0.5)

    def one_block(start):
        query_block = lax.dynamic_slice_in_dim(query, start, block, 1)
        logit_scores = block_scores(query_block, key_matrix, seg_row, start, score_scale)
        top = jnp.max(logit_scores, axis=-1, keepdims=True)
        weights = jnp.exp(logit_scores - top)
        total = jnp.sum(weights, axis=-1, keepdims=True)
        attention_probabilities = (weights / total).astype(jnp.bfloat16)
        layer_result = jnp.einsum(
            "szjr,srn->sjzn",
            attention_probabilities,
            value_matrix,
            preferred_element_type=jnp.float32,
        )
        return (layer_result.astype(jnp.bfloat16), (top + jnp.log(total))[..., 0])

    starts = jnp.arange(0, length, block, dtype=jnp.int32)
    return lax.map(one_block, starts)


def attend_backward(query, key_matrix, value_matrix, seg_row, grads_out, lse, block):
    length = key_matrix.shape[1]
    score_scale = HD ** (-0.5)

    def one_block(carry, item):
        d_key, d_value = carry
        start, sums = item
        query_block = lax.dynamic_slice_in_dim(query, start, block, 1)
        gradient_block = lax.dynamic_slice_in_dim(grads_out, start, block, 1)
        logit_scores = block_scores(query_block, key_matrix, seg_row, start, score_scale)
        attention_probabilities = jnp.exp(logit_scores - sums[..., None])
        reduced_probabilities = attention_probabilities.astype(jnp.bfloat16)
        d_value = d_value + jnp.einsum(
            "syer,seyo->sro",
            reduced_probabilities,
            gradient_block,
            preferred_element_type=jnp.float32,
        )
        probability_gradient = jnp.einsum(
            "zjfr,zyr->zfjy", gradient_block, value_matrix, preferred_element_type=jnp.float32
        )
        inner = jnp.sum(attention_probabilities * probability_gradient, axis=-1, keepdims=True)
        score_gradient = (attention_probabilities * (probability_gradient - inner)).astype(
            jnp.bfloat16
        )
        d_query = (
            jnp.einsum(
                "szjr,srn->sjzn", score_gradient, key_matrix, preferred_element_type=jnp.float32
            )
            * score_scale
        )
        d_key = (
            d_key
            + jnp.einsum(
                "syer,seyo->sro", score_gradient, query_block, preferred_element_type=jnp.float32
            )
            * score_scale
        )
        return ((d_key, d_value), d_query)

    starts = jnp.arange(0, length, block, dtype=jnp.int32)
    zeros = jnp.zeros(key_matrix.shape, jnp.float32)
    carry, d_query = lax.scan(one_block, (zeros, zeros), (starts, lse))
    return (d_query, carry[0], carry[1])


def shards(
    tokens,
    segment_ids,
    cotangent,
    attn_gain,
    w_qkv,
    w_out,
    ffn_gain,
    w_gate,
    w_up,
    w_down,
    q_gain,
    k_gain,
):
    groups = lax.axis_size("seq")
    rows_dev, len_dev, width = tokens.shape
    count = rows_dev * len_dev
    per_group = QH // KVG
    places = (KVG + groups - 1) // groups * groups
    place_dev = places // groups
    length = len_dev * groups
    block = min(512, length)
    items = rows_dev * place_dev
    gain_one, qkv_w, out_w, gain_two, gate_w, up_w, down_w = (
        lax.all_gather(attn_gain, ("seq", "rep"), axis=0, tiled=True),
        lax.all_gather(w_qkv, ("seq", "rep"), axis=0, tiled=True),
        lax.all_gather(w_out, ("seq", "rep"), axis=0, tiled=True),
        lax.all_gather(ffn_gain, ("seq", "rep"), axis=0, tiled=True),
        lax.all_gather(w_gate, ("seq", "rep"), axis=0, tiled=True),
        lax.all_gather(w_up, ("seq", "rep"), axis=0, tiled=True),
        lax.all_gather(w_down, ("seq", "rep"), axis=0, tiled=True),
    )
    row_seg = lax.all_gather(segment_ids, "seq", axis=1, tiled=True)
    offset = lax.axis_index("seq") * len_dev
    earlier = jnp.sum((row_seg[:, None, :] < segment_ids[:, :, None]).astype(jnp.int32), axis=2)
    positions = (offset + jnp.arange(len_dev, dtype=jnp.int32)[None, :] - earlier).reshape(count)
    seg_items = jnp.repeat(row_seg, place_dev, axis=0)
    x_rows = tokens.reshape(count, width).astype(jnp.float32)
    gain_a = gain_one.astype(jnp.float32)
    gain_b = gain_two.astype(jnp.float32)
    q_scale = q_gain.astype(jnp.float32)
    k_scale = k_gain.astype(jnp.float32)
    normed = norm_rows(x_rows, gain_a).astype(jnp.bfloat16)
    qkv = jnp.dot(normed, qkv_w, preferred_element_type=jnp.float32)
    query, key, value = heads_prep(qkv, q_scale, k_scale, positions)
    packed = jnp.concatenate(
        [query.reshape(count, KVG, per_group * HD), key, value], axis=2
    ).astype(jnp.bfloat16)
    packed = jnp.pad(packed, ((0, 0), (0, places - KVG), (0, 0))).reshape(
        rows_dev, len_dev, places, -1
    )
    arrived = lax.all_to_all(packed, "seq", split_axis=2, concat_axis=1, tiled=True)
    arrived = arrived.transpose(0, 2, 1, 3).reshape(items, length, -1)
    q_heads = arrived[..., : per_group * HD].reshape(items, length, per_group, HD)
    k_heads = arrived[..., per_group * HD : (per_group + 1) * HD]
    v_heads = arrived[..., (per_group + 1) * HD :]
    outs, lse = attend_forward(q_heads, k_heads, v_heads, seg_items, block)
    attended = (
        outs.transpose(1, 0, 2, 3, 4)
        .reshape(rows_dev, place_dev, length, per_group * HD)
        .transpose(0, 2, 1, 3)
    )
    returned = lax.all_to_all(attended, "seq", split_axis=1, concat_axis=2, tiled=True)
    mixed = returned[:, :, :KVG].reshape(count, QW)
    hidden = x_rows + times_rows(mixed, out_w)
    normed_two = norm_rows(hidden, gain_b).astype(jnp.bfloat16)
    d_result = cotangent.reshape(count, width).astype(jnp.float32)
    gate = jnp.dot(normed_two, gate_w, preferred_element_type=jnp.float32)
    upward = jnp.dot(normed_two, up_w, preferred_element_type=jnp.float32)
    active = (jax.nn.silu(gate) * upward).astype(jnp.bfloat16)
    layer_result = hidden + times_rows(active, down_w)
    d_branch = d_result.astype(jnp.bfloat16)
    d_active = jnp.dot(d_branch, down_w, preferred_element_type=jnp.float32)
    grad_down = token_sum(d_branch, active)
    swiglu_out, swiglu_back = jax.vjp(
        lambda gate_in, up_in: jax.nn.silu(gate_in) * up_in, gate, upward
    )
    d_gate, d_up = swiglu_back(d_active)
    d_gate = d_gate.astype(jnp.bfloat16)
    d_up = d_up.astype(jnp.bfloat16)
    grad_gate = token_sum(normed_two, d_gate)
    grad_up = token_sum(normed_two, d_up)
    d_normed_two = times_rows(d_gate, gate_w) + times_rows(d_up, up_w)
    activations = layer_result.astype(jnp.bfloat16).reshape(rows_dev, len_dev, width)
    second_out, second_back = jax.vjp(norm_rows, hidden, gain_b)
    d_hidden, grad_gain_b = second_back(d_normed_two)
    d_hidden = d_hidden + d_result
    d_attn = d_hidden.astype(jnp.bfloat16)
    grad_out = token_sum(d_attn, mixed)
    d_mixed = jnp.dot(d_attn, out_w, preferred_element_type=jnp.float32).astype(jnp.bfloat16)
    d_pack = jnp.pad(
        d_mixed.reshape(count, KVG, per_group * HD), ((0, 0), (0, places - KVG), (0, 0))
    )
    d_pack = d_pack.reshape(rows_dev, len_dev, places, -1)
    d_arrived = lax.all_to_all(d_pack, "seq", split_axis=2, concat_axis=1, tiled=True)
    d_items = d_arrived.transpose(0, 2, 1, 3).reshape(items, length, per_group, HD)
    d_query, d_key, d_value = attend_backward(
        q_heads, k_heads, v_heads, seg_items, d_items, lse, block
    )
    d_query = d_query.transpose(1, 0, 2, 3, 4).reshape(items, length, per_group * HD)
    d_heads = jnp.concatenate([d_query, d_key, d_value], axis=2).astype(jnp.bfloat16)
    d_heads = d_heads.reshape(rows_dev, place_dev, length, -1).transpose(0, 2, 1, 3)
    d_back = lax.all_to_all(d_heads, "seq", split_axis=1, concat_axis=2, tiled=True)
    d_back = d_back[:, :, :KVG].reshape(count, KVG, -1).astype(jnp.float32)
    d_q_rows = d_back[..., : per_group * HD].reshape(count, QH, HD)
    d_k_rows = d_back[..., per_group * HD : (per_group + 1) * HD]
    d_v_rows = d_back[..., (per_group + 1) * HD :]
    prep_out, prep_back = jax.vjp(
        lambda qkv_in, qs_in, ks_in: heads_prep(qkv_in, qs_in, ks_in, positions),
        qkv,
        q_scale,
        k_scale,
    )
    d_qkv, grad_q_scale, grad_k_scale = prep_back((d_q_rows, d_k_rows, d_v_rows))
    d_qkv = d_qkv.astype(jnp.bfloat16)
    grad_qkv = token_sum(normed, d_qkv)
    d_normed = times_rows(d_qkv, qkv_w)
    first_out, first_back = jax.vjp(norm_rows, x_rows, gain_a)
    d_tokens, grad_gain_a = first_back(d_normed)
    d_tokens = d_tokens + d_hidden
    head_sums = lax.psum((grad_q_scale, grad_k_scale), ("seq", "rep"))
    parts = (
        lax.psum_scatter(grad_gain_a, ("seq", "rep"), scatter_dimension=0, tiled=True),
        lax.psum_scatter(grad_qkv, ("seq", "rep"), scatter_dimension=0, tiled=True),
        lax.psum_scatter(grad_out, ("seq", "rep"), scatter_dimension=0, tiled=True),
        lax.psum_scatter(grad_gain_b, ("seq", "rep"), scatter_dimension=0, tiled=True),
        lax.psum_scatter(grad_gate, ("seq", "rep"), scatter_dimension=0, tiled=True),
        lax.psum_scatter(grad_up, ("seq", "rep"), scatter_dimension=0, tiled=True),
        lax.psum_scatter(grad_down, ("seq", "rep"), scatter_dimension=0, tiled=True),
    )
    return (
        activations,
        d_tokens.reshape(rows_dev, len_dev, width),
        parts[0],
        parts[1],
        parts[2],
        parts[3],
        parts[4],
        parts[5],
        parts[6],
        head_sums[0],
        head_sums[1],
    )


MESH = pl.DeviceIdType.MESH
BF = jnp.bfloat16
F32 = jnp.float32
EPS = norm_eps
NEG = -1e30
VMEM_BYTES = 60 * 2**20


def place():
    s = lax.axis_index("seq")
    r = lax.axis_index("rep")
    return lax.div(s, 2), lax.rem(s, 2), lax.div(r, 2), lax.rem(r, 2)


def dev(x, c, z, y):
    return {"seq": 2 * x + c, "rep": 2 * z + y}


def flip(v, by):
    return v if by == 0 else 1 - v


def send(src, dst, send_sem, recv_sem, target):
    copy = pltpu.make_async_remote_copy(
        src_ref=src,
        dst_ref=dst,
        send_sem=send_sem,
        recv_sem=recv_sem,
        device_id=target,
        device_id_type=MESH,
    )
    copy.start()
    return copy


def arrived(ref, sem):
    pltpu.make_async_copy(ref, ref, sem).wait()


def rows_of(ref, index, size):
    return ref.at[pl.ds(pl.multiple_of(index * size, size), size)]


def greet(targets):
    barrier = pltpu.get_barrier_semaphore()
    for target in targets:
        pl.semaphore_signal(barrier, inc=1, device_id=target, device_id_type=MESH)
    pl.semaphore_wait(barrier, len(targets))


def plane_targets(x, c, z, y):
    found = []
    for dx in range(2):
        for dy in range(2):
            for dc in range(2):
                if dx or dy or dc:
                    found.append(dev(flip(x, dx), flip(c, dc), z, flip(y, dy)))
    return found


def column_targets(x, c, z, y):
    found = []
    for dz in range(1, DZ):
        for dx in range(2):
            for dy in range(2):
                found.append(
                    dev(flip(x, dx), c, lax.rem(z + dz, DZ), flip(y, dy))
                )
    return found


def spread_start(src, full, send_sems, recv_sems):
    x, c, z, y = place()
    slot = 2 * x + c
    spot = rows_of(full, slot, BLK)
    for k, (dx, dy) in enumerate(((1, 1), (1, 0), (0, 1))):
        send(
            src, spot, send_sems.at[k], recv_sems.at[slot], dev(flip(x, dx), y, z, flip(y, dy))
        )

    @pl.when(c == y)
    def _():
        pltpu.make_async_copy(src, spot, recv_sems.at[slot]).start()

    @pl.when(c != y)
    def _():
        send(src, spot, send_sems.at[3], recv_sems.at[slot], dev(x, y, z, y))


def spread_wait(full, recv_sems):
    for j in range(4):
        arrived(rows_of(full, j, BLK), recv_sems.at[j])


def spread_sent(src, send_sems):
    x, c, z, y = place()
    for k in range(3):
        arrived(src, send_sems.at[k])

    @pl.when(c != y)
    def _():
        arrived(src, send_sems.at[3])


BLOCK_ORDER = ((1, 1), (1, 0), (0, 1), (0, 0))


def block_at(order):
    x, c, z, y = place()
    dx, dc = BLOCK_ORDER[order]
    return 2 * flip(x, dx) + flip(c, dc)


def collect_start(order, partial, inbox, send_sems, recv_sems):
    x, c, z, y = place()
    dx, dc = BLOCK_ORDER[order]
    src = rows_of(partial, block_at(order), BLK)
    slot = 2 * x + y
    spot = inbox.at[slot]
    target = dev(flip(x, dx), flip(c, dc), z, c)
    if dx or dc:
        send(src, spot, send_sems.at[order], recv_sems.at[slot], target)
        return

    @pl.when(c == y)
    def _():
        pltpu.make_async_copy(src, spot, recv_sems.at[slot]).start()

    @pl.when(c != y)
    def _():
        send(src, spot, send_sems.at[order], recv_sems.at[slot], target)


def collect_wait(inbox, recv_sems):
    for j in range(4):
        arrived(inbox.at[j], recv_sems.at[j])


def collect_sent(inbox, send_sems):
    x, c, z, y = place()
    for k in range(3):
        arrived(inbox.at[0], send_sems.at[k])

    @pl.when(c == y)
    def _():
        pass

    @pl.when(c != y)
    def _():
        arrived(inbox.at[0], send_sems.at[3])


def inbox_sum(inbox):
    return (inbox[0].astype(F32) + inbox[1].astype(F32)) + (
        inbox[2].astype(F32) + inbox[3].astype(F32)
    )


def mm(left, right):
    return lax.dot_general(left, right, (((1,), (0,)), ((), ())), preferred_element_type=F32)


def mm_nt(left, right):
    return lax.dot_general(left, right, (((1,), (1,)), ((), ())), preferred_element_type=F32)


def mm_tn(left, right):
    return lax.dot_general(left, right, (((0,), (0,)), ((), ())), preferred_element_type=F32)


def mask_of(seg_ref):
    seg_col = seg_ref[:, 0:1].astype(F32)
    seg_row = jnp.transpose(seg_ref[...].astype(F32))[0:1, :]
    key_at = lax.broadcasted_iota(jnp.int32, (LEN4, LEN4), 0)
    query_at = lax.broadcasted_iota(jnp.int32, (LEN4, LEN4), 1)
    return seg_col, seg_row, (key_at <= query_at) & (seg_col == seg_row)


def group_of(local_head):
    x, c, z, y = place()
    shard = 2 * x + y
    return jnp.where(local_head + shard >= 4, 1, 0)


def k1_body(
    tok, cot, seg, wa, wg, wu, wd, gq, gk, fr,
    w3_o, wa_o, dyf_o, hid_o, n2_o, qt_o, kt_o, k_o, vt_o, v_o, qkvt_o, lse_o, att_o, n1_o, cs_o, grow_o, segf_o,
    xf, wav, attt, part, inbox,
    tok_ss, tok_rs, cot_ss, cot_rs, seg_ss, seg_rs, out_ss, out_rs, w_ss, w_rs, c_ss, c_rs, loc,
):
    x, c, z, y = place()
    me = (2 * x + c) * 2 * DZ + 2 * z + y
    source = (2 * x + y) * DZ + z
    greet(plane_targets(x, c, z, y) + column_targets(x, c, z, y))

    def weight_piece(m, shard):
        wide = pl.ds(pl.multiple_of(shard * FFS, 128), FFS)
        if m == 0:
            return wa.at[shard]
        return (wg, wu, wd)[m - 1].at[:, wide]

    def weight_view(m, first, count):
        rows = pl.ds(pl.multiple_of(first, count), count)
        if m == 0:
            return wav.at[rows]
        return w3_o.at[rows, pl.ds((m - 1) * FFS, FFS)]

    def weights_start(m):
        for dz in range(DZ):
            for dx in range(2):
                for dy in range(2):
                    tx, ty, tz = flip(x, dx), flip(y, dy), lax.rem(z + dz, DZ)
                    src = weight_piece(m, 2 * tx + ty)
                    spot = weight_view(m, me * BR, BR)
                    k = (dz * 2 + dx) * 2 + dy
                    if k == 0:
                        pltpu.make_async_copy(src, spot, w_rs.at[m, source]).start()
                    else:
                        send(src, spot, w_ss.at[m, k], w_rs.at[m, source], dev(tx, c, tz, ty))

    def weights_sent(m):
        for k in range(1, 4 * DZ):
            arrived(weight_view(m, 0, BR), w_ss.at[m, k])

    def weights_swap(m):
        for k in range(4 * DZ):
            arrived(weight_view(m, 0, BR), w_rs.at[m, k])
        for tx in range(2):
            half = weight_view(m, (2 * tx + c) * HALF, HALF)
            send(half, half, c_ss.at[m, tx], c_rs.at[m, tx], dev(x, 1 - c, z, y))

    def weights_wait(m):
        for tx in range(2):
            arrived(weight_view(m, 0, HALF), c_rs.at[m, tx])

    def swap_sent(m):
        for tx in range(2):
            arrived(weight_view(m, 0, HALF), c_ss.at[m, tx])

    spread_start(seg, segf_o, seg_ss, seg_rs)
    spread_start(tok, xf, tok_ss, tok_rs)
    weights_start(0)
    spread_wait(segf_o, seg_rs)
    seg_col, seg_row, allowed = mask_of(segf_o)
    earlier = jnp.sum(jnp.where(seg_col < seg_row, 1.0, 0.0), axis=0, keepdims=True)
    index = lax.broadcasted_iota(jnp.int32, (1, LEN4), 1).astype(F32)
    angles = fr[...] * (index - earlier)
    cos, sin = jnp.cos(angles), jnp.sin(angles)
    cs_o[0:32, :] = cos
    cs_o[32:64, :] = sin
    spread_wait(xf, tok_rs)
    weights_swap(0)
    weights_wait(0)
    for m in range(1, 4):
        weights_start(m)
    spread_start(cot, dyf_o, cot_ss, cot_rs)
    keep = pltpu.make_async_copy(wav, wa_o, loc.at[0])
    keep.start()
    gains = jnp.transpose(wav[:, 512:640].astype(F32))[64:72, :]
    grow_o[...] = gains
    gain_a, gain_b = grow_o[0:1, :], grow_o[1:2, :]

    @pl.loop(0, 4)
    def _(j):
        rows = pl.ds(pl.multiple_of(j * BLK, BLK), BLK)
        v = xf[rows, :].astype(F32)
        n1_o[rows, :] = (
            v * lax.rsqrt(jnp.mean(v * v, axis=1, keepdims=True) + EPS) * gain_a
        ).astype(BF)

    @pl.loop(0, 5)
    def _(j):
        wide = pl.ds(pl.multiple_of(j * 128, 128), 128)
        qkvt_o[wide, :] = jnp.transpose(mm(n1_o[...], wav[:, wide]))

    def rotated(v, gain):
        v = v * lax.rsqrt(jnp.mean(v * v, axis=0, keepdims=True) + EPS) * gain
        first, second = v[0:32, :], v[32:64, :]
        return first * cos - second * sin, second * cos + first * sin

    for h in range(QS):
        first, second = rotated(qkvt_o[h * 64 : h * 64 + 64, :], gq[...])
        qt_o[h, 0:32, :] = first.astype(BF)
        qt_o[h, 32:64, :] = second.astype(BF)
    for g in range(2):
        base = QS * 64 + g * 64
        first, second = rotated(qkvt_o[base : base + 64, :], gk[...])
        both = jnp.concatenate([first, second], axis=0)
        kt_o[g] = both.astype(BF)
        k_o[g] = jnp.transpose(both).astype(BF)
        value = qkvt_o[base + 128 : base + 192, :]
        vt_o[g] = value.astype(BF)
        v_o[g] = jnp.transpose(value).astype(BF)
    lse_o[...] = jnp.zeros_like(lse_o)
    attt[QS * 64 :, :] = jnp.zeros((384 - QS * 64, LEN4), F32)
    for h in range(QS):
        g = group_of(h)
        scores = jnp.where(allowed, mm(k_o[g], qt_o[h]) * SCALE, NEG)
        top = jnp.max(scores, axis=0, keepdims=True)
        weights = jnp.exp(scores - top)
        total = jnp.sum(weights, axis=0, keepdims=True)
        lse_o[h : h + 1, :] = top + jnp.log(total)
        attt[h * 64 : h * 64 + 64, :] = mm(vt_o[g], (weights / total).astype(BF))
    att_o[...] = jnp.transpose(attt[...]).astype(BF)
    for order in range(4):
        rows = pl.ds(pl.multiple_of(block_at(order) * BLK, BLK), BLK)
        part[rows, :] = mm_nt(att_o[rows, :], wav[:, 640:1024]).astype(BF)
        collect_start(order, part, inbox, out_ss, out_rs)
    collect_wait(inbox, out_rs)
    hidden = tok[...].astype(F32) + inbox_sum(inbox)
    hid_o[...] = hidden
    n2_o[...] = (
        hidden * lax.rsqrt(jnp.mean(hidden * hidden, axis=1, keepdims=True) + EPS) * gain_b
    ).astype(BF)
    for m in range(1, 4):
        weights_swap(m)
    spread_wait(dyf_o, cot_rs)
    spread_sent(seg, seg_ss)
    spread_sent(tok, tok_ss)
    spread_sent(cot, cot_ss)
    collect_sent(inbox, out_ss)
    for m in range(4):
        weights_sent(m)
        swap_sent(m)
    for m in range(1, 4):
        weights_wait(m)
    keep.wait()


def k2_body(
    n2, dyf_h, w3_h, hid, cot, grow,
    act_o, dhid_o, dab_o, g_o, gp_o,
    n2f, dyf, w3, dact, active, dgu, part, inbox, inbox_y, gsend, grecv,
    n_ss, n_rs, d_ss, d_rs, y_ss, y_rs, g_ss, g_rs, loc,
):
    x, c, z, y = place()
    greet(plane_targets(x, c, z, y))
    spread_start(n2, n2f, n_ss, n_rs)
    loads = (
        pltpu.make_async_copy(dyf_h, dyf, loc.at[0]),
        pltpu.make_async_copy(w3_h.at[:, pl.ds(2 * FFS, FFS)], w3.at[:, pl.ds(2 * FFS, FFS)], loc.at[1]),
        pltpu.make_async_copy(w3_h.at[:, pl.ds(0, 2 * FFS)], w3.at[:, pl.ds(0, 2 * FFS)], loc.at[2]),
    )
    for load in loads:
        load.start()
    loads[0].wait()
    loads[1].wait()
    tiles = FF_TILES
    for lo, wide in tiles:
        dact[:, lo : lo + wide] = mm(dyf[...], w3[:, 2 * FFS + lo : 2 * FFS + lo + wide])
    loads[2].wait()
    spread_wait(n2f, n_rs)
    for lo, wide in tiles:
        gate = mm(n2f[...], w3[:, lo : lo + wide])
        upward = mm(n2f[...], w3[:, FFS + lo : FFS + lo + wide])
        sig = 1.0 / (1.0 + jnp.exp(-gate))
        silu = gate * sig
        grad = dact[:, lo : lo + wide]
        active[:, lo : lo + wide] = (silu * upward).astype(BF)
        dgu[:, lo : lo + wide] = (grad * upward * (sig * (1.0 + gate * (1.0 - sig)))).astype(BF)
        dgu[:, FFS + lo : FFS + lo + wide] = (grad * silu).astype(BF)
    for order in range(4):
        rows = pl.ds(pl.multiple_of(block_at(order) * BLK, BLK), BLK)

        @pl.loop(0, 4)
        def _(j):
            wide = pl.ds(pl.multiple_of(j * 512, 512), 512)
            part[0, rows, wide] = mm_nt(dgu[rows, :], w3[wide, 0 : 2 * FFS]).astype(BF)

        collect_start(order, part.at[0], inbox, d_ss, d_rs)
    for order in range(4):
        rows = pl.ds(pl.multiple_of(block_at(order) * BLK, BLK), BLK)

        @pl.loop(0, 4)
        def _(j):
            wide = pl.ds(pl.multiple_of(j * 512, 512), 512)
            part[1, rows, wide] = mm_nt(active[rows, :], w3[wide, 2 * FFS : 3 * FFS]).astype(BF)

        collect_start(order, part.at[1], inbox_y, y_ss, y_rs)

    def grads(core, row):
        first = (2 * lax.div(row, 2) + core) * HALF + lax.rem(row, 2) * 256
        wide = pl.ds(pl.multiple_of(first, 256), 256)
        return mm_tn(n2f[:, wide], dgu[...]), mm_tn(dyf[:, wide], active[...])

    @pl.loop(0, 4)
    def _(j):
        gu, down = grads(1 - c, j)
        rows = pl.ds(pl.multiple_of(j * 256, 256), 256)
        gsend[rows, 0 : 2 * FFS] = gu.astype(BF)
        gsend[rows, 2 * FFS : 3 * FFS] = down.astype(BF)

    swap = send(gsend, grecv, g_ss, g_rs, dev(x, 1 - c, z, y))
    collect_wait(inbox, d_rs)
    dn = inbox_sum(inbox)
    h = hid[...]
    r = lax.rsqrt(jnp.mean(h * h, axis=1, keepdims=True) + EPS)
    gp_o[...] = jnp.broadcast_to(jnp.sum(dn * h * r, axis=0, keepdims=True), gp_o.shape)
    a = dn * grow[1:2, :]
    dh = cot[...].astype(F32) + r * (a - h * (r * r * jnp.mean(a * h, axis=1, keepdims=True)))
    dhid_o[...] = dh
    dab_o[...] = dh.astype(BF)
    swap.wait_recv()

    @pl.loop(0, 4)
    def _(j):
        gu, down = grads(c, j)
        rows = pl.ds(pl.multiple_of(j * 256, 256), 256)
        g_o[rows, 0 : 2 * FFS] = (gu + grecv[rows, 0 : 2 * FFS].astype(F32)).astype(BF)
        g_o[rows, 2 * FFS : 3 * FFS] = (down + grecv[rows, 2 * FFS : 3 * FFS].astype(F32)).astype(BF)

    collect_wait(inbox_y, y_rs)
    act_o[...] = (hid[...] + inbox_sum(inbox_y)).astype(BF)
    swap.wait_send()
    spread_sent(n2, n_ss)
    collect_sent(inbox, d_ss)
    collect_sent(inbox_y, y_ss)


def k3_body(
    g_h, dab, dhid, tok, wa_h, qt, kt, k, vt, v, qkvt, lse, att, n1, cs, grow, seg, gp2, gq, gk,
    dtok_o, gr_o, ar_o, vr_o,
    dabf, wav, dot_s, dqkvt, dqkv, part, inbox, asend, arecv, aown, vec, vecr, vecs, dkt, dvt,
    b_ss, b_rs, t_ss, t_rs, w_ss, w_rs, a_ss, a_rs, v_ss, v_rs, c_ss, c_rs, loc,
):
    x, c, z, y = place()
    source = (2 * x + y) * DZ + z
    greet(plane_targets(x, c, z, y) + column_targets(x, c, z, y))

    def owners_start(src, dst, send_sems, recv_sems):
        for dz in range(DZ):
            for dx in range(2):
                for dy in range(2):
                    tx, ty, tz = flip(x, dx), flip(y, dy), lax.rem(z + dz, DZ)
                    piece = src((tx * DZ + tz) * 2 + ty)
                    k_at = (dz * 2 + dx) * 2 + dy
                    if k_at == 0:
                        pltpu.make_async_copy(piece, dst.at[source], recv_sems.at[source]).start()
                    else:
                        send(
                            piece, dst.at[source], send_sems.at[k_at], recv_sems.at[source], dev(tx, c, tz, ty)
                        )

    def owners_wait(dst, send_sems, recv_sems):
        for i in range(1, 4 * DZ):
            arrived(dst.at[0], send_sems.at[i])
        for i in range(4 * DZ):
            arrived(dst.at[i], recv_sems.at[i])

    spread_start(dab, dabf, b_ss, b_rs)
    load = pltpu.make_async_copy(wa_h, wav, loc.at[0])
    load.start()
    owners_start(lambda i: rows_of(g_h, i, BR), gr_o, w_ss, w_rs)
    seg_col, seg_row, allowed = mask_of(seg)
    cos, sin = cs[0:32, :], cs[32:64, :]
    load.wait()
    spread_wait(dabf, b_rs)
    dot_s[...] = jnp.transpose(mm(dabf[...], wav[:, 640:1024]).astype(BF).astype(F32)).astype(BF)
    dkt[...] = jnp.zeros_like(dkt)
    dvt[...] = jnp.zeros_like(dvt)

    def unrotated(first, second, raw, gain):
        d_first = first * cos + second * sin
        d_second = second * cos - first * sin
        d = jnp.concatenate([d_first, d_second], axis=0)
        r = lax.rsqrt(jnp.mean(raw * raw, axis=0, keepdims=True) + EPS)
        d_gain = jnp.sum(d * raw * r, axis=1, keepdims=True)
        a = d * gain
        return r * (a - raw * (r * r * jnp.mean(a * raw, axis=0, keepdims=True))), d_gain

    dq_gain = jnp.zeros((64, 1), F32)
    for h in range(QS):
        g = group_of(h)
        scores = mm(k[g], qt[h]) * SCALE
        p = jnp.where(allowed, jnp.exp(scores - lse[h : h + 1, :]), 0.0)
        d_out = dot_s[h * 64 : h * 64 + 64, :]
        dvt[g] += mm_nt(d_out, p.astype(BF))
        dp = mm(v[g], d_out)
        ds = (p * (dp - jnp.sum(p * dp, axis=0, keepdims=True))).astype(BF)
        dkt[g] += mm_nt(qt[h], ds) * SCALE
        dq = (mm(kt[g], ds) * SCALE).astype(BF).astype(F32)
        d, more = unrotated(dq[0:32, :], dq[32:64, :], qkvt[h * 64 : h * 64 + 64, :], gq[...])
        dq_gain = dq_gain + more
        dqkvt[h * 64 : h * 64 + 64, :] = d
    dk_gain = jnp.zeros((64, 1), F32)
    for g in range(2):
        base = QS * 64 + g * 64
        dk = dkt[g].astype(BF).astype(F32)
        d, more = unrotated(dk[0:32, :], dk[32:64, :], qkvt[base : base + 64, :], gk[...])
        dk_gain = dk_gain + more
        dqkvt[base : base + 64, :] = d
        dqkvt[base + 128 : base + 192, :] = dvt[g]
    dqkvt[576:640, :] = jnp.zeros((64, LEN4), F32)
    dqkv[...] = jnp.transpose(dqkvt[...]).astype(BF)
    for order in range(4):
        rows = pl.ds(pl.multiple_of(block_at(order) * BLK, BLK), BLK)
        part[rows, :] = mm_nt(dqkv[rows, :], wav[:, 0:640]).astype(BF)
        collect_start(order, part, inbox, t_ss, t_rs)

    def grads(core, row):
        first = (2 * lax.div(row, 2) + core) * HALF + lax.rem(row, 2) * 256
        wide = pl.ds(pl.multiple_of(first, 256), 256)
        return mm_tn(n1[:, wide], dqkv[...]), mm_tn(dabf[:, wide], att[...])

    @pl.loop(0, 4)
    def _(j):
        one, two = grads(1 - c, j)
        rows = pl.ds(pl.multiple_of(j * 256, 256), 256)
        asend[rows, 0:640] = one.astype(BF)
        asend[rows, 640:1024] = two.astype(BF)

    swap = send(asend, arecv, c_ss.at[0], c_rs.at[0], dev(x, 1 - c, z, y))
    swap.wait_recv()

    @pl.loop(0, 4)
    def _(j):
        one, two = grads(c, j)
        rows = pl.ds(pl.multiple_of(j * 256, 256), 256)
        aown[rows, 0:640] = (one + arecv[rows, 0:640].astype(F32)).astype(BF)
        aown[rows, 640:1024] = (two + arecv[rows, 640:1024].astype(F32)).astype(BF)

    owners_start(lambda i: rows_of(aown, i, BR), ar_o, a_ss, a_rs)
    collect_wait(inbox, t_rs)
    dn = inbox_sum(inbox)
    xv = tok[...].astype(F32)
    r = lax.rsqrt(jnp.mean(xv * xv, axis=1, keepdims=True) + EPS)
    gain_a = jnp.sum(dn * xv * r, axis=0, keepdims=True)
    b = dn * grow[0:1, :]
    dtok_o[...] = dhid[...] + r * (b - xv * (r * r * jnp.mean(b * xv, axis=1, keepdims=True)))
    qk = jnp.transpose(jnp.concatenate([jnp.broadcast_to(dq_gain, (64, 128)), jnp.broadcast_to(dk_gain, (64, 128))], axis=0))
    gain_b = gp2[0:1, :]
    for i in range(4 * DZ):
        for half in range(2):
            at = (((i // (2 * DZ)) * 2 + half) * 2 * DZ + i % (2 * DZ)) * BR
            rows4 = jnp.concatenate(
                [gain_a[:, at : at + BR], gain_b[:, at : at + BR], qk[0:1, 0:64], qk[0:1, 64:128]], axis=0
            )
            vec[half, i, 0:4, 0:64] = rows4

    vecs[...] = vec[c]
    swap_v = send(vec.at[1 - c], vecr, c_ss.at[1], c_rs.at[1], dev(x, 1 - c, z, y))
    swap_v.wait_recv()
    vecs[...] += vecr[...]
    owners_start(lambda i: vecs.at[i], vr_o, v_ss, v_rs)
    owners_wait(gr_o, w_ss, w_rs)
    owners_wait(ar_o, a_ss, a_rs)
    owners_wait(vr_o, v_ss, v_rs)
    swap.wait_send()
    swap_v.wait_send()
    spread_sent(dab, b_ss)
    collect_sent(inbox, t_ss)


QS = 5
DZ = 4
BLK = 128
LEN4 = 512
FFS = 896
BR = 64
HALF = 512
SCALE = HD ** (-0.5)
FF_TILES = ((0, 256), (256, 256), (512, 256), (768, 128))
ANY = pl.ANY
VM = pltpu.VMEM


def kernel_call(body, args, kinds, outs, scratch, cid):
    params = pltpu.CompilerParams(
        collective_id=cid, has_side_effects=True, vmem_limit_bytes=VMEM_BYTES
    )
    return pl.pallas_call(
        body,
        out_shape=[jax.ShapeDtypeStruct(shape, kind) for shape, kind, _ in outs],
        in_specs=[pl.BlockSpec(memory_space=ANY if kind == "h" else VM) for kind in kinds],
        out_specs=[pl.BlockSpec(memory_space=ANY if where == "h" else VM) for _, _, where in outs],
        scratch_shapes=scratch,
        compiler_params=params,
    )(*args)


def plane_plan(
    tokens, segment_ids, cotangent, attn_gain, w_qkv, w_out, ffn_gain, w_gate, w_up, w_down, q_gain, k_gain
):
    width = tokens.shape[-1]
    tok = tokens.reshape(BLK, width)
    cot = cotangent.reshape(BLK, width)
    seg = jnp.broadcast_to(segment_ids.reshape(BLK, 1).astype(BF), (BLK, 128))
    gains = jnp.concatenate(
        [attn_gain[:, None], ffn_gain[:, None], jnp.zeros((BR, 62), BF)], axis=1
    )
    tail = jnp.zeros((BR, 64), BF)
    wa = jnp.stack(
        [
            jnp.concatenate(
                [
                    w_qkv[:, 320 * t : 320 * t + 320],
                    w_qkv[:, QW + 64 * t : QW + 64 * t + 128],
                    w_qkv[:, QW + KW + 64 * t : QW + KW + 64 * t + 128],
                    gains,
                    w_out[:, 320 * t : 320 * t + 320],
                    tail,
                ],
                axis=1,
            )
            for t in range(4)
        ]
    )
    gq = q_gain.astype(F32).reshape(64, 1)
    gk = k_gain.astype(F32).reshape(64, 1)
    fr = (rope_base ** (-jnp.arange(32, dtype=jnp.float32) * 2.0 / 64)).reshape(32, 1)
    sem = pltpu.SemaphoreType.DMA
    vm = pltpu.VMEM
    (
        w3, wah, dyf, hid, n2, qt, kt, k, vt, v, qkvt, lse, att, n1, cs, grow, segf
    ) = kernel_call(
        k1_body,
        (tok, cot, seg, wa, w_gate, w_up, w_down, gq, gk, fr),
        "vhhhhhhvvv",
        [
            ((2048, 3 * FFS), BF, "h"),
            ((2048, 1024), BF, "h"),
            ((LEN4, width), BF, "h"),
            ((BLK, width), F32, "v"),
            ((BLK, width), BF, "v"),
            ((QS, 64, LEN4), BF, "v"),
            ((2, 64, LEN4), BF, "v"),
            ((2, LEN4, 64), BF, "v"),
            ((2, 64, LEN4), BF, "v"),
            ((2, LEN4, 64), BF, "v"),
            ((640, LEN4), F32, "v"),
            ((8, LEN4), F32, "v"),
            ((LEN4, 384), BF, "v"),
            ((LEN4, width), BF, "v"),
            ((64, LEN4), F32, "v"),
            ((8, width), F32, "v"),
            ((LEN4, 128), BF, "v"),
        ],
        [
            vm((LEN4, width), BF),
            vm((2048, 1024), BF),
            vm((384, LEN4), F32),
            vm((LEN4, width), BF),
            vm((4, BLK, width), BF),
            sem((4,)), sem((4,)), sem((4,)), sem((4,)), sem((4,)), sem((4,)), sem((4,)), sem((4,)),
            sem((4, 4 * DZ)), sem((4, 4 * DZ)), sem((4, 2)), sem((4, 2)), sem((1,)),
        ],
        0,
    )
    act, dhid, dab, g, gp = kernel_call(
        k2_body,
        (n2, dyf, w3, hid, cot, grow),
        "hhhvvv",
        [
            ((BLK, width), BF, "v"),
            ((BLK, width), F32, "v"),
            ((BLK, width), BF, "v"),
            ((1024, 3 * FFS), BF, "v"),
            ((8, width), F32, "v"),
        ],
        [
            vm((LEN4, width), BF),
            vm((LEN4, width), BF),
            vm((2048, 3 * FFS), BF),
            vm((LEN4, FFS), F32),
            vm((LEN4, FFS), BF),
            vm((LEN4, 2 * FFS), BF),
            vm((2, LEN4, width), BF),
            vm((4, BLK, width), BF),
            vm((4, BLK, width), BF),
            vm((1024, 3 * FFS), BF),
            vm((1024, 3 * FFS), BF),
            sem((4,)), sem((4,)), sem((4,)), sem((4,)), sem((4,)), sem((4,)), sem, sem, sem((3,)),
        ],
        1,
    )
    dtok, gr, ar, vr = kernel_call(
        k3_body,
        (g, dab, dhid, tok, wah, qt, kt, k, vt, v, qkvt, lse, att, n1, cs, grow, segf, gp, gq, gk),
        "hhvvhvvvvvvvvvvvvvvv",
        [
            ((BLK, width), F32, "v"),
            ((4 * DZ, BR, 3 * FFS), BF, "h"),
            ((4 * DZ, BR, 1024), BF, "h"),
            ((4 * DZ, 8, 128), F32, "h"),
        ],
        [
            vm((LEN4, width), BF),
            vm((2048, 1024), BF),
            vm((384, LEN4), BF),
            vm((640, LEN4), F32),
            vm((LEN4, 640), BF),
            vm((LEN4, width), BF),
            vm((4, BLK, width), BF),
            vm((1024, 1024), BF),
            vm((1024, 1024), BF),
            vm((1024, 1024), BF),
            vm((2, 4 * DZ, 8, 128), F32),
            vm((4 * DZ, 8, 128), F32),
            vm((4 * DZ, 8, 128), F32),
            vm((2, 64, LEN4), F32),
            vm((2, 64, LEN4), F32),
            sem((4,)), sem((4,)), sem((4,)), sem((4,)),
            sem((4 * DZ,)), sem((4 * DZ,)), sem((4 * DZ,)), sem((4 * DZ,)), sem((4 * DZ,)), sem((4 * DZ,)),
            sem((2,)), sem((2,)), sem((1,)),
        ],
        2,
    )
    ffn = jnp.sum(gr.reshape(4, DZ, BR, 3, FFS).astype(F32), axis=1)
    ffn = ffn.transpose(2, 1, 0, 3).reshape(3, BR, 4 * FFS)
    att_w = jnp.sum(ar.reshape(4, DZ, BR, 1024).astype(F32), axis=1)
    none = jnp.zeros((BR, 64), F32)

    def groups(at):
        first = jnp.concatenate([att_w[t][:, at : at + 64] for t in range(4)] + [none], axis=1)
        second = jnp.concatenate([none] + [att_w[t][:, at + 64 : at + 128] for t in range(4)], axis=1)
        return first + second

    g_qkv = jnp.concatenate(
        [att_w[t][:, 0:320] for t in range(4)] + [groups(320), groups(448)], axis=1
    )
    g_out = jnp.concatenate([att_w[t][:, 640:960] for t in range(4)], axis=1)
    vec = jnp.sum(vr, axis=0)
    return (
        act.reshape(tokens.shape),
        dtok.reshape(tokens.shape),
        vec[0, :64],
        g_qkv,
        g_out,
        vec[1, :64],
        ffn[0],
        ffn[1],
        ffn[2],
        vec[2, :64],
        vec[3, :64],
    )


def solution(mesh):
    in_specs = (
        P("rep", "seq", None),
        P("rep", "seq"),
        P("rep", "seq", None),
        P(("seq", "rep")),
        P(("seq", "rep"), None),
        P(("seq", "rep"), None),
        P(("seq", "rep")),
        P(("seq", "rep"), None),
        P(("seq", "rep"), None),
        P(("seq", "rep"), None),
        P(),
        P(),
    )
    out_specs = (
        P("rep", "seq", None),
        P("rep", "seq", None),
        P(("seq", "rep")),
        P(("seq", "rep"), None),
        P(("seq", "rep"), None),
        P(("seq", "rep")),
        P(("seq", "rep"), None),
        P(("seq", "rep"), None),
        P(("seq", "rep"), None),
        P(),
        P(),
    )
    planes = mesh.shape["seq"] == 4 and mesh.shape["rep"] == 8
    body = plane_plan if planes else shards
    return jax.shard_map(body, mesh=mesh, in_specs=in_specs, out_specs=out_specs, check_vma=False)
```

```python
import jax
import jax.numpy as jnp
from jax import lax
from jax.experimental import pallas as pl
from jax.experimental.pallas import tpu as pltpu
from jax.sharding import PartitionSpec as P

QH = 20
KVG = 5
HD = 64
QW = 1280
KW = 320


norm_eps = 1e-06
rope_base = 10000.0


def norm_rows(value_matrix, gain):
    return (
        value_matrix
        * lax.rsqrt(jnp.mean(value_matrix * value_matrix, axis=-1, keepdims=True) + norm_eps)
        * gain
    )


def rotate_heads(value_matrix, positions):
    half = value_matrix.shape[-1] // 2
    freqs = rope_base ** (-jnp.arange(half, dtype=jnp.float32) * 2.0 / value_matrix.shape[-1])
    angles = positions.astype(jnp.float32)[:, None] * freqs[None, :]
    cosine = jnp.cos(angles)[:, None, :]
    sine = jnp.sin(angles)[:, None, :]
    first = value_matrix[..., :half]
    second = value_matrix[..., half:]
    return jnp.concatenate(
        [first * cosine - second * sine, second * cosine + first * sine], axis=-1
    )


def heads_prep(qkv, q_scale, k_scale, positions):
    count = qkv.shape[0]
    query = qkv[:, :QW].reshape(count, QH, HD)
    key = qkv[:, QW : QW + KW].reshape(count, KVG, HD)
    value = qkv[:, QW + KW :].reshape(count, KVG, HD)
    query = rotate_heads(norm_rows(query, q_scale), positions)
    key = rotate_heads(norm_rows(key, k_scale), positions)
    return (query, key, value)


def times_rows(left, right):
    return lax.dot_general(
        left, right, (((1,), (1,)), ((), ())), preferred_element_type=jnp.float32
    )


def token_sum(left, right):
    return lax.dot_general(
        left, right, (((0,), (0,)), ((), ())), preferred_element_type=jnp.float32
    )


def block_scores(query_block, key_matrix, seg_row, start, score_scale):
    width = query_block.shape[1]
    length = key_matrix.shape[1]
    logit_scores = (
        jnp.einsum("zjfr,zyr->zfjy", query_block, key_matrix, preferred_element_type=jnp.float32)
        * score_scale
    )
    rows = start + jnp.arange(width, dtype=jnp.int32)
    cols = jnp.arange(length, dtype=jnp.int32)
    seg_blk = lax.dynamic_slice_in_dim(seg_row, start, width, 1)
    allowed = (cols[None, None, :] <= rows[None, :, None]) & (
        seg_row[:, None, :] == seg_blk[:, :, None]
    )
    return jnp.where(allowed[:, None], logit_scores, -1e30)


def attend_forward(query, key_matrix, value_matrix, seg_row, block):
    length = key_matrix.shape[1]
    score_scale = HD ** (-0.5)

    def one_block(start):
        query_block = lax.dynamic_slice_in_dim(query, start, block, 1)
        logit_scores = block_scores(query_block, key_matrix, seg_row, start, score_scale)
        top = jnp.max(logit_scores, axis=-1, keepdims=True)
        weights = jnp.exp(logit_scores - top)
        total = jnp.sum(weights, axis=-1, keepdims=True)
        attention_probabilities = (weights / total).astype(jnp.bfloat16)
        layer_result = jnp.einsum(
            "szjr,srn->sjzn",
            attention_probabilities,
            value_matrix,
            preferred_element_type=jnp.float32,
        )
        return (layer_result.astype(jnp.bfloat16), (top + jnp.log(total))[..., 0])

    starts = jnp.arange(0, length, block, dtype=jnp.int32)
    return lax.map(one_block, starts)


def attend_backward(query, key_matrix, value_matrix, seg_row, grads_out, lse, block):
    length = key_matrix.shape[1]
    score_scale = HD ** (-0.5)

    def one_block(carry, item):
        d_key, d_value = carry
        start, sums = item
        query_block = lax.dynamic_slice_in_dim(query, start, block, 1)
        gradient_block = lax.dynamic_slice_in_dim(grads_out, start, block, 1)
        logit_scores = block_scores(query_block, key_matrix, seg_row, start, score_scale)
        attention_probabilities = jnp.exp(logit_scores - sums[..., None])
        reduced_probabilities = attention_probabilities.astype(jnp.bfloat16)
        d_value = d_value + jnp.einsum(
            "syer,seyo->sro",
            reduced_probabilities,
            gradient_block,
            preferred_element_type=jnp.float32,
        )
        probability_gradient = jnp.einsum(
            "zjfr,zyr->zfjy", gradient_block, value_matrix, preferred_element_type=jnp.float32
        )
        inner = jnp.sum(attention_probabilities * probability_gradient, axis=-1, keepdims=True)
        score_gradient = (attention_probabilities * (probability_gradient - inner)).astype(
            jnp.bfloat16
        )
        d_query = (
            jnp.einsum(
                "szjr,srn->sjzn", score_gradient, key_matrix, preferred_element_type=jnp.float32
            )
            * score_scale
        )
        d_key = (
            d_key
            + jnp.einsum(
                "syer,seyo->sro", score_gradient, query_block, preferred_element_type=jnp.float32
            )
            * score_scale
        )
        return ((d_key, d_value), d_query)

    starts = jnp.arange(0, length, block, dtype=jnp.int32)
    zeros = jnp.zeros(key_matrix.shape, jnp.float32)
    carry, d_query = lax.scan(one_block, (zeros, zeros), (starts, lse))
    return (d_query, carry[0], carry[1])


def shards(
    tokens,
    segment_ids,
    cotangent,
    attn_gain,
    w_qkv,
    w_out,
    ffn_gain,
    w_gate,
    w_up,
    w_down,
    q_gain,
    k_gain,
):
    groups = lax.axis_size("seq")
    rows_dev, len_dev, width = tokens.shape
    count = rows_dev * len_dev
    per_group = QH // KVG
    places = (KVG + groups - 1) // groups * groups
    place_dev = places // groups
    length = len_dev * groups
    block = min(512, length)
    items = rows_dev * place_dev
    gain_one, qkv_w, out_w, gain_two, gate_w, up_w, down_w = (
        lax.all_gather(attn_gain, ("seq", "rep"), axis=0, tiled=True),
        lax.all_gather(w_qkv, ("seq", "rep"), axis=0, tiled=True),
        lax.all_gather(w_out, ("seq", "rep"), axis=0, tiled=True),
        lax.all_gather(ffn_gain, ("seq", "rep"), axis=0, tiled=True),
        lax.all_gather(w_gate, ("seq", "rep"), axis=0, tiled=True),
        lax.all_gather(w_up, ("seq", "rep"), axis=0, tiled=True),
        lax.all_gather(w_down, ("seq", "rep"), axis=0, tiled=True),
    )
    row_seg = lax.all_gather(segment_ids, "seq", axis=1, tiled=True)
    offset = lax.axis_index("seq") * len_dev
    earlier = jnp.sum((row_seg[:, None, :] < segment_ids[:, :, None]).astype(jnp.int32), axis=2)
    positions = (offset + jnp.arange(len_dev, dtype=jnp.int32)[None, :] - earlier).reshape(count)
    seg_items = jnp.repeat(row_seg, place_dev, axis=0)
    x_rows = tokens.reshape(count, width).astype(jnp.float32)
    gain_a = gain_one.astype(jnp.float32)
    gain_b = gain_two.astype(jnp.float32)
    q_scale = q_gain.astype(jnp.float32)
    k_scale = k_gain.astype(jnp.float32)
    normed = norm_rows(x_rows, gain_a).astype(jnp.bfloat16)
    qkv = jnp.dot(normed, qkv_w, preferred_element_type=jnp.float32)
    query, key, value = heads_prep(qkv, q_scale, k_scale, positions)
    packed = jnp.concatenate(
        [query.reshape(count, KVG, per_group * HD), key, value], axis=2
    ).astype(jnp.bfloat16)
    packed = jnp.pad(packed, ((0, 0), (0, places - KVG), (0, 0))).reshape(
        rows_dev, len_dev, places, -1
    )
    arrived = lax.all_to_all(packed, "seq", split_axis=2, concat_axis=1, tiled=True)
    arrived = arrived.transpose(0, 2, 1, 3).reshape(items, length, -1)
    q_heads = arrived[..., : per_group * HD].reshape(items, length, per_group, HD)
    k_heads = arrived[..., per_group * HD : (per_group + 1) * HD]
    v_heads = arrived[..., (per_group + 1) * HD :]
    outs, lse = attend_forward(q_heads, k_heads, v_heads, seg_items, block)
    attended = (
        outs.transpose(1, 0, 2, 3, 4)
        .reshape(rows_dev, place_dev, length, per_group * HD)
        .transpose(0, 2, 1, 3)
    )
    returned = lax.all_to_all(attended, "seq", split_axis=1, concat_axis=2, tiled=True)
    mixed = returned[:, :, :KVG].reshape(count, QW)
    hidden = x_rows + times_rows(mixed, out_w)
    normed_two = norm_rows(hidden, gain_b).astype(jnp.bfloat16)
    d_result = cotangent.reshape(count, width).astype(jnp.float32)
    gate = jnp.dot(normed_two, gate_w, preferred_element_type=jnp.float32)
    upward = jnp.dot(normed_two, up_w, preferred_element_type=jnp.float32)
    active = (jax.nn.silu(gate) * upward).astype(jnp.bfloat16)
    layer_result = hidden + times_rows(active, down_w)
    d_branch = d_result.astype(jnp.bfloat16)
    d_active = jnp.dot(d_branch, down_w, preferred_element_type=jnp.float32)
    grad_down = token_sum(d_branch, active)
    swiglu_out, swiglu_back = jax.vjp(
        lambda gate_in, up_in: jax.nn.silu(gate_in) * up_in, gate, upward
    )
    d_gate, d_up = swiglu_back(d_active)
    d_gate = d_gate.astype(jnp.bfloat16)
    d_up = d_up.astype(jnp.bfloat16)
    grad_gate = token_sum(normed_two, d_gate)
    grad_up = token_sum(normed_two, d_up)
    d_normed_two = times_rows(d_gate, gate_w) + times_rows(d_up, up_w)
    activations = layer_result.astype(jnp.bfloat16).reshape(rows_dev, len_dev, width)
    second_out, second_back = jax.vjp(norm_rows, hidden, gain_b)
    d_hidden, grad_gain_b = second_back(d_normed_two)
    d_hidden = d_hidden + d_result
    d_attn = d_hidden.astype(jnp.bfloat16)
    grad_out = token_sum(d_attn, mixed)
    d_mixed = jnp.dot(d_attn, out_w, preferred_element_type=jnp.float32).astype(jnp.bfloat16)
    d_pack = jnp.pad(
        d_mixed.reshape(count, KVG, per_group * HD), ((0, 0), (0, places - KVG), (0, 0))
    )
    d_pack = d_pack.reshape(rows_dev, len_dev, places, -1)
    d_arrived = lax.all_to_all(d_pack, "seq", split_axis=2, concat_axis=1, tiled=True)
    d_items = d_arrived.transpose(0, 2, 1, 3).reshape(items, length, per_group, HD)
    d_query, d_key, d_value = attend_backward(
        q_heads, k_heads, v_heads, seg_items, d_items, lse, block
    )
    d_query = d_query.transpose(1, 0, 2, 3, 4).reshape(items, length, per_group * HD)
    d_heads = jnp.concatenate([d_query, d_key, d_value], axis=2).astype(jnp.bfloat16)
    d_heads = d_heads.reshape(rows_dev, place_dev, length, -1).transpose(0, 2, 1, 3)
    d_back = lax.all_to_all(d_heads, "seq", split_axis=1, concat_axis=2, tiled=True)
    d_back = d_back[:, :, :KVG].reshape(count, KVG, -1).astype(jnp.float32)
    d_q_rows = d_back[..., : per_group * HD].reshape(count, QH, HD)
    d_k_rows = d_back[..., per_group * HD : (per_group + 1) * HD]
    d_v_rows = d_back[..., (per_group + 1) * HD :]
    prep_out, prep_back = jax.vjp(
        lambda qkv_in, qs_in, ks_in: heads_prep(qkv_in, qs_in, ks_in, positions),
        qkv,
        q_scale,
        k_scale,
    )
    d_qkv, grad_q_scale, grad_k_scale = prep_back((d_q_rows, d_k_rows, d_v_rows))
    d_qkv = d_qkv.astype(jnp.bfloat16)
    grad_qkv = token_sum(normed, d_qkv)
    d_normed = times_rows(d_qkv, qkv_w)
    first_out, first_back = jax.vjp(norm_rows, x_rows, gain_a)
    d_tokens, grad_gain_a = first_back(d_normed)
    d_tokens = d_tokens + d_hidden
    head_sums = lax.psum((grad_q_scale, grad_k_scale), ("seq", "rep"))
    parts = (
        lax.psum_scatter(grad_gain_a, ("seq", "rep"), scatter_dimension=0, tiled=True),
        lax.psum_scatter(grad_qkv, ("seq", "rep"), scatter_dimension=0, tiled=True),
        lax.psum_scatter(grad_out, ("seq", "rep"), scatter_dimension=0, tiled=True),
        lax.psum_scatter(grad_gain_b, ("seq", "rep"), scatter_dimension=0, tiled=True),
        lax.psum_scatter(grad_gate, ("seq", "rep"), scatter_dimension=0, tiled=True),
        lax.psum_scatter(grad_up, ("seq", "rep"), scatter_dimension=0, tiled=True),
        lax.psum_scatter(grad_down, ("seq", "rep"), scatter_dimension=0, tiled=True),
    )
    return (
        activations,
        d_tokens.reshape(rows_dev, len_dev, width),
        parts[0],
        parts[1],
        parts[2],
        parts[3],
        parts[4],
        parts[5],
        parts[6],
        head_sums[0],
        head_sums[1],
    )


MESH = pl.DeviceIdType.MESH
BF = jnp.bfloat16
F32 = jnp.float32
NEG = -1e30
VMEM_BYTES = 61 * 2**20
QS = 5
DZ = 4
BLK = 128
LEN4 = 512
FFS = 896
BR = 64
HALF = 512
AW = 1024
QKV_W = 640
SCALE = HD ** (-0.5)
FF_TILES = ((0, 256), (256, 256), (512, 256), (768, 128))
QKV_M, OUT_M, DOWN_M, GATE_M, UP_M = range(5)
FF_AT = {DOWN_M: 2 * FFS, GATE_M: 0, UP_M: FFS}


def place():
    s = lax.axis_index("seq")
    r = lax.axis_index("rep")
    return lax.div(s, 2), lax.rem(s, 2), lax.div(r, 2), lax.rem(r, 2)


def dev(x, c, z, y):
    return {"seq": 2 * x + c, "rep": 2 * z + y}


def flip(v, by):
    return v if by == 0 else 1 - v


def near(z):
    return z + 1 - 2 * lax.rem(z, 2)


def inner(z):
    return (z == 1) | (z == 2)


def send(src, dst, send_sem, recv_sem, target):
    pltpu.make_async_remote_copy(
        src_ref=src,
        dst_ref=dst,
        send_sem=send_sem,
        recv_sem=recv_sem,
        device_id=target,
        device_id_type=MESH,
    ).start()


def arrived(ref, sem):
    pltpu.make_async_copy(ref, ref, sem).wait()


def many(first, count):
    return pl.ds(pl.multiple_of(first, count), count)


def rows_of(ref, index, size):
    return ref.at[many(index * size, size)]


def greet(x, c, z, y):
    found = []
    for dz in range(DZ):
        for dx in range(2):
            for dy in range(2):
                for dc in range(2):
                    if (dx or dy or dc) if dz == 0 else dc == 0:
                        found.append(
                            dev(flip(x, dx), flip(c, dc), lax.rem(z + dz, DZ), flip(y, dy))
                        )
    barrier = pltpu.get_barrier_semaphore()
    for target in found:
        pl.semaphore_signal(barrier, inc=1, device_id=target, device_id_type=MESH)
    pl.semaphore_wait(barrier, len(found))


def spread_start(src, spot, ss, rs):
    x, c, z, y = place()
    slot = 2 * x + c
    for k, (dx, dy) in enumerate(((1, 1), (1, 0), (0, 1))):
        send(src, spot, ss.at[k], rs.at[slot], dev(flip(x, dx), y, z, flip(y, dy)))

    @pl.when(c == y)
    def _():
        pltpu.make_async_copy(src, spot, rs.at[slot]).start()

    @pl.when(c != y)
    def _():
        send(src, spot, ss.at[3], rs.at[slot], dev(x, y, z, y))


def spread_wait(block, rs):
    for j in range(4):
        arrived(block, rs.at[j])


def spread_sent(src, ss):
    x, c, z, y = place()
    for k in range(3):
        arrived(src, ss.at[k])

    @pl.when(c != y)
    def _():
        arrived(src, ss.at[3])


BLOCK_ORDER = ((1, 1), (1, 0), (0, 1), (0, 0))


def block_at(order):
    x, c, z, y = place()
    dx, dc = BLOCK_ORDER[order]
    return 2 * flip(x, dx) + flip(c, dc)


def collect_start(order, partial, inbox, ss, rs):
    x, c, z, y = place()
    dx, dc = BLOCK_ORDER[order]
    src = rows_of(partial, block_at(order), BLK)
    slot = 2 * x + y
    spot = inbox.at[slot]
    target = dev(flip(x, dx), flip(c, dc), z, c)
    if dx or dc:
        send(src, spot, ss.at[order], rs.at[slot], target)
        return

    @pl.when(c == y)
    def _():
        pltpu.make_async_copy(src, spot, rs.at[slot]).start()

    @pl.when(c != y)
    def _():
        send(src, spot, ss.at[order], rs.at[slot], target)


def collect_wait(inbox, rs):
    for j in range(4):
        arrived(inbox.at[j], rs.at[j])


def collect_sent(inbox, ss):
    x, c, z, y = place()
    for k in range(3):
        arrived(inbox.at[0], ss.at[k])

    @pl.when(c != y)
    def _():
        arrived(inbox.at[0], ss.at[3])


def inbox_sum(inbox):
    return (inbox[0].astype(F32) + inbox[1].astype(F32)) + (
        inbox[2].astype(F32) + inbox[3].astype(F32)
    )


def mm(left, right):
    return lax.dot_general(left, right, (((1,), (0,)), ((), ())), preferred_element_type=F32)


def mm_nt(left, right):
    return lax.dot_general(left, right, (((1,), (1,)), ((), ())), preferred_element_type=F32)


def mm_tn(left, right):
    return lax.dot_general(left, right, (((0,), (0,)), ((), ())), preferred_element_type=F32)


def group_of(local_head):
    x, c, z, y = place()
    return jnp.where(local_head + 2 * x + y >= 4, 1, 0)


def layer_body(
    tok, cot, small, wq, wo, wg, wu, wd,
    act_o, dtok_o, gate_o, up_o, down_o, ga_o, vec_o, gr,
    wap, smallf, xf, n1, wav, w3, dyf, n2f, part, inbox, dact, active, dgu,
    qkvt, dqkvt, dqkv, qt, kt, kk, vt, vv, lse, att, cs, grow, hid, blk, dot_s, dkt, dvt,
    help_f, help_a, arecv, ar, vec, vecr, vr, gp2,
    sp_ss, sp_rs, co_ss, co_rs, w_ss, w_rs, f_ss, c_ss, c_rs, g_ss, g_rs, h_ss, h_rs, o_ss, o_rs, v_ss, v_rs, loc,
    ready,
):
    x, c, z, y = place()
    shard = 2 * x + y
    me = (2 * x + c) * 2 * DZ + 2 * z + y
    mid = inner(z)
    sibling = dev(x, 1 - c, z, y)
    pair, across = near(z), DZ - 1 - z
    SMALL, TOK, COT, N2, DAB = range(5)
    OUT, DN, YY, DT = range(4)

    def own_piece(m, to_shard):
        if m == QKV_M:
            return wap.at[to_shard, :, pl.ds(0, QKV_W)]
        if m == OUT_M:
            return wap.at[to_shard, :, pl.ds(QKV_W, AW - QKV_W)]
        return {DOWN_M: wd, GATE_M: wg, UP_M: wu}[m].at[
            :, pl.ds(pl.multiple_of(to_shard * FFS, 128), FFS)
        ]

    def held(m, first, count):
        rows = many(first, count)
        if m == QKV_M:
            return wav.at[rows, pl.ds(0, QKV_W)]
        if m == OUT_M:
            return wav.at[rows, pl.ds(QKV_W, AW - QKV_W)]
        return w3.at[rows, pl.ds(FF_AT[m], FFS)]

    def weights_start(m):
        def to_plane(tz, base):
            for dx in range(2):
                for dy in range(2):
                    tx, ty = flip(x, dx), flip(y, dy)
                    send(
                        own_piece(m, 2 * tx + ty),
                        held(m, me * BR, BR),
                        w_ss.at[m, base + 2 * dx + dy],
                        w_rs.at[m, z * 4 + shard],
                        dev(tx, c, tz, ty),
                    )

        to_plane(pair, 4)

        @pl.when(mid)
        def _():
            to_plane(across, 8)

        for dx in range(2):
            for dy in range(2):
                src = own_piece(m, 2 * flip(x, dx) + flip(y, dy))
                spot = held(m, me * BR, BR)
                sem = w_rs.at[m, z * 4 + shard]
                if dx or dy:
                    send(src, spot, w_ss.at[m, 2 * dx + dy], sem, dev(flip(x, dx), c, z, flip(y, dy)))
                else:
                    pltpu.make_async_copy(src, spot, sem).start()

    def pass_on(m, from_plane, to_plane, base):
        for tx in range(2):
            for ty in range(2):
                k = 2 * tx + ty
                sem = w_rs.at[m, from_plane * 4 + k]
                piece = held(m, ((2 * tx + c) * 2 * DZ + 2 * from_plane + ty) * BR, BR)
                arrived(piece, sem)
                send(piece, piece, f_ss.at[m, base + k], sem, dev(x, c, to_plane, y))

    def weights_pass_near(m):
        @pl.when(mid)
        def _():
            pass_on(m, pair, across, 0)
            pass_on(m, across, pair, 4)

    def weights_pass_far(m):
        @pl.when(mid)
        def _():
            pass_on(m, DZ - 1 - pair, pair, 8)

    def weights_swap(m):
        @pl.when(jnp.logical_not(mid))
        def _():
            for i in range(4 * DZ):
                arrived(held(m, 0, BR), w_rs.at[m, i])

        @pl.when(mid)
        def _():
            for k in range(4):
                arrived(held(m, 0, BR), w_rs.at[m, z * 4 + k])

        for tx in range(2):
            half = held(m, (2 * tx + c) * HALF, HALF)
            send(half, half, c_ss.at[m, tx], c_rs.at[m, tx], sibling)

    def weights_wait(m):
        for tx in range(2):
            arrived(held(m, 0, HALF), c_rs.at[m, tx])

    def weights_sent(m):
        for k in range(1, 8):
            arrived(held(m, 0, BR), w_ss.at[m, k])

        @pl.when(mid)
        def _():
            for k in range(8, 12):
                arrived(held(m, 0, BR), w_ss.at[m, k])
            for k in range(12):
                arrived(held(m, 0, BR), f_ss.at[m, k])

        for tx in range(2):
            arrived(held(m, 0, HALF), c_ss.at[m, tx])

    def slot_of(to_plane):
        return shard * 3 + z - jnp.where(to_plane >= 2, 1, 0)

    def grads_to_plane(kind, piece, inbox_at, tz, base):
        spot = inbox_at(slot_of(tz))
        for dx in range(2):
            for dy in range(2):
                tx, ty = flip(x, dx), flip(y, dy)
                send(
                    piece(tz, tx, ty),
                    spot,
                    o_ss.at[kind, base + 2 * dx + dy],
                    o_rs.at[kind, slot_of(tz)],
                    dev(tx, c, tz, ty),
                )

    def grads_start(kind, piece, inbox_at, pair_rows, help_ref):
        @pl.when(jnp.logical_not(mid))
        def _():
            for i, tz in enumerate((DZ - 1 - pair, DZ - 1 - z)):
                for tx in range(2):
                    send(
                        pair_rows(tx, tz),
                        help_ref.at[i, pl.ds(tx * 2 * BR, 2 * BR)],
                        h_ss.at[kind, 2 * i + tx],
                        h_rs.at[kind, 2 * i + tx],
                        dev(x, c, pair, y),
                    )

        grads_to_plane(kind, piece, inbox_at, pair, 4)
        spot = inbox_at(slot_of(z))
        sem = o_rs.at[kind, slot_of(z)]
        for dx in range(2):
            for dy in range(2):
                tx, ty = flip(x, dx), flip(y, dy)
                if dx or dy:
                    send(piece(z, tx, ty), spot, o_ss.at[kind, 2 * dx + dy], sem, dev(tx, c, z, ty))
                else:
                    pltpu.make_async_copy(piece(z, x, y), spot, sem).start()

    def grads_join(kind, piece, inbox_at, pair_rows, help_ref):
        @pl.when(mid)
        def _():
            for i, tz in enumerate((across, DZ - 1 - pair)):
                for tx in range(2):
                    rows = pair_rows(tx, tz)
                    arrived(rows, h_rs.at[kind, 2 * i + tx])
                    rows[...] = (
                        rows[...].astype(F32)
                        + help_ref[i, tx * 2 * BR : (tx + 1) * 2 * BR, :].astype(F32)
                    ).astype(BF)
                grads_to_plane(kind, piece, inbox_at, tz, 8 + 4 * i)

    def grads_wait(kind, inbox_at, pair_rows):
        for k in range(12):
            arrived(inbox_at(0), o_rs.at[kind, k])
        for k in range(1, 8):
            arrived(inbox_at(0), o_ss.at[kind, k])

        @pl.when(mid)
        def _():
            for k in range(8, 16):
                arrived(inbox_at(0), o_ss.at[kind, k])

        @pl.when(jnp.logical_not(mid))
        def _():
            for k in range(4):
                arrived(pair_rows(0, 0), h_ss.at[kind, k])

    def grad_refs(ref, first_row, lo, width, inbox, helper):
        lanes = pl.ds(lo, width)

        def piece(tz, tx, ty):
            return ref.at[many(first_row + ((tx * DZ + tz) * 2 + ty) * BR, BR), lanes]

        def inbox_at(slot):
            return inbox.at[many(slot * BR, BR), lanes]

        def pair_rows(tx, tz):
            return ref.at[many(first_row + (tx * DZ + tz) * 2 * BR, 2 * BR), lanes]

        return piece, inbox_at, pair_rows, helper

    ffn_refs = [
        grad_refs(w3, 1024, j * FFS, FFS, gr, help_f.at[j]) for j in range(3)
    ]
    out_refs = grad_refs(arecv, 0, QKV_W, AW - QKV_W, ar, help_a.at[:, :, pl.ds(QKV_W, AW - QKV_W)])
    qkv_refs = grad_refs(arecv, 0, 0, QKV_W, ar, help_a.at[:, :, pl.ds(0, QKV_W)])
    kind_refs = ffn_refs + [out_refs, qkv_refs]

    def join(kind):
        grads_join(kind, *kind_refs[kind])

    def start(kind):
        grads_start(kind, *kind_refs[kind])

    greet(x, c, z, y)
    spot = smallf.at[:, many((2 * x + c) * BLK, BLK)]
    spread_start(small, spot, sp_ss.at[SMALL], sp_rs.at[SMALL])
    spread_start(tok, rows_of(xf, 2 * x + c, BLK), sp_ss.at[TOK], sp_rs.at[TOK])
    turned = jnp.transpose(small[...])
    lane = lax.broadcasted_iota(jnp.int32, (BR, 64), 1)
    gains = jnp.where(lane == 0, turned[0:64, 0:1], jnp.where(lane == 1, turned[0:64, 1:2], 0.0))
    gq, gk, fr = turned[0:64, 2:3], turned[0:64, 3:4], turned[0:32, 5:6]
    for t in range(4):
        wap[t, :, 0:320] = wq[:, 320 * t : 320 * t + 320]
        wap[t, :, 320:448] = wq[:, QW + 64 * t : QW + 64 * t + 128]
        wap[t, :, 448:576] = wq[:, QW + KW + 64 * t : QW + KW + 64 * t + 128]
        wap[t, :, 576:640] = gains.astype(BF)
        wap[t, :, 640:960] = wo[:, 320 * t : 320 * t + 320]
        wap[t, :, 960:1024] = jnp.zeros((BR, 64), BF)
    weights_start(QKV_M)
    weights_start(OUT_M)
    spread_wait(spot, sp_rs.at[SMALL])
    seg_row = smallf[4:5, :]
    seg_col = jnp.transpose(smallf[...])[:, 4:5]
    key_at = lax.broadcasted_iota(jnp.int32, (LEN4, LEN4), 0)
    query_at = lax.broadcasted_iota(jnp.int32, (LEN4, LEN4), 1)
    allowed = (key_at <= query_at) & (seg_col == seg_row)
    earlier = jnp.sum(jnp.where(seg_col < seg_row, 1.0, 0.0), axis=0, keepdims=True)
    index = lax.broadcasted_iota(jnp.int32, (1, LEN4), 1).astype(F32)
    angles = fr * (index - earlier)
    cs[0:32, :] = jnp.cos(angles)
    cs[32:64, :] = jnp.sin(angles)
    spread_wait(rows_of(xf, 0, BLK), sp_rs.at[TOK])
    weights_pass_near(QKV_M)
    weights_pass_far(QKV_M)
    weights_pass_near(OUT_M)
    weights_pass_far(OUT_M)
    for m in (DOWN_M, GATE_M, UP_M):
        weights_start(m)
    spread_start(cot, rows_of(dyf, 2 * x + c, BLK), sp_ss.at[COT], sp_rs.at[COT])
    weights_swap(QKV_M)
    weights_swap(OUT_M)
    weights_wait(QKV_M)
    grow[...] = jnp.transpose(wav[:, 512:640].astype(F32))[64:72, :]

    @pl.loop(0, 4)
    def _(j):
        rows = many(j * BLK, BLK)
        v = xf[rows, :].astype(F32)
        n1[rows, :] = (
            v * lax.rsqrt(jnp.mean(v * v, axis=1, keepdims=True) + norm_eps) * grow[0:1, :]
        ).astype(BF)

    @pl.loop(0, 5)
    def _(j):
        wide = many(j * 128, 128)
        qkvt[wide, :] = jnp.transpose(mm(n1[...], wav[:, wide]))

    def rotated(v, gain):
        cos, sin = cs[0:32, :], cs[32:64, :]
        v = v * lax.rsqrt(jnp.mean(v * v, axis=0, keepdims=True) + norm_eps) * gain
        first, second = v[0:32, :], v[32:64, :]
        return first * cos - second * sin, second * cos + first * sin

    for h in range(QS):
        first, second = rotated(qkvt[h * 64 : h * 64 + 64, :], gq)
        qt[h, 0:32, :] = first.astype(BF)
        qt[h, 32:64, :] = second.astype(BF)
    for g in range(2):
        base = QS * 64 + g * 64
        first, second = rotated(qkvt[base : base + 64, :], gk)
        both = jnp.concatenate([first, second], axis=0)
        kt[g] = both.astype(BF)
        kk[g] = jnp.transpose(both).astype(BF)
        value = qkvt[base + 128 : base + 192, :]
        vt[g] = value.astype(BF)
        vv[g] = jnp.transpose(value).astype(BF)
    dqkvt[QS * 64 : 384, :] = jnp.zeros((384 - QS * 64, LEN4), F32)
    for h in range(QS):
        g = group_of(h)
        scores = jnp.where(allowed, mm(kk[g], qt[h]) * SCALE, NEG)
        top = jnp.max(scores, axis=0, keepdims=True)
        weights = jnp.exp(scores - top)
        total = jnp.sum(weights, axis=0, keepdims=True)
        lse[h : h + 1, :] = top + jnp.log(total)
        dqkvt[h * 64 : h * 64 + 64, :] = mm(vt[g], (weights / total).astype(BF))
    att[...] = jnp.transpose(dqkvt[0:384, :]).astype(BF)
    weights_wait(OUT_M)
    for order in range(4):
        rows = many(block_at(order) * BLK, BLK)
        part[0, rows, :] = mm_nt(att[rows, :], wav[:, QKV_W:AW]).astype(BF)
        collect_start(order, part.at[0], inbox.at[0], co_ss.at[OUT], co_rs.at[OUT])
    for m in (DOWN_M, GATE_M, UP_M):
        weights_pass_near(m)
    collect_wait(inbox.at[0], co_rs.at[OUT])
    hidden = tok[...].astype(F32) + inbox_sum(inbox.at[0])
    hid[...] = hidden
    blk[0] = (
        hidden
        * lax.rsqrt(jnp.mean(hidden * hidden, axis=1, keepdims=True) + norm_eps)
        * grow[1:2, :]
    ).astype(BF)
    spread_start(blk.at[0], rows_of(n2f, 2 * x + c, BLK), sp_ss.at[N2], sp_rs.at[N2])
    for m in (DOWN_M, GATE_M, UP_M):
        weights_pass_far(m)
    weights_swap(DOWN_M)
    spread_wait(rows_of(dyf, 0, BLK), sp_rs.at[COT])
    weights_wait(DOWN_M)
    for lo, wide in FF_TILES:
        dact[:, lo : lo + wide] = mm(dyf[...], w3[:, 2 * FFS + lo : 2 * FFS + lo + wide])
    weights_swap(GATE_M)
    weights_swap(UP_M)
    spread_wait(rows_of(n2f, 0, BLK), sp_rs.at[N2])
    weights_wait(GATE_M)
    weights_wait(UP_M)
    for lo, wide in FF_TILES:
        gate = mm(n2f[...], w3[:, lo : lo + wide])
        upward = mm(n2f[...], w3[:, FFS + lo : FFS + lo + wide])
        sig = 1.0 / (1.0 + jnp.exp(-gate))
        silu = gate * sig
        grad = dact[:, lo : lo + wide]
        active[:, lo : lo + wide] = (silu * upward).astype(BF)
        dgu[:, lo : lo + wide] = (grad * upward * (sig * (1.0 + gate * (1.0 - sig)))).astype(BF)
        dgu[:, FFS + lo : FFS + lo + wide] = (grad * silu).astype(BF)
    for order in range(4):
        rows = many(block_at(order) * BLK, BLK)

        @pl.loop(0, 4)
        def _(j):
            wide = many(j * 512, 512)
            part[1, rows, wide] = mm_nt(dgu[rows, :], w3[wide, 0 : 2 * FFS]).astype(BF)

        collect_start(order, part.at[1], inbox.at[1], co_ss.at[DN], co_rs.at[DN])
    collect_sent(inbox.at[0], co_ss.at[OUT])
    for order in range(4):
        rows = many(block_at(order) * BLK, BLK)

        @pl.loop(0, 4)
        def _(j):
            wide = many(j * 512, 512)
            part[0, rows, wide] = mm_nt(active[rows, :], w3[wide, 2 * FFS : 3 * FFS]).astype(BF)

        collect_start(order, part.at[0], inbox.at[0], co_ss.at[YY], co_rs.at[YY])
    for m in range(5):
        weights_sent(m)
    pl.semaphore_signal(ready, inc=1, device_id=sibling, device_id_type=MESH)

    def ffn_grads(core, row, j):
        first = (2 * lax.div(row, 2) + core) * HALF + lax.rem(row, 2) * 256
        wide = many(first, 256)
        if j < 2:
            return mm_tn(n2f[:, wide], dgu[:, j * FFS : (j + 1) * FFS])
        return mm_tn(dyf[:, wide], active[...])

    for j in range(3):
        lanes = pl.ds(j * FFS, FFS)

        @pl.loop(0, 4)
        def _(row):
            w3[many(row * 256, 256), lanes] = ffn_grads(1 - c, row, j).astype(BF)

        if j == 0:
            pl.semaphore_wait(ready, 1)
        send(
            w3.at[pl.ds(0, 1024), lanes], w3.at[pl.ds(1024, 1024), lanes], g_ss.at[j], g_rs.at[j], sibling
        )
    collect_wait(inbox.at[1], co_rs.at[DN])
    dn = inbox_sum(inbox.at[1])
    h = hid[...]
    r = lax.rsqrt(jnp.mean(h * h, axis=1, keepdims=True) + norm_eps)
    gp2[...] = jnp.broadcast_to(jnp.sum(dn * h * r, axis=0, keepdims=True), gp2.shape)
    a = dn * grow[1:2, :]
    dh = cot[...].astype(F32) + r * (a - h * (r * r * jnp.mean(a * h, axis=1, keepdims=True)))
    dtok_o[...] = dh
    blk[1] = dh.astype(BF)
    spread_start(blk.at[1], rows_of(xf, 2 * x + c, BLK), sp_ss.at[DAB], sp_rs.at[DAB])
    for j in range(3):
        lanes = pl.ds(j * FFS, FFS)
        arrived(w3.at[pl.ds(1024, 1024), lanes], g_rs.at[j])

        @pl.loop(0, 4)
        def _(row):
            rows = many(1024 + row * 256, 256)
            w3[rows, lanes] = (ffn_grads(c, row, j) + w3[rows, lanes].astype(F32)).astype(BF)

        start(j)
    collect_wait(inbox.at[0], co_rs.at[YY])
    act_o[...] = (hid[...] + inbox_sum(inbox.at[0])).astype(BF)
    spread_wait(rows_of(xf, 0, BLK), sp_rs.at[DAB])
    dot_s[...] = jnp.transpose(mm(xf[...], wav[:, QKV_W:AW]).astype(BF).astype(F32)).astype(BF)
    dkt[...] = jnp.zeros_like(dkt)
    dvt[...] = jnp.zeros_like(dvt)

    def unrotated(first, second, raw, gain):
        cos, sin = cs[0:32, :], cs[32:64, :]
        d_first = first * cos + second * sin
        d_second = second * cos - first * sin
        d = jnp.concatenate([d_first, d_second], axis=0)
        r = lax.rsqrt(jnp.mean(raw * raw, axis=0, keepdims=True) + norm_eps)
        d_gain = jnp.sum(d * raw * r, axis=1, keepdims=True)
        a = d * gain
        return r * (a - raw * (r * r * jnp.mean(a * raw, axis=0, keepdims=True))), d_gain

    dq_gain = jnp.zeros((64, 1), F32)
    for h in range(QS):
        g = group_of(h)
        scores = mm(kk[g], qt[h]) * SCALE
        p = jnp.where(allowed, jnp.exp(scores - lse[h : h + 1, :]), 0.0)
        d_out = dot_s[h * 64 : h * 64 + 64, :]
        dvt[g] += mm_nt(d_out, p.astype(BF))
        dp = mm(vv[g], d_out)
        ds = (p * (dp - jnp.sum(p * dp, axis=0, keepdims=True))).astype(BF)
        dkt[g] += mm_nt(qt[h], ds) * SCALE
        dq = (mm(kt[g], ds) * SCALE).astype(BF).astype(F32)
        d, more = unrotated(dq[0:32, :], dq[32:64, :], qkvt[h * 64 : h * 64 + 64, :], gq)
        dq_gain = dq_gain + more
        dqkvt[h * 64 : h * 64 + 64, :] = d
        if h in JOIN_AFTER:
            join(JOIN_AFTER[h])
    dk_gain = jnp.zeros((64, 1), F32)
    for g in range(2):
        base = QS * 64 + g * 64
        dk = dkt[g].astype(BF).astype(F32)
        d, more = unrotated(dk[0:32, :], dk[32:64, :], qkvt[base : base + 64, :], gk)
        dk_gain = dk_gain + more
        dqkvt[base : base + 64, :] = d
        dqkvt[base + 128 : base + 192, :] = dvt[g]
    dqkvt[576:640, :] = jnp.zeros((64, LEN4), F32)
    dqkv[...] = jnp.transpose(dqkvt[...]).astype(BF)
    collect_sent(inbox.at[1], co_ss.at[DN])
    for order in range(4):
        rows = many(block_at(order) * BLK, BLK)
        part[1, rows, :] = mm_nt(dqkv[rows, :], wav[:, 0:QKV_W]).astype(BF)
        collect_start(order, part.at[1], inbox.at[1], co_ss.at[DT], co_rs.at[DT])

    def att_grads(core, row, kind):
        first = (2 * lax.div(row, 2) + core) * HALF + lax.rem(row, 2) * 256
        wide = many(first, 256)
        if kind == 4:
            return mm_tn(n1[:, wide], dqkv[...])
        return mm_tn(xf[:, wide], att[...])

    att_lanes = {k: pl.ds(ATT_LO[k], ATT_WIDE[k]) for k in (3, 4)}
    for kind in (3, 4):

        @pl.loop(0, 4)
        def _(row):
            side = lax.div(row, 2) * AW + ATT_LO[kind]
            dyf[many(lax.rem(row, 2) * 256, 256), pl.ds(pl.multiple_of(side, 128), ATT_WIDE[kind])] = (
                att_grads(1 - c, row, kind).astype(BF)
            )

        for side in range(2):
            send(
                dyf.at[:, pl.ds(side * AW + ATT_LO[kind], ATT_WIDE[kind])],
                arecv.at[pl.ds(side * HALF, HALF), att_lanes[kind]],
                g_ss.at[2 * kind - 3 + side],
                g_rs.at[2 * kind - 3 + side],
                sibling,
            )
    for kind in (3, 4):
        for side in range(2):
            arrived(arecv.at[pl.ds(0, HALF), att_lanes[kind]], g_rs.at[2 * kind - 3 + side])

        @pl.loop(0, 4)
        def _(row):
            rows = many(row * 256, 256)
            arecv[rows, att_lanes[kind]] = (
                att_grads(c, row, kind) + arecv[rows, att_lanes[kind]].astype(F32)
            ).astype(BF)

        start(kind)
    collect_wait(inbox.at[1], co_rs.at[DT])
    dn = inbox_sum(inbox.at[1])
    xv = tok[...].astype(F32)
    r = lax.rsqrt(jnp.mean(xv * xv, axis=1, keepdims=True) + norm_eps)
    gain_a = jnp.sum(dn * xv * r, axis=0, keepdims=True)
    b = dn * grow[0:1, :]
    dtok_o[...] += r * (b - xv * (r * r * jnp.mean(b * xv, axis=1, keepdims=True)))
    qk = jnp.transpose(
        jnp.concatenate(
            [jnp.broadcast_to(dq_gain, (64, 128)), jnp.broadcast_to(dk_gain, (64, 128))], axis=0
        )
    )
    gain_b = gp2[0:1, :]
    vec[...] = jnp.zeros_like(vec)
    for i in range(4 * DZ):
        for half in range(2):
            at = (((i // (2 * DZ)) * 2 + half) * 2 * DZ + i % (2 * DZ)) * BR
            vec[half, i, 0:4, 0:64] = jnp.concatenate(
                [gain_a[:, at : at + BR], gain_b[:, at : at + BR], qk[0:1, 0:64], qk[0:1, 64:128]], axis=0
            )
    send(vec.at[1 - c], vecr, g_ss.at[7], g_rs.at[7], sibling)
    arrived(vecr, g_rs.at[7])
    vecr[...] += vec[c]
    source = shard * DZ + z
    for dz in range(DZ):
        for dx in range(2):
            for dy in range(2):
                tx, ty, tz = flip(x, dx), flip(y, dy), lax.rem(z + dz, DZ)
                src = vecr.at[(tx * DZ + tz) * 2 + ty]
                k = (dz * 2 + dx) * 2 + dy
                if k == 0:
                    pltpu.make_async_copy(src, vr.at[source], v_rs.at[source]).start()
                else:
                    send(src, vr.at[source], v_ss.at[k], v_rs.at[source], dev(tx, c, tz, ty))
    join(3)
    join(4)
    for j in range(3):
        grads_wait(j, *kind_refs[j][1:3])
    for j in range(3):
        arrived(w3.at[pl.ds(0, 1024), pl.ds(j * FFS, FFS)], g_ss.at[j])
    load = pltpu.make_async_copy(gr, w3.at[pl.ds(0, 12 * BR)], loc.at[0])
    load.start()
    load.wait()

    def three(ref, t, lo, width):
        lanes = pl.ds(lo, width)
        at = t * 3 * BR
        return (
            ref[at : at + BR, lanes].astype(F32) + ref[at + BR : at + 2 * BR, lanes].astype(F32)
        ) + ref[at + 2 * BR : at + 3 * BR, lanes].astype(F32)

    leave = []
    for j, out in enumerate((gate_o, up_o, down_o)):
        for t in range(4):
            rows = pl.ds((j % 2) * 4 * BR + t * BR, BR)
            if j == 2:
                leave[t].wait()
            dact[rows, :] = three(w3, t, j * FFS, FFS)
            leave.append(
                pltpu.make_async_copy(
                    dact.at[rows], out.at[:, pl.ds(t * FFS, FFS)], loc.at[1 + 4 * j + t]
                )
            )
            leave[-1].start()
    for j in (3, 4):
        grads_wait(j, *kind_refs[j][1:3])
    for t in range(4):
        ga_o[t] = three(ar, t, 0, AW)
    for i in range(4 * DZ):
        arrived(vr.at[0], v_rs.at[i])
    for i in range(1, 4 * DZ):
        arrived(vr.at[0], v_ss.at[i])
    for copy in leave[4:]:
        copy.wait()
    vec_o[...] = jnp.sum(vr[...], axis=0)
    for j in (3, 4):
        for side in range(2):
            arrived(arecv.at[pl.ds(0, HALF), att_lanes[j]], g_ss.at[2 * j - 3 + side])
    arrived(vecr, g_ss.at[7])
    spread_sent(small, sp_ss.at[SMALL])
    spread_sent(tok, sp_ss.at[TOK])
    spread_sent(cot, sp_ss.at[COT])
    spread_sent(blk.at[0], sp_ss.at[N2])
    spread_sent(blk.at[1], sp_ss.at[DAB])
    collect_sent(inbox.at[0], co_ss.at[YY])
    collect_sent(inbox.at[1], co_ss.at[DT])


JOIN_AFTER = {1: 0, 3: 1, 4: 2}
ATT_LO = {3: QKV_W, 4: 0}
ATT_WIDE = {3: AW - QKV_W, 4: QKV_W}


def plane_plan(
    tokens, segment_ids, cotangent, attn_gain, w_qkv, w_out, ffn_gain, w_gate, w_up, w_down, q_gain, k_gain
):
    width = tokens.shape[-1]
    freqs = rope_base ** (-jnp.arange(32, dtype=jnp.float32) * 2.0 / HD)

    def lanes(v):
        v = v.astype(F32).reshape(1, -1)
        return jnp.pad(v, ((0, 0), (0, BLK - v.shape[1])))

    small = jnp.concatenate(
        [lanes(v) for v in (attn_gain, ffn_gain, q_gain, k_gain, segment_ids, freqs)]
        + [jnp.zeros((2, BLK), F32)],
        axis=0,
    )
    dma = pltpu.SemaphoreType.DMA
    vm = pltpu.VMEM
    far, close = pl.BlockSpec(memory_space=pl.ANY), pl.BlockSpec(memory_space=pltpu.VMEM)
    act, dtok, gate, up, down, ga, vec, _ = pl.pallas_call(
        layer_body,
        out_shape=[
            jax.ShapeDtypeStruct((BLK, width), BF),
            jax.ShapeDtypeStruct((BLK, width), F32),
            jax.ShapeDtypeStruct((BR, 4 * FFS), F32),
            jax.ShapeDtypeStruct((BR, 4 * FFS), F32),
            jax.ShapeDtypeStruct((BR, 4 * FFS), F32),
            jax.ShapeDtypeStruct((4, BR, AW), F32),
            jax.ShapeDtypeStruct((8, BLK), F32),
            jax.ShapeDtypeStruct((12 * BR, 3 * FFS), BF),
        ],
        in_specs=[close] * 5 + [far] * 3,
        out_specs=[close] * 2 + [far] * 3 + [close] * 2 + [far],
        scratch_shapes=[
            vm((4, BR, AW), BF),
            vm((8, LEN4), F32),
            vm((LEN4, width), BF),
            vm((LEN4, width), BF),
            vm((2048, AW), BF),
            vm((2048, 3 * FFS), BF),
            vm((LEN4, width), BF),
            vm((LEN4, width), BF),
            vm((2, LEN4, width), BF),
            vm((2, 4, BLK, width), BF),
            vm((LEN4, FFS), F32),
            vm((LEN4, FFS), BF),
            vm((LEN4, 2 * FFS), BF),
            vm((QKV_W, LEN4), F32),
            vm((QKV_W, LEN4), F32),
            vm((LEN4, QKV_W), BF),
            vm((QS, 64, LEN4), BF),
            vm((2, 64, LEN4), BF),
            vm((2, LEN4, 64), BF),
            vm((2, 64, LEN4), BF),
            vm((2, LEN4, 64), BF),
            vm((8, LEN4), F32),
            vm((LEN4, 384), BF),
            vm((64, LEN4), F32),
            vm((8, width), F32),
            vm((BLK, width), F32),
            vm((2, BLK, width), BF),
            vm((384, LEN4), BF),
            vm((2, 64, LEN4), F32),
            vm((2, 64, LEN4), F32),
            vm((3, 2, 4 * BR, FFS), BF),
            vm((2, 4 * BR, AW), BF),
            vm((1024, AW), BF),
            vm((12 * BR, AW), BF),
            vm((2, 4 * DZ, 8, BLK), F32),
            vm((4 * DZ, 8, BLK), F32),
            vm((4 * DZ, 8, BLK), F32),
            vm((8, width), F32),
            dma((5, 4)), dma((5, 4)),
            dma((4, 4)), dma((4, 4)),
            dma((5, 12)), dma((5, 16)), dma((5, 12)),
            dma((5, 2)), dma((5, 2)),
            dma((8,)), dma((8,)),
            dma((5, 4)), dma((5, 4)),
            dma((5, 16)), dma((5, 12)),
            dma((16,)), dma((16,)),
            dma((13,)),
            pltpu.SemaphoreType.REGULAR,
        ],
        compiler_params=pltpu.CompilerParams(
            collective_id=0, has_side_effects=True, vmem_limit_bytes=VMEM_BYTES
        ),
    )(
        tokens.reshape(BLK, width), cotangent.reshape(BLK, width), small, w_qkv, w_out, w_gate, w_up, w_down
    )
    none = jnp.zeros((BR, 64), F32)

    def groups(at):
        first = jnp.concatenate([ga[t][:, at : at + 64] for t in range(4)] + [none], axis=1)
        second = jnp.concatenate([none] + [ga[t][:, at + 64 : at + 128] for t in range(4)], axis=1)
        return first + second

    g_qkv = jnp.concatenate([ga[t][:, 0:320] for t in range(4)] + [groups(320), groups(448)], axis=1)
    g_out = jnp.concatenate([ga[t][:, 640:960] for t in range(4)], axis=1)
    return (
        act.reshape(tokens.shape),
        dtok.reshape(tokens.shape),
        vec[0, :64],
        g_qkv,
        g_out,
        vec[1, :64],
        gate,
        up,
        down,
        vec[2, :64],
        vec[3, :64],
    )


def solution(mesh):
    in_specs = (
        P("rep", "seq", None),
        P("rep", "seq"),
        P("rep", "seq", None),
        P(("seq", "rep")),
        P(("seq", "rep"), None),
        P(("seq", "rep"), None),
        P(("seq", "rep")),
        P(("seq", "rep"), None),
        P(("seq", "rep"), None),
        P(("seq", "rep"), None),
        P(),
        P(),
    )
    out_specs = (
        P("rep", "seq", None),
        P("rep", "seq", None),
        P(("seq", "rep")),
        P(("seq", "rep"), None),
        P(("seq", "rep"), None),
        P(("seq", "rep")),
        P(("seq", "rep"), None),
        P(("seq", "rep"), None),
        P(("seq", "rep"), None),
        P(),
        P(),
    )
    planes = mesh.shape["seq"] == 4 and mesh.shape["rep"] == 8
    body = plane_plan if planes else shards
    return jax.shard_map(body, mesh=mesh, in_specs=in_specs, out_specs=out_specs, check_vma=False)
```

```python
import jax
import jax.numpy as jnp
from jax import lax
from jax.experimental import pallas as pl
from jax.experimental.pallas import tpu as pltpu
from jax.sharding import PartitionSpec as P

QH = 20
KVG = 5
HD = 64
QW = 1280
KW = 320


norm_eps = 1e-06
rope_base = 10000.0


def norm_rows(value_matrix, gain):
    return (
        value_matrix
        * lax.rsqrt(jnp.mean(value_matrix * value_matrix, axis=-1, keepdims=True) + norm_eps)
        * gain
    )


def rotate_heads(value_matrix, positions):
    half = value_matrix.shape[-1] // 2
    freqs = rope_base ** (-jnp.arange(half, dtype=jnp.float32) * 2.0 / value_matrix.shape[-1])
    angles = positions.astype(jnp.float32)[:, None] * freqs[None, :]
    cosine = jnp.cos(angles)[:, None, :]
    sine = jnp.sin(angles)[:, None, :]
    first = value_matrix[..., :half]
    second = value_matrix[..., half:]
    return jnp.concatenate(
        [first * cosine - second * sine, second * cosine + first * sine], axis=-1
    )


def heads_prep(qkv, q_scale, k_scale, positions):
    count = qkv.shape[0]
    query = qkv[:, :QW].reshape(count, QH, HD)
    key = qkv[:, QW : QW + KW].reshape(count, KVG, HD)
    value = qkv[:, QW + KW :].reshape(count, KVG, HD)
    query = rotate_heads(norm_rows(query, q_scale), positions)
    key = rotate_heads(norm_rows(key, k_scale), positions)
    return (query, key, value)


def times_rows(left, right):
    return lax.dot_general(
        left, right, (((1,), (1,)), ((), ())), preferred_element_type=jnp.float32
    )


def token_sum(left, right):
    return lax.dot_general(
        left, right, (((0,), (0,)), ((), ())), preferred_element_type=jnp.float32
    )


def block_scores(query_block, key_matrix, seg_row, start, score_scale):
    width = query_block.shape[1]
    length = key_matrix.shape[1]
    logit_scores = (
        jnp.einsum("zjfr,zyr->zfjy", query_block, key_matrix, preferred_element_type=jnp.float32)
        * score_scale
    )
    rows = start + jnp.arange(width, dtype=jnp.int32)
    cols = jnp.arange(length, dtype=jnp.int32)
    seg_blk = lax.dynamic_slice_in_dim(seg_row, start, width, 1)
    allowed = (cols[None, None, :] <= rows[None, :, None]) & (
        seg_row[:, None, :] == seg_blk[:, :, None]
    )
    return jnp.where(allowed[:, None], logit_scores, -1e30)


def attend_forward(query, key_matrix, value_matrix, seg_row, block):
    length = key_matrix.shape[1]
    score_scale = HD ** (-0.5)

    def one_block(start):
        query_block = lax.dynamic_slice_in_dim(query, start, block, 1)
        logit_scores = block_scores(query_block, key_matrix, seg_row, start, score_scale)
        top = jnp.max(logit_scores, axis=-1, keepdims=True)
        weights = jnp.exp(logit_scores - top)
        total = jnp.sum(weights, axis=-1, keepdims=True)
        attention_probabilities = (weights / total).astype(jnp.bfloat16)
        layer_result = jnp.einsum(
            "szjr,srn->sjzn",
            attention_probabilities,
            value_matrix,
            preferred_element_type=jnp.float32,
        )
        return (layer_result.astype(jnp.bfloat16), (top + jnp.log(total))[..., 0])

    starts = jnp.arange(0, length, block, dtype=jnp.int32)
    return lax.map(one_block, starts)


def attend_backward(query, key_matrix, value_matrix, seg_row, grads_out, lse, block):
    length = key_matrix.shape[1]
    score_scale = HD ** (-0.5)

    def one_block(carry, item):
        d_key, d_value = carry
        start, sums = item
        query_block = lax.dynamic_slice_in_dim(query, start, block, 1)
        gradient_block = lax.dynamic_slice_in_dim(grads_out, start, block, 1)
        logit_scores = block_scores(query_block, key_matrix, seg_row, start, score_scale)
        attention_probabilities = jnp.exp(logit_scores - sums[..., None])
        reduced_probabilities = attention_probabilities.astype(jnp.bfloat16)
        d_value = d_value + jnp.einsum(
            "syer,seyo->sro",
            reduced_probabilities,
            gradient_block,
            preferred_element_type=jnp.float32,
        )
        probability_gradient = jnp.einsum(
            "zjfr,zyr->zfjy", gradient_block, value_matrix, preferred_element_type=jnp.float32
        )
        inner = jnp.sum(attention_probabilities * probability_gradient, axis=-1, keepdims=True)
        score_gradient = (attention_probabilities * (probability_gradient - inner)).astype(
            jnp.bfloat16
        )
        d_query = (
            jnp.einsum(
                "szjr,srn->sjzn", score_gradient, key_matrix, preferred_element_type=jnp.float32
            )
            * score_scale
        )
        d_key = (
            d_key
            + jnp.einsum(
                "syer,seyo->sro", score_gradient, query_block, preferred_element_type=jnp.float32
            )
            * score_scale
        )
        return ((d_key, d_value), d_query)

    starts = jnp.arange(0, length, block, dtype=jnp.int32)
    zeros = jnp.zeros(key_matrix.shape, jnp.float32)
    carry, d_query = lax.scan(one_block, (zeros, zeros), (starts, lse))
    return (d_query, carry[0], carry[1])


def shards(
    tokens,
    segment_ids,
    cotangent,
    attn_gain,
    w_qkv,
    w_out,
    ffn_gain,
    w_gate,
    w_up,
    w_down,
    q_gain,
    k_gain,
):
    groups = lax.axis_size("seq")
    rows_dev, len_dev, width = tokens.shape
    count = rows_dev * len_dev
    per_group = QH // KVG
    places = (KVG + groups - 1) // groups * groups
    place_dev = places // groups
    length = len_dev * groups
    block = min(512, length)
    items = rows_dev * place_dev
    gain_one, qkv_w, out_w, gain_two, gate_w, up_w, down_w = (
        lax.all_gather(attn_gain, ("seq", "rep"), axis=0, tiled=True),
        lax.all_gather(w_qkv, ("seq", "rep"), axis=0, tiled=True),
        lax.all_gather(w_out, ("seq", "rep"), axis=0, tiled=True),
        lax.all_gather(ffn_gain, ("seq", "rep"), axis=0, tiled=True),
        lax.all_gather(w_gate, ("seq", "rep"), axis=0, tiled=True),
        lax.all_gather(w_up, ("seq", "rep"), axis=0, tiled=True),
        lax.all_gather(w_down, ("seq", "rep"), axis=0, tiled=True),
    )
    row_seg = lax.all_gather(segment_ids, "seq", axis=1, tiled=True)
    offset = lax.axis_index("seq") * len_dev
    earlier = jnp.sum((row_seg[:, None, :] < segment_ids[:, :, None]).astype(jnp.int32), axis=2)
    positions = (offset + jnp.arange(len_dev, dtype=jnp.int32)[None, :] - earlier).reshape(count)
    seg_items = jnp.repeat(row_seg, place_dev, axis=0)
    x_rows = tokens.reshape(count, width).astype(jnp.float32)
    gain_a = gain_one.astype(jnp.float32)
    gain_b = gain_two.astype(jnp.float32)
    q_scale = q_gain.astype(jnp.float32)
    k_scale = k_gain.astype(jnp.float32)
    normed = norm_rows(x_rows, gain_a).astype(jnp.bfloat16)
    qkv = jnp.dot(normed, qkv_w, preferred_element_type=jnp.float32)
    query, key, value = heads_prep(qkv, q_scale, k_scale, positions)
    packed = jnp.concatenate(
        [query.reshape(count, KVG, per_group * HD), key, value], axis=2
    ).astype(jnp.bfloat16)
    packed = jnp.pad(packed, ((0, 0), (0, places - KVG), (0, 0))).reshape(
        rows_dev, len_dev, places, -1
    )
    arrived = lax.all_to_all(packed, "seq", split_axis=2, concat_axis=1, tiled=True)
    arrived = arrived.transpose(0, 2, 1, 3).reshape(items, length, -1)
    q_heads = arrived[..., : per_group * HD].reshape(items, length, per_group, HD)
    k_heads = arrived[..., per_group * HD : (per_group + 1) * HD]
    v_heads = arrived[..., (per_group + 1) * HD :]
    outs, lse = attend_forward(q_heads, k_heads, v_heads, seg_items, block)
    attended = (
        outs.transpose(1, 0, 2, 3, 4)
        .reshape(rows_dev, place_dev, length, per_group * HD)
        .transpose(0, 2, 1, 3)
    )
    returned = lax.all_to_all(attended, "seq", split_axis=1, concat_axis=2, tiled=True)
    mixed = returned[:, :, :KVG].reshape(count, QW)
    hidden = x_rows + times_rows(mixed, out_w)
    normed_two = norm_rows(hidden, gain_b).astype(jnp.bfloat16)
    d_result = cotangent.reshape(count, width).astype(jnp.float32)
    gate = jnp.dot(normed_two, gate_w, preferred_element_type=jnp.float32)
    upward = jnp.dot(normed_two, up_w, preferred_element_type=jnp.float32)
    active = (jax.nn.silu(gate) * upward).astype(jnp.bfloat16)
    layer_result = hidden + times_rows(active, down_w)
    d_branch = d_result.astype(jnp.bfloat16)
    d_active = jnp.dot(d_branch, down_w, preferred_element_type=jnp.float32)
    grad_down = token_sum(d_branch, active)
    swiglu_out, swiglu_back = jax.vjp(
        lambda gate_in, up_in: jax.nn.silu(gate_in) * up_in, gate, upward
    )
    d_gate, d_up = swiglu_back(d_active)
    d_gate = d_gate.astype(jnp.bfloat16)
    d_up = d_up.astype(jnp.bfloat16)
    grad_gate = token_sum(normed_two, d_gate)
    grad_up = token_sum(normed_two, d_up)
    d_normed_two = times_rows(d_gate, gate_w) + times_rows(d_up, up_w)
    activations = layer_result.astype(jnp.bfloat16).reshape(rows_dev, len_dev, width)
    second_out, second_back = jax.vjp(norm_rows, hidden, gain_b)
    d_hidden, grad_gain_b = second_back(d_normed_two)
    d_hidden = d_hidden + d_result
    d_attn = d_hidden.astype(jnp.bfloat16)
    grad_out = token_sum(d_attn, mixed)
    d_mixed = jnp.dot(d_attn, out_w, preferred_element_type=jnp.float32).astype(jnp.bfloat16)
    d_pack = jnp.pad(
        d_mixed.reshape(count, KVG, per_group * HD), ((0, 0), (0, places - KVG), (0, 0))
    )
    d_pack = d_pack.reshape(rows_dev, len_dev, places, -1)
    d_arrived = lax.all_to_all(d_pack, "seq", split_axis=2, concat_axis=1, tiled=True)
    d_items = d_arrived.transpose(0, 2, 1, 3).reshape(items, length, per_group, HD)
    d_query, d_key, d_value = attend_backward(
        q_heads, k_heads, v_heads, seg_items, d_items, lse, block
    )
    d_query = d_query.transpose(1, 0, 2, 3, 4).reshape(items, length, per_group * HD)
    d_heads = jnp.concatenate([d_query, d_key, d_value], axis=2).astype(jnp.bfloat16)
    d_heads = d_heads.reshape(rows_dev, place_dev, length, -1).transpose(0, 2, 1, 3)
    d_back = lax.all_to_all(d_heads, "seq", split_axis=1, concat_axis=2, tiled=True)
    d_back = d_back[:, :, :KVG].reshape(count, KVG, -1).astype(jnp.float32)
    d_q_rows = d_back[..., : per_group * HD].reshape(count, QH, HD)
    d_k_rows = d_back[..., per_group * HD : (per_group + 1) * HD]
    d_v_rows = d_back[..., (per_group + 1) * HD :]
    prep_out, prep_back = jax.vjp(
        lambda qkv_in, qs_in, ks_in: heads_prep(qkv_in, qs_in, ks_in, positions),
        qkv,
        q_scale,
        k_scale,
    )
    d_qkv, grad_q_scale, grad_k_scale = prep_back((d_q_rows, d_k_rows, d_v_rows))
    d_qkv = d_qkv.astype(jnp.bfloat16)
    grad_qkv = token_sum(normed, d_qkv)
    d_normed = times_rows(d_qkv, qkv_w)
    first_out, first_back = jax.vjp(norm_rows, x_rows, gain_a)
    d_tokens, grad_gain_a = first_back(d_normed)
    d_tokens = d_tokens + d_hidden
    head_sums = lax.psum((grad_q_scale, grad_k_scale), ("seq", "rep"))
    parts = (
        lax.psum_scatter(grad_gain_a, ("seq", "rep"), scatter_dimension=0, tiled=True),
        lax.psum_scatter(grad_qkv, ("seq", "rep"), scatter_dimension=0, tiled=True),
        lax.psum_scatter(grad_out, ("seq", "rep"), scatter_dimension=0, tiled=True),
        lax.psum_scatter(grad_gain_b, ("seq", "rep"), scatter_dimension=0, tiled=True),
        lax.psum_scatter(grad_gate, ("seq", "rep"), scatter_dimension=0, tiled=True),
        lax.psum_scatter(grad_up, ("seq", "rep"), scatter_dimension=0, tiled=True),
        lax.psum_scatter(grad_down, ("seq", "rep"), scatter_dimension=0, tiled=True),
    )
    return (
        activations,
        d_tokens.reshape(rows_dev, len_dev, width),
        parts[0],
        parts[1],
        parts[2],
        parts[3],
        parts[4],
        parts[5],
        parts[6],
        head_sums[0],
        head_sums[1],
    )


MESH = pl.DeviceIdType.MESH
BF = jnp.bfloat16
F32 = jnp.float32
NEG = -1e30
VMEM_BYTES = 63 * 2**20
QS = 5
DZ = 4
BLK = 128
LEN4 = 512
FFS = 896
BR = 64
HALF = 512
AW = 1024
QKV_W = 640
SCALE = HD ** (-0.5)
CHUNKS = ((0, 384), (384, 512))
QKV_M, OUT_M, F0_M, F1_M = range(4)


def place():
    s = lax.axis_index("seq")
    r = lax.axis_index("rep")
    return lax.div(s, 2), lax.rem(s, 2), lax.div(r, 2), lax.rem(r, 2)


def dev(x, c, z, y):
    return {"seq": 2 * x + c, "rep": 2 * z + y}


def flip(v, by):
    return v if by == 0 else 1 - v


def near(z):
    return z + 1 - 2 * lax.rem(z, 2)


def inner(z):
    return (z == 1) | (z == 2)


def send(src, dst, send_sem, recv_sem, target):
    pltpu.make_async_remote_copy(
        src_ref=src,
        dst_ref=dst,
        send_sem=send_sem,
        recv_sem=recv_sem,
        device_id=target,
        device_id_type=MESH,
    ).start()


def arrived(ref, sem):
    pltpu.make_async_copy(ref, ref, sem).wait()


def many(first, count):
    return pl.ds(pl.multiple_of(first, count), count)


def rows_of(ref, index, size):
    return ref.at[many(index * size, size)]


def greet(x, c, z, y):
    found = []
    for dz in range(DZ):
        for dx in range(2):
            for dy in range(2):
                for dc in range(2):
                    if (dx or dy or dc) if dz == 0 else dc == 0:
                        found.append(
                            dev(flip(x, dx), flip(c, dc), lax.rem(z + dz, DZ), flip(y, dy))
                        )
    barrier = pltpu.get_barrier_semaphore()
    for target in found:
        pl.semaphore_signal(barrier, inc=1, device_id=target, device_id_type=MESH)
    return lambda: pl.semaphore_wait(barrier, len(found))


def spread_start(src, spot, ss, rs):
    x, c, z, y = place()
    slot = 2 * x + c
    for k, (dx, dy) in enumerate(((1, 1), (1, 0), (0, 1))):
        send(src, spot, ss.at[k], rs.at[slot], dev(flip(x, dx), y, z, flip(y, dy)))

    @pl.when(c == y)
    def _():
        pltpu.make_async_copy(src, spot, rs.at[slot]).start()

    @pl.when(c != y)
    def _():
        send(src, spot, ss.at[3], rs.at[slot], dev(x, y, z, y))


def spread_wait(block, rs):
    for j in range(4):
        arrived(block, rs.at[j])


def spread_sent(src, ss):
    x, c, z, y = place()
    for k in range(3):
        arrived(src, ss.at[k])

    @pl.when(c != y)
    def _():
        arrived(src, ss.at[3])


BLOCK_ORDER = ((1, 1), (1, 0), (0, 1), (0, 0))


def block_at(order):
    x, c, z, y = place()
    dx, dc = BLOCK_ORDER[order]
    return 2 * flip(x, dx) + flip(c, dc)


def collect_start(order, partial, inbox, ss, rs):
    x, c, z, y = place()
    dx, dc = BLOCK_ORDER[order]
    src = rows_of(partial, block_at(order), BLK)
    slot = 2 * x + y
    spot = inbox.at[slot]
    target = dev(flip(x, dx), flip(c, dc), z, c)
    if dx or dc:
        send(src, spot, ss.at[order], rs.at[slot], target)
        return

    @pl.when(c == y)
    def _():
        pltpu.make_async_copy(src, spot, rs.at[slot]).start()

    @pl.when(c != y)
    def _():
        send(src, spot, ss.at[order], rs.at[slot], target)


def collect_wait(inbox, rs):
    for j in range(4):
        arrived(inbox.at[j], rs.at[j])


def collect_sent(inbox, ss):
    x, c, z, y = place()
    for k in range(3):
        arrived(inbox.at[0], ss.at[k])

    @pl.when(c != y)
    def _():
        arrived(inbox.at[0], ss.at[3])


def inbox_sum(inbox):
    return (inbox[0].astype(F32) + inbox[1].astype(F32)) + (
        inbox[2].astype(F32) + inbox[3].astype(F32)
    )


def mm(left, right):
    return lax.dot_general(left, right, (((1,), (0,)), ((), ())), preferred_element_type=F32)


def mm_nt(left, right):
    return lax.dot_general(left, right, (((1,), (1,)), ((), ())), preferred_element_type=F32)


def mm_tn(left, right):
    return lax.dot_general(left, right, (((0,), (0,)), ((), ())), preferred_element_type=F32)


def group_of(local_head):
    x, c, z, y = place()
    return jnp.where(local_head + 2 * x + y >= 4, 1, 0)


def layer_body(
    tok, cot, small, wq, wo, wg, wu, wd,
    act_o, dtok_o, ga_o, gqkv_o, go_o, gf_o, gate_o, up_o, down_o, gq_o, gk_o,
    wap, smallf, xf, n1, wav, w3, dyf, n2f, part, inbox, stage, active, dgu,
    qkvt, dqkvt, dqkv, qt, kt, kk, vt, vv, lse, att, cs, grow, hid, blk, dot_s, dkt, dvt,
    help_f, come_f, end_f, help_a, come_a, end_a, arecv, vec, vecr, vr, gp2,
    sp_ss, sp_rs, co_ss, co_rs, w_ss, w_rs, l_ss, l_rs, c_ss, c_rs, g_ss, g_rs, h_ss, h_rs, o_ss, o_rs, p_ss, p_rs, v_ss, v_rs, loc,
    ready,
):
    x, c, z, y = place()
    shard = 2 * x + y
    me = (2 * x + c) * 2 * DZ + 2 * z + y
    mid = inner(z)
    sibling = dev(x, 1 - c, z, y)
    pair, across = near(z), DZ - 1 - z
    far = DZ - 1 - pair
    SMALL, TOK, COT, N2, DAB = range(5)
    OUT, DN, YY, DT = range(4)

    def own_pieces(m, to_shard):
        if m == QKV_M:
            return [wap.at[to_shard, :, pl.ds(0, QKV_W)]]
        if m == OUT_M:
            return [wap.at[to_shard, :, pl.ds(QKV_W, AW - QKV_W)]]
        lo, wide = CHUNKS[m - F0_M]
        lanes = pl.ds(pl.multiple_of(to_shard * FFS + lo, 128), wide)
        return [ref.at[:, lanes] for ref in (wg, wu, wd)]

    def spots(m, rows):
        if m < F0_M:
            return [held(m, rows, BR)]
        lo, wide = CHUNKS[m - F0_M]
        return [w3.at[many(rows, BR), pl.ds(3 * lo + j * wide, wide)] for j in range(3)]

    def held(m, first, count):
        rows = many(first, count)
        if m == QKV_M:
            return wav.at[rows, pl.ds(0, QKV_W)]
        if m == OUT_M:
            return wav.at[rows, pl.ds(QKV_W, AW - QKV_W)]
        lo, wide = CHUNKS[m - F0_M]
        return w3.at[rows, pl.ds(3 * lo, 3 * wide)]

    def weights_start(m):
        for dx, dy in ((1, 1), (1, 0), (0, 1), (0, 0)):
            tx, ty = flip(x, dx), flip(y, dy)
            for src, spot in zip(own_pieces(m, 2 * tx + ty), spots(m, me * BR)):
                if dx or dy:
                    send(src, spot, w_ss.at[m, 2 * dx + dy - 1], w_rs.at[m, shard], dev(tx, c, z, ty))
                else:
                    pltpu.make_async_copy(src, spot, w_rs.at[m, shard]).start()

    def line(m, from_plane, to_plane, k):
        for tx in range(2):
            slab = held(m, ((2 * tx + c) * DZ + from_plane) * 2 * BR, 2 * BR)
            send(slab, slab, l_ss.at[m, 2 * k + tx], l_rs.at[m, 2 * from_plane + tx], dev(x, c, to_plane, y))

    def line_wait(m, plane):
        for tx in range(2):
            arrived(held(m, 0, 2 * BR), l_rs.at[m, 2 * plane + tx])

    def weights_line(m):
        for k in range(4):
            arrived(held(m, 0, BR), w_rs.at[m, k])
        line(m, z, pair, 0)

        @pl.when(mid)
        def _():
            line(m, z, across, 1)

    def weights_pass_near(m):
        @pl.when(mid)
        def _():
            line_wait(m, pair)
            line(m, pair, across, 2)
            line_wait(m, across)
            line(m, across, pair, 3)

    def weights_pass_far(m):
        @pl.when(mid)
        def _():
            line_wait(m, far)
            line(m, far, pair, 4)

    def weights_swap(m):
        @pl.when(jnp.logical_not(mid))
        def _():
            for plane in (pair, far, across):
                line_wait(m, plane)

        for tx in range(2):
            half = held(m, (2 * tx + c) * HALF, HALF)
            send(half, half, c_ss.at[m, tx], c_rs.at[m, tx], sibling)

    def weights_wait(m):
        for tx in range(2):
            arrived(held(m, 0, HALF), c_rs.at[m, tx])

    def weights_sent(m):
        for k in range(3):
            arrived(held(m, 0, BR), w_ss.at[m, k])
        for k in range(2):
            arrived(held(m, 0, 2 * BR), l_ss.at[m, k])

        @pl.when(mid)
        def _():
            for k in range(2, 10):
                arrived(held(m, 0, 2 * BR), l_ss.at[m, k])

        for tx in range(2):
            arrived(held(m, 0, HALF), c_ss.at[m, tx])

    class Grad:
        pass

    def grad(kind, ref, first_row, lo, width, helped, come, final):
        g = Grad()
        lanes = pl.ds(lo, width)
        g.slab = lambda tx, plane: ref.at[many(first_row + (tx * DZ + plane) * 2 * BR, 2 * BR), lanes]
        g.helped, g.come, g.final, g.kind = helped, come, final, kind
        return g

    def start(g):
        k = g.kind

        @pl.when(jnp.logical_not(mid))
        def _():
            for i, plane in enumerate((far, across)):
                for tx in range(2):
                    send(
                        g.slab(tx, plane), g.helped(i, tx), h_ss.at[k, 2 * i + tx], h_rs.at[k, 2 * i + tx],
                        dev(x, c, pair, y),
                    )

        for tx in range(2):
            send(g.slab(tx, pair), g.come(0, tx), o_ss.at[k, tx], o_rs.at[k, tx], dev(x, c, pair, y))

    def join(g, i):
        k = g.kind
        plane = (across, far)[i]

        @pl.when(mid)
        def _():
            for _ in range(1):
                for tx in range(2):
                    rows, more = g.slab(tx, plane), g.helped(i, tx)
                    arrived(more, h_rs.at[k, 2 * i + tx])
                    rows[...] = (rows[...].astype(F32) + more[...].astype(F32)).astype(BF)
                    send(
                        rows, g.come(1, tx), o_ss.at[k, 2 + 2 * i + tx], o_rs.at[k, 2 + tx], dev(x, c, plane, y)
                    )

    def finish(g):
        k = g.kind
        for tx in range(2):
            rows = g.slab(tx, z)
            for i in range(2):
                arrived(rows, o_rs.at[k, 2 * i + tx])
            rows[...] = (
                rows[...].astype(F32) + g.come(0, tx)[...].astype(F32) + g.come(1, tx)[...].astype(F32)
            ).astype(BF)
        for dx, dy in ((1, 1), (1, 0), (0, 1), (0, 0)):
            tx, ty = flip(x, dx), flip(y, dy)
            src = g.slab(tx, z).at[many(ty * BR, BR)]
            if dx or dy:
                send(src, g.final(shard), p_ss.at[k, 2 * dx + dy - 1], p_rs.at[k, shard], dev(tx, c, z, ty))
            else:
                pltpu.make_async_copy(src, g.final(shard), p_rs.at[k, shard]).start()

    def final_wait(g):
        for t in range(4):
            arrived(g.final(0), p_rs.at[g.kind, t])

    def grad_sent(g):
        k = g.kind
        for i in range(3):
            arrived(g.final(0), p_ss.at[k, i])
        for i in range(2):
            arrived(g.slab(0, 0), o_ss.at[k, i])

        @pl.when(mid)
        def _():
            for i in range(2, 6):
                arrived(g.slab(0, 0), o_ss.at[k, i])

        @pl.when(jnp.logical_not(mid))
        def _():
            for i in range(4):
                arrived(g.slab(0, 0), h_ss.at[k, i])

    def ffn_grad(j):
        lo, wide = CHUNKS[j]
        lanes = pl.ds(3 * lo, 3 * wide)
        return grad(
            j, w3, 1024, 3 * lo, 3 * wide,
            lambda i, tx: help_f.at[i, pl.ds(tx * 2 * BR, 2 * BR), lanes],
            lambda i, tx: come_f.at[i, pl.ds(tx * 2 * BR, 2 * BR), lanes],
            lambda t: end_f.at[t, :, lanes],
        )

    def att_grad(kind):
        lanes = pl.ds(ATT_LO[kind], ATT_WIDE[kind])
        return grad(
            kind, arecv, 0, ATT_LO[kind], ATT_WIDE[kind],
            lambda i, tx: help_a.at[i, pl.ds(tx * 2 * BR, 2 * BR), lanes],
            lambda i, tx: come_a.at[i, pl.ds(tx * 2 * BR, 2 * BR), lanes],
            lambda t: end_a.at[t, :, lanes],
        )

    F0, F1, GO, GQ = ffn_grad(0), ffn_grad(1), att_grad(2), att_grad(3)

    everyone_here = greet(x, c, z, y)
    turned = jnp.transpose(small[...])
    lane = lax.broadcasted_iota(jnp.int32, (BR, 64), 1)
    gains = jnp.where(lane == 0, turned[0:64, 0:1], jnp.where(lane == 1, turned[0:64, 1:2], 0.0))
    gq, gk, fr = turned[0:64, 2:3], turned[0:64, 3:4], turned[0:32, 5:6]
    for t in range(4):
        wap[t, :, 0:320] = wq[:, 320 * t : 320 * t + 320]
        wap[t, :, 320:448] = wq[:, QW + 64 * t : QW + 64 * t + 128]
        wap[t, :, 448:576] = wq[:, QW + KW + 64 * t : QW + KW + 64 * t + 128]
        wap[t, :, 576:640] = gains.astype(BF)
        wap[t, :, 640:960] = wo[:, 320 * t : 320 * t + 320]
        wap[t, :, 960:1024] = jnp.zeros((BR, 64), BF)
    everyone_here()
    weights_start(QKV_M)
    spot = smallf.at[:, many((2 * x + c) * BLK, BLK)]
    spread_start(small, spot, sp_ss.at[SMALL], sp_rs.at[SMALL])
    weights_start(OUT_M)
    spread_start(tok, rows_of(xf, 2 * x + c, BLK), sp_ss.at[TOK], sp_rs.at[TOK])
    weights_start(F0_M)
    weights_start(F1_M)
    weights_line(QKV_M)
    weights_line(OUT_M)
    spread_wait(spot, sp_rs.at[SMALL])
    seg_row = smallf[4:5, :]
    seg_col = jnp.transpose(smallf[...])[:, 4:5]
    key_at = lax.broadcasted_iota(jnp.int32, (LEN4, LEN4), 0)
    query_at = lax.broadcasted_iota(jnp.int32, (LEN4, LEN4), 1)
    allowed = (key_at <= query_at) & (seg_col == seg_row)
    earlier = jnp.sum(jnp.where(seg_col < seg_row, 1.0, 0.0), axis=0, keepdims=True)
    index = lax.broadcasted_iota(jnp.int32, (1, LEN4), 1).astype(F32)
    angles = fr * (index - earlier)
    cs[0:32, :] = jnp.cos(angles)
    cs[32:64, :] = jnp.sin(angles)
    weights_pass_near(QKV_M)
    weights_pass_near(OUT_M)
    weights_pass_far(QKV_M)
    weights_pass_far(OUT_M)
    weights_line(F0_M)
    weights_line(F1_M)
    weights_swap(QKV_M)
    spread_wait(rows_of(xf, 0, BLK), sp_rs.at[TOK])
    spread_start(cot, rows_of(dyf, 2 * x + c, BLK), sp_ss.at[COT], sp_rs.at[COT])
    weights_wait(QKV_M)
    grow[...] = jnp.transpose(wav[:, 512:640].astype(F32))[64:72, :]

    @pl.loop(0, 4)
    def _(j):
        rows = many(j * BLK, BLK)
        v = xf[rows, :].astype(F32)
        n1[rows, :] = (
            v * lax.rsqrt(jnp.mean(v * v, axis=1, keepdims=True) + norm_eps) * grow[0:1, :]
        ).astype(BF)

    @pl.loop(0, 5)
    def _(j):
        wide = many(j * 128, 128)
        qkvt[wide, :] = jnp.transpose(mm(n1[...], wav[:, wide]))

    def rotated(v, gain):
        cos, sin = cs[0:32, :], cs[32:64, :]
        v = v * lax.rsqrt(jnp.mean(v * v, axis=0, keepdims=True) + norm_eps) * gain
        first, second = v[0:32, :], v[32:64, :]
        return first * cos - second * sin, second * cos + first * sin

    for h in range(QS):
        first, second = rotated(qkvt[h * 64 : h * 64 + 64, :], gq)
        qt[h, 0:32, :] = first.astype(BF)
        qt[h, 32:64, :] = second.astype(BF)
    for g in range(2):
        base = QS * 64 + g * 64
        first, second = rotated(qkvt[base : base + 64, :], gk)
        both = jnp.concatenate([first, second], axis=0)
        kt[g] = both.astype(BF)
        kk[g] = jnp.transpose(both).astype(BF)
        value = qkvt[base + 128 : base + 192, :]
        vt[g] = value.astype(BF)
        vv[g] = jnp.transpose(value).astype(BF)
    weights_swap(OUT_M)
    dqkvt[QS * 64 : 384, :] = jnp.zeros((384 - QS * 64, LEN4), F32)
    for h in range(QS):
        g = group_of(h)
        scores = jnp.where(allowed, mm(kk[g], qt[h]) * SCALE, NEG)
        top = jnp.max(scores, axis=0, keepdims=True)
        weights = jnp.exp(scores - top)
        total = jnp.sum(weights, axis=0, keepdims=True)
        lse[h : h + 1, :] = top + jnp.log(total)
        dqkvt[h * 64 : h * 64 + 64, :] = mm(vt[g], (weights / total).astype(BF))
    att[...] = jnp.transpose(dqkvt[0:384, :]).astype(BF)
    weights_pass_near(F0_M)
    weights_wait(OUT_M)
    for order in range(4):
        rows = many(block_at(order) * BLK, BLK)
        part[0, rows, :] = mm_nt(att[rows, :], wav[:, QKV_W:AW]).astype(BF)
        collect_start(order, part.at[0], inbox.at[0], co_ss.at[OUT], co_rs.at[OUT])
    weights_pass_near(F1_M)
    weights_pass_far(F0_M)
    collect_wait(inbox.at[0], co_rs.at[OUT])
    hidden = tok[...].astype(F32) + inbox_sum(inbox.at[0])
    hid[...] = hidden
    blk[0] = (
        hidden
        * lax.rsqrt(jnp.mean(hidden * hidden, axis=1, keepdims=True) + norm_eps)
        * grow[1:2, :]
    ).astype(BF)
    spread_start(blk.at[0], rows_of(n2f, 2 * x + c, BLK), sp_ss.at[N2], sp_rs.at[N2])
    weights_pass_far(F1_M)
    weights_swap(F0_M)
    spread_wait(rows_of(dyf, 0, BLK), sp_rs.at[COT])
    spread_wait(rows_of(n2f, 0, BLK), sp_rs.at[N2])
    weights_wait(F0_M)

    def hidden_units(j):
        first, width = CHUNKS[j]
        base = 3 * first
        for lo in range(0, width, 256):
            wide = min(256, width - lo)
            gate = mm(n2f[...], w3[:, base + lo : base + lo + wide])
            upward = mm(n2f[...], w3[:, base + width + lo : base + width + lo + wide])
            grad_in = mm(dyf[...], w3[:, base + 2 * width + lo : base + 2 * width + lo + wide])
            sig = 1.0 / (1.0 + jnp.exp(-gate))
            silu = gate * sig
            active[:, first + lo : first + lo + wide] = (silu * upward).astype(BF)
            at = 2 * first + lo
            dgu[:, at : at + wide] = (grad_in * upward * (sig * (1.0 + gate * (1.0 - sig)))).astype(BF)
            at = at + width
            dgu[:, at : at + wide] = (grad_in * silu).astype(BF)

    def dn_part(j, rows, wide):
        first, width = CHUNKS[j]
        return mm_nt(dgu[rows, 2 * first : 2 * first + 2 * width], w3[wide, 3 * first : 3 * first + 2 * width])

    def y_part(j, rows, wide):
        first, width = CHUNKS[j]
        at = 3 * first + 2 * width
        return mm_nt(active[rows, first : first + width], w3[wide, at : at + width])

    def ffn_grads(j, core, row):
        first, width = CHUNKS[j]
        wide = many((2 * lax.div(row, 2) + core) * HALF + lax.rem(row, 2) * 256, 256)
        return (
            mm_tn(n2f[:, wide], dgu[:, 2 * first : 2 * first + 2 * width]),
            mm_tn(dyf[:, wide], active[:, first : first + width]),
        )

    def chunk_lanes(j):
        first, width = CHUNKS[j]
        return pl.ds(3 * first, 2 * width), pl.ds(3 * first + 2 * width, width), pl.ds(3 * first, 3 * width)

    def grads_swap(j):
        two, one, both = chunk_lanes(j)
        weights_sent(F0_M + j)
        pl.semaphore_signal(ready.at[j], inc=1, device_id=sibling, device_id_type=MESH)

        @pl.loop(0, 4)
        def _(row):
            rows = many(row * 256, 256)
            gu, down = ffn_grads(j, 1 - c, row)
            w3[rows, two] = gu.astype(BF)
            w3[rows, one] = down.astype(BF)

        pl.semaphore_wait(ready.at[j], 1)
        send(
            w3.at[pl.ds(0, 1024), both], w3.at[pl.ds(1024, 1024), both], g_ss.at[j], g_rs.at[j], sibling
        )

    def grads_own(j):
        two, one, both = chunk_lanes(j)
        arrived(w3.at[pl.ds(1024, 1024), both], g_rs.at[j])

        @pl.loop(0, 4)
        def _(row):
            rows = many(1024 + row * 256, 256)
            gu, down = ffn_grads(j, c, row)
            w3[rows, two] = (gu + w3[rows, two].astype(F32)).astype(BF)
            w3[rows, one] = (down + w3[rows, one].astype(F32)).astype(BF)

    every = slice(0, LEN4)
    hidden_units(0)
    collect_sent(inbox.at[0], co_ss.at[OUT])

    @pl.loop(0, 8)
    def _(j):
        wide = many(j * 256, 256)
        part[1, :, wide] = dn_part(0, every, wide).astype(BF)
        part[0, :, wide] = y_part(0, every, wide).astype(BF)

    grads_swap(0)
    grads_own(0)
    start(F0)
    weights_swap(F1_M)
    weights_wait(F1_M)
    hidden_units(1)
    for order in range(4):
        rows = many(block_at(order) * BLK, BLK)

        @pl.loop(0, 4)
        def _(j):
            wide = many(j * 512, 512)
            part[1, rows, wide] = (part[1, rows, wide].astype(F32) + dn_part(1, rows, wide)).astype(BF)

        collect_start(order, part.at[1], inbox.at[1], co_ss.at[DN], co_rs.at[DN])

    @pl.loop(0, 8)
    def _(j):
        wide = many(j * 256, 256)
        part[0, :, wide] = (part[0, :, wide].astype(F32) + y_part(1, every, wide)).astype(BF)

    grads_swap(1)
    join(F0, 0)
    grads_own(1)
    start(F1)
    join(F0, 1)
    collect_wait(inbox.at[1], co_rs.at[DN])
    dn = inbox_sum(inbox.at[1])
    h = hid[...]
    r = lax.rsqrt(jnp.mean(h * h, axis=1, keepdims=True) + norm_eps)
    gp2[...] = jnp.broadcast_to(jnp.sum(dn * h * r, axis=0, keepdims=True), gp2.shape)
    a = dn * grow[1:2, :]
    dh = cot[...].astype(F32) + r * (a - h * (r * r * jnp.mean(a * h, axis=1, keepdims=True)))
    dtok_o[...] = dh
    blk[1] = dh.astype(BF)
    spread_start(blk.at[1], rows_of(xf, 2 * x + c, BLK), sp_ss.at[DAB], sp_rs.at[DAB])
    for order in range(4):
        collect_start(order, part.at[0], inbox.at[0], co_ss.at[YY], co_rs.at[YY])
    finish(F0)
    join(F1, 0)
    def att_grads(core, row, kind):
        wide = many((2 * lax.div(row, 2) + core) * HALF + lax.rem(row, 2) * 256, 256)
        if kind == 3:
            return mm_tn(n1[:, wide], dqkv[...])
        return mm_tn(xf[:, wide], att[...])

    att_lanes = {k: pl.ds(ATT_LO[k], ATT_WIDE[k]) for k in (2, 3)}

    def att_grads_swap(kind):
        @pl.loop(0, 4)
        def _(row):
            side = lax.div(row, 2) * AW + ATT_LO[kind]
            dyf[many(lax.rem(row, 2) * 256, 256), pl.ds(pl.multiple_of(side, 128), ATT_WIDE[kind])] = (
                att_grads(1 - c, row, kind).astype(BF)
            )

        for side in range(2):
            send(
                dyf.at[:, pl.ds(side * AW + ATT_LO[kind], ATT_WIDE[kind])],
                arecv.at[pl.ds(side * HALF, HALF), att_lanes[kind]],
                g_ss.at[2 * kind - 2 + side],
                g_rs.at[2 * kind - 2 + side],
                sibling,
            )

    def att_grads_own(kind):
        for side in range(2):
            arrived(arecv.at[pl.ds(0, HALF), att_lanes[kind]], g_rs.at[2 * kind - 2 + side])

        @pl.loop(0, 4)
        def _(row):
            rows = many(row * 256, 256)
            arecv[rows, att_lanes[kind]] = (
                att_grads(c, row, kind) + arecv[rows, att_lanes[kind]].astype(F32)
            ).astype(BF)

    spread_wait(rows_of(xf, 0, BLK), sp_rs.at[DAB])
    att_grads_swap(2)
    dot_s[...] = jnp.transpose(mm(xf[...], wav[:, QKV_W:AW]).astype(BF).astype(F32)).astype(BF)
    att_grads_own(2)
    start(GO)
    dkt[...] = jnp.zeros_like(dkt)
    dvt[...] = jnp.zeros_like(dvt)

    def unrotated(first, second, raw, gain):
        cos, sin = cs[0:32, :], cs[32:64, :]
        d_first = first * cos + second * sin
        d_second = second * cos - first * sin
        d = jnp.concatenate([d_first, d_second], axis=0)
        r = lax.rsqrt(jnp.mean(raw * raw, axis=0, keepdims=True) + norm_eps)
        d_gain = jnp.sum(d * raw * r, axis=1, keepdims=True)
        a = d * gain
        return r * (a - raw * (r * r * jnp.mean(a * raw, axis=0, keepdims=True))), d_gain

    dq_gain = jnp.zeros((64, 1), F32)
    for h in range(QS):
        g = group_of(h)
        scores = mm(kk[g], qt[h]) * SCALE
        p = jnp.where(allowed, jnp.exp(scores - lse[h : h + 1, :]), 0.0)
        d_out = dot_s[h * 64 : h * 64 + 64, :]
        dvt[g] += mm_nt(d_out, p.astype(BF))
        dp = mm(vv[g], d_out)
        ds = (p * (dp - jnp.sum(p * dp, axis=0, keepdims=True))).astype(BF)
        dkt[g] += mm_nt(qt[h], ds) * SCALE
        dq = (mm(kt[g], ds) * SCALE).astype(BF).astype(F32)
        d, more = unrotated(dq[0:32, :], dq[32:64, :], qkvt[h * 64 : h * 64 + 64, :], gq)
        dq_gain = dq_gain + more
        dqkvt[h * 64 : h * 64 + 64, :] = d
        for g_at, i in JOIN_AFTER.get(h, ()):
            join((F0, F1, GO, GQ)[g_at], i)
    dk_gain = jnp.zeros((64, 1), F32)
    for g in range(2):
        base = QS * 64 + g * 64
        dk = dkt[g].astype(BF).astype(F32)
        d, more = unrotated(dk[0:32, :], dk[32:64, :], qkvt[base : base + 64, :], gk)
        dk_gain = dk_gain + more
        dqkvt[base : base + 64, :] = d
        dqkvt[base + 128 : base + 192, :] = dvt[g]
    dqkvt[576:640, :] = jnp.zeros((64, LEN4), F32)
    dqkv[...] = jnp.transpose(dqkvt[...]).astype(BF)
    collect_sent(inbox.at[1], co_ss.at[DN])
    for order in range(4):
        rows = many(block_at(order) * BLK, BLK)
        part[1, rows, :] = mm_nt(dqkv[rows, :], wav[:, 0:QKV_W]).astype(BF)
        collect_start(order, part.at[1], inbox.at[1], co_ss.at[DT], co_rs.at[DT])

    att_grads_swap(3)
    att_grads_own(3)
    start(GQ)
    join(GO, 0)
    join(GO, 1)
    finish(F1)
    collect_wait(inbox.at[0], co_rs.at[YY])
    act_o[...] = (hid[...] + inbox_sum(inbox.at[0])).astype(BF)
    collect_wait(inbox.at[1], co_rs.at[DT])
    dn = inbox_sum(inbox.at[1])
    xv = tok[...].astype(F32)
    r = lax.rsqrt(jnp.mean(xv * xv, axis=1, keepdims=True) + norm_eps)
    gain_a = jnp.sum(dn * xv * r, axis=0, keepdims=True)
    b = dn * grow[0:1, :]
    dtok_o[...] += r * (b - xv * (r * r * jnp.mean(b * xv, axis=1, keepdims=True)))
    qk = jnp.transpose(
        jnp.concatenate(
            [jnp.broadcast_to(dq_gain, (64, 128)), jnp.broadcast_to(dk_gain, (64, 128))], axis=0
        )
    )
    gain_b = gp2[0:1, :]
    vec[...] = jnp.zeros_like(vec)
    for i in range(4 * DZ):
        for half in range(2):
            at = (((i // (2 * DZ)) * 2 + half) * 2 * DZ + i % (2 * DZ)) * BR
            vec[half, i, 0:4, 0:64] = jnp.concatenate(
                [gain_a[:, at : at + BR], gain_b[:, at : at + BR], qk[0:1, 0:64], qk[0:1, 64:128]], axis=0
            )
    send(vec.at[1 - c], vecr, g_ss.at[6], g_rs.at[6], sibling)
    arrived(vecr, g_rs.at[6])
    vecr[...] += vec[c]
    source = shard * DZ + z
    for dz in range(DZ):
        for dx in range(2):
            for dy in range(2):
                tx, ty, tz = flip(x, dx), flip(y, dy), lax.rem(z + dz, DZ)
                src = vecr.at[(tx * DZ + tz) * 2 + ty]
                k = (dz * 2 + dx) * 2 + dy
                if k == 0:
                    pltpu.make_async_copy(src, vr.at[source], v_rs.at[source]).start()
                else:
                    send(src, vr.at[source], v_ss.at[k], v_rs.at[source], dev(tx, c, tz, ty))
    join(GQ, 0)
    join(GQ, 1)
    finish(GO)
    leave = []
    for g in (F0, F1):
        final_wait(g)
    for j, out in enumerate((gate_o, up_o, down_o)):
        for t in range(4):
            rows = pl.ds(t * BR, BR)
            if j > 0:
                leave[4 * (j - 1) + t].wait()
            for first, width in CHUNKS:
                at = 3 * first + j * width
                stage[rows, first : first + width] = end_f[t, :, at : at + width].astype(F32)
            leave.append(
                pltpu.make_async_copy(
                    stage.at[rows], out.at[:, pl.ds(t * FFS, FFS)], loc.at[4 * j + t]
                )
            )
            leave[-1].start()
    finish(GQ)
    for i in range(4 * DZ):
        arrived(vr.at[0], v_rs.at[i])
    sums = jnp.sum(vr[...], axis=0)
    for i, out in enumerate((ga_o, gf_o, gq_o, gk_o)):
        out[...] = sums[i : i + 1, 0:64]
    final_wait(GO)
    for t in range(4):
        go_o[:, 320 * t : 320 * t + 320] = end_a[t, :, 640:960].astype(F32)
    final_wait(GQ)
    for t in range(4):
        gqkv_o[:, 320 * t : 320 * t + 320] = end_a[t, :, 0:320].astype(F32)
    for lo, to in ((320, QW), (448, QW + KW)):
        for g in range(5):
            parts = []
            if g < 4:
                parts.append(end_a[g, :, lo : lo + 64].astype(F32))
            if g > 0:
                parts.append(end_a[g - 1, :, lo + 64 : lo + 128].astype(F32))
            gqkv_o[:, to + 64 * g : to + 64 * g + 64] = sum(parts[1:], parts[0])
    for copy in leave[8:]:
        copy.wait()
    for g in (F0, F1, GO, GQ):
        grad_sent(g)
    weights_sent(QKV_M)
    weights_sent(OUT_M)
    for i in range(1, 4 * DZ):
        arrived(vr.at[0], v_ss.at[i])
    for j in range(2):
        arrived(w3.at[pl.ds(0, 1024), chunk_lanes(j)[2]], g_ss.at[j])
    for j in (2, 3):
        for side in range(2):
            arrived(arecv.at[pl.ds(0, HALF), att_lanes[j]], g_ss.at[2 * j - 2 + side])
    arrived(vecr, g_ss.at[6])
    spread_sent(small, sp_ss.at[SMALL])
    spread_sent(tok, sp_ss.at[TOK])
    spread_sent(cot, sp_ss.at[COT])
    spread_sent(blk.at[0], sp_ss.at[N2])
    spread_sent(blk.at[1], sp_ss.at[DAB])
    collect_sent(inbox.at[0], co_ss.at[YY])
    collect_sent(inbox.at[1], co_ss.at[DT])


JOIN_AFTER = {4: ((1, 1),)}
ATT_LO = {2: QKV_W, 3: 0}
ATT_WIDE = {2: AW - QKV_W, 3: QKV_W}


def plane_plan(
    tokens, segment_ids, cotangent, attn_gain, w_qkv, w_out, ffn_gain, w_gate, w_up, w_down, q_gain, k_gain
):
    width = tokens.shape[-1]
    freqs = rope_base ** (-jnp.arange(32, dtype=jnp.float32) * 2.0 / HD)

    def lanes(v):
        v = v.astype(F32).reshape(1, -1)
        return jnp.pad(v, ((0, 0), (0, BLK - v.shape[1])))

    small = jnp.concatenate(
        [lanes(v) for v in (attn_gain, ffn_gain, q_gain, k_gain, segment_ids, freqs)]
        + [jnp.zeros((2, BLK), F32)],
        axis=0,
    )
    dma = pltpu.SemaphoreType.DMA
    vm = pltpu.VMEM
    far, close = pl.BlockSpec(memory_space=pl.ANY), pl.BlockSpec(memory_space=pltpu.VMEM)
    outs = pl.pallas_call(
        layer_body,
        out_shape=[
            jax.ShapeDtypeStruct((BLK, width), BF),
            jax.ShapeDtypeStruct((BLK, width), F32),
            jax.ShapeDtypeStruct((1, BR), F32),
            jax.ShapeDtypeStruct(w_qkv.shape, F32),
            jax.ShapeDtypeStruct(w_out.shape, F32),
            jax.ShapeDtypeStruct((1, BR), F32),
            jax.ShapeDtypeStruct(w_gate.shape, F32),
            jax.ShapeDtypeStruct(w_up.shape, F32),
            jax.ShapeDtypeStruct(w_down.shape, F32),
            jax.ShapeDtypeStruct((1, HD), F32),
            jax.ShapeDtypeStruct((1, HD), F32),
        ],
        in_specs=[close] * 5 + [far] * 3,
        out_specs=[close] * 6 + [far] * 3 + [close] * 2,
        scratch_shapes=[
            vm((4, BR, AW), BF),
            vm((8, LEN4), F32),
            vm((LEN4, width), BF),
            vm((LEN4, width), BF),
            vm((2048, AW), BF),
            vm((2048, 3 * FFS), BF),
            vm((LEN4, width), BF),
            vm((LEN4, width), BF),
            vm((2, LEN4, width), BF),
            vm((2, 4, BLK, width), BF),
            vm((4 * BR, FFS), F32),
            vm((LEN4, FFS), BF),
            vm((LEN4, 2 * FFS), BF),
            vm((QKV_W, LEN4), F32),
            vm((QKV_W, LEN4), F32),
            vm((LEN4, QKV_W), BF),
            vm((QS, 64, LEN4), BF),
            vm((2, 64, LEN4), BF),
            vm((2, LEN4, 64), BF),
            vm((2, 64, LEN4), BF),
            vm((2, LEN4, 64), BF),
            vm((8, LEN4), F32),
            vm((LEN4, 384), BF),
            vm((64, LEN4), F32),
            vm((8, width), F32),
            vm((BLK, width), F32),
            vm((2, BLK, width), BF),
            vm((384, LEN4), BF),
            vm((2, 64, LEN4), F32),
            vm((2, 64, LEN4), F32),
            vm((2, 4 * BR, 3 * FFS), BF),
            vm((2, 4 * BR, 3 * FFS), BF),
            vm((4, BR, 3 * FFS), BF),
            vm((2, 4 * BR, AW), BF),
            vm((2, 4 * BR, AW), BF),
            vm((4, BR, AW), BF),
            vm((1024, AW), BF),
            vm((2, 4 * DZ, 8, BLK), F32),
            vm((4 * DZ, 8, BLK), F32),
            vm((4 * DZ, 8, BLK), F32),
            vm((8, width), F32),
            dma((5, 4)), dma((5, 4)),
            dma((4, 4)), dma((4, 4)),
            dma((5, 3)), dma((5, 4)), dma((5, 10)), dma((5, 8)),
            dma((5, 2)), dma((5, 2)),
            dma((8,)), dma((8,)),
            dma((5, 4)), dma((5, 4)),
            dma((5, 6)), dma((5, 4)), dma((5, 3)), dma((5, 4)),
            dma((16,)), dma((16,)),
            dma((12,)),
            pltpu.SemaphoreType.REGULAR((2,)),
        ],
        compiler_params=pltpu.CompilerParams(
            collective_id=0, has_side_effects=True, vmem_limit_bytes=VMEM_BYTES
        ),
    )(
        tokens.reshape(BLK, width), cotangent.reshape(BLK, width), small, w_qkv, w_out, w_gate, w_up, w_down
    )
    shapes = (
        tokens.shape, tokens.shape, (BR,), w_qkv.shape, w_out.shape, (BR,), w_gate.shape, w_up.shape, w_down.shape,
        (HD,), (HD,),
    )
    return tuple(out.reshape(shape) for out, shape in zip(outs, shapes))


def solution(mesh):
    in_specs = (
        P("rep", "seq", None),
        P("rep", "seq"),
        P("rep", "seq", None),
        P(("seq", "rep")),
        P(("seq", "rep"), None),
        P(("seq", "rep"), None),
        P(("seq", "rep")),
        P(("seq", "rep"), None),
        P(("seq", "rep"), None),
        P(("seq", "rep"), None),
        P(),
        P(),
    )
    out_specs = (
        P("rep", "seq", None),
        P("rep", "seq", None),
        P(("seq", "rep")),
        P(("seq", "rep"), None),
        P(("seq", "rep"), None),
        P(("seq", "rep")),
        P(("seq", "rep"), None),
        P(("seq", "rep"), None),
        P(("seq", "rep"), None),
        P(),
        P(),
    )
    planes = mesh.shape["seq"] == 4 and mesh.shape["rep"] == 8
    body = plane_plan if planes else shards
    return jax.shard_map(body, mesh=mesh, in_specs=in_specs, out_specs=out_specs, check_vma=False)
```

```python
import jax
import jax.numpy as jnp
from jax import lax
from jax.experimental import pallas as pl
from jax.experimental.pallas import tpu as pltpu
from jax.sharding import PartitionSpec as P

QH = 20
KVG = 5
HD = 64
QW = 1280
KW = 320


norm_eps = 1e-06
rope_base = 10000.0


def norm_rows(value_matrix, gain):
    return (
        value_matrix
        * lax.rsqrt(jnp.mean(value_matrix * value_matrix, axis=-1, keepdims=True) + norm_eps)
        * gain
    )


def rotate_heads(value_matrix, positions):
    half = value_matrix.shape[-1] // 2
    freqs = rope_base ** (-jnp.arange(half, dtype=jnp.float32) * 2.0 / value_matrix.shape[-1])
    angles = positions.astype(jnp.float32)[:, None] * freqs[None, :]
    cosine = jnp.cos(angles)[:, None, :]
    sine = jnp.sin(angles)[:, None, :]
    first = value_matrix[..., :half]
    second = value_matrix[..., half:]
    return jnp.concatenate(
        [first * cosine - second * sine, second * cosine + first * sine], axis=-1
    )


def heads_prep(qkv, q_scale, k_scale, positions):
    count = qkv.shape[0]
    query = qkv[:, :QW].reshape(count, QH, HD)
    key = qkv[:, QW : QW + KW].reshape(count, KVG, HD)
    value = qkv[:, QW + KW :].reshape(count, KVG, HD)
    query = rotate_heads(norm_rows(query, q_scale), positions)
    key = rotate_heads(norm_rows(key, k_scale), positions)
    return (query, key, value)


def times_rows(left, right):
    return lax.dot_general(
        left, right, (((1,), (1,)), ((), ())), preferred_element_type=jnp.float32
    )


def token_sum(left, right):
    return lax.dot_general(
        left, right, (((0,), (0,)), ((), ())), preferred_element_type=jnp.float32
    )


def block_scores(query_block, key_matrix, seg_row, start, score_scale):
    width = query_block.shape[1]
    length = key_matrix.shape[1]
    logit_scores = (
        jnp.einsum("zjfr,zyr->zfjy", query_block, key_matrix, preferred_element_type=jnp.float32)
        * score_scale
    )
    rows = start + jnp.arange(width, dtype=jnp.int32)
    cols = jnp.arange(length, dtype=jnp.int32)
    seg_blk = lax.dynamic_slice_in_dim(seg_row, start, width, 1)
    allowed = (cols[None, None, :] <= rows[None, :, None]) & (
        seg_row[:, None, :] == seg_blk[:, :, None]
    )
    return jnp.where(allowed[:, None], logit_scores, -1e30)


def attend_forward(query, key_matrix, value_matrix, seg_row, block):
    length = key_matrix.shape[1]
    score_scale = HD ** (-0.5)

    def one_block(start):
        query_block = lax.dynamic_slice_in_dim(query, start, block, 1)
        logit_scores = block_scores(query_block, key_matrix, seg_row, start, score_scale)
        top = jnp.max(logit_scores, axis=-1, keepdims=True)
        weights = jnp.exp(logit_scores - top)
        total = jnp.sum(weights, axis=-1, keepdims=True)
        attention_probabilities = (weights / total).astype(jnp.bfloat16)
        layer_result = jnp.einsum(
            "szjr,srn->sjzn",
            attention_probabilities,
            value_matrix,
            preferred_element_type=jnp.float32,
        )
        return (layer_result.astype(jnp.bfloat16), (top + jnp.log(total))[..., 0])

    starts = jnp.arange(0, length, block, dtype=jnp.int32)
    return lax.map(one_block, starts)


def attend_backward(query, key_matrix, value_matrix, seg_row, grads_out, lse, block):
    length = key_matrix.shape[1]
    score_scale = HD ** (-0.5)

    def one_block(carry, item):
        d_key, d_value = carry
        start, sums = item
        query_block = lax.dynamic_slice_in_dim(query, start, block, 1)
        gradient_block = lax.dynamic_slice_in_dim(grads_out, start, block, 1)
        logit_scores = block_scores(query_block, key_matrix, seg_row, start, score_scale)
        attention_probabilities = jnp.exp(logit_scores - sums[..., None])
        reduced_probabilities = attention_probabilities.astype(jnp.bfloat16)
        d_value = d_value + jnp.einsum(
            "syer,seyo->sro",
            reduced_probabilities,
            gradient_block,
            preferred_element_type=jnp.float32,
        )
        probability_gradient = jnp.einsum(
            "zjfr,zyr->zfjy", gradient_block, value_matrix, preferred_element_type=jnp.float32
        )
        inner = jnp.sum(attention_probabilities * probability_gradient, axis=-1, keepdims=True)
        score_gradient = (attention_probabilities * (probability_gradient - inner)).astype(
            jnp.bfloat16
        )
        d_query = (
            jnp.einsum(
                "szjr,srn->sjzn", score_gradient, key_matrix, preferred_element_type=jnp.float32
            )
            * score_scale
        )
        d_key = (
            d_key
            + jnp.einsum(
                "syer,seyo->sro", score_gradient, query_block, preferred_element_type=jnp.float32
            )
            * score_scale
        )
        return ((d_key, d_value), d_query)

    starts = jnp.arange(0, length, block, dtype=jnp.int32)
    zeros = jnp.zeros(key_matrix.shape, jnp.float32)
    carry, d_query = lax.scan(one_block, (zeros, zeros), (starts, lse))
    return (d_query, carry[0], carry[1])


def shards(
    tokens,
    segment_ids,
    cotangent,
    attn_gain,
    w_qkv,
    w_out,
    ffn_gain,
    w_gate,
    w_up,
    w_down,
    q_gain,
    k_gain,
):
    groups = lax.axis_size("seq")
    rows_dev, len_dev, width = tokens.shape
    count = rows_dev * len_dev
    per_group = QH // KVG
    places = (KVG + groups - 1) // groups * groups
    place_dev = places // groups
    length = len_dev * groups
    block = min(512, length)
    items = rows_dev * place_dev
    gain_one, qkv_w, out_w, gain_two, gate_w, up_w, down_w = (
        lax.all_gather(attn_gain, ("seq", "rep"), axis=0, tiled=True),
        lax.all_gather(w_qkv, ("seq", "rep"), axis=0, tiled=True),
        lax.all_gather(w_out, ("seq", "rep"), axis=0, tiled=True),
        lax.all_gather(ffn_gain, ("seq", "rep"), axis=0, tiled=True),
        lax.all_gather(w_gate, ("seq", "rep"), axis=0, tiled=True),
        lax.all_gather(w_up, ("seq", "rep"), axis=0, tiled=True),
        lax.all_gather(w_down, ("seq", "rep"), axis=0, tiled=True),
    )
    row_seg = lax.all_gather(segment_ids, "seq", axis=1, tiled=True)
    offset = lax.axis_index("seq") * len_dev
    earlier = jnp.sum((row_seg[:, None, :] < segment_ids[:, :, None]).astype(jnp.int32), axis=2)
    positions = (offset + jnp.arange(len_dev, dtype=jnp.int32)[None, :] - earlier).reshape(count)
    seg_items = jnp.repeat(row_seg, place_dev, axis=0)
    x_rows = tokens.reshape(count, width).astype(jnp.float32)
    gain_a = gain_one.astype(jnp.float32)
    gain_b = gain_two.astype(jnp.float32)
    q_scale = q_gain.astype(jnp.float32)
    k_scale = k_gain.astype(jnp.float32)
    normed = norm_rows(x_rows, gain_a).astype(jnp.bfloat16)
    qkv = jnp.dot(normed, qkv_w, preferred_element_type=jnp.float32)
    query, key, value = heads_prep(qkv, q_scale, k_scale, positions)
    packed = jnp.concatenate(
        [query.reshape(count, KVG, per_group * HD), key, value], axis=2
    ).astype(jnp.bfloat16)
    packed = jnp.pad(packed, ((0, 0), (0, places - KVG), (0, 0))).reshape(
        rows_dev, len_dev, places, -1
    )
    arrived = lax.all_to_all(packed, "seq", split_axis=2, concat_axis=1, tiled=True)
    arrived = arrived.transpose(0, 2, 1, 3).reshape(items, length, -1)
    q_heads = arrived[..., : per_group * HD].reshape(items, length, per_group, HD)
    k_heads = arrived[..., per_group * HD : (per_group + 1) * HD]
    v_heads = arrived[..., (per_group + 1) * HD :]
    outs, lse = attend_forward(q_heads, k_heads, v_heads, seg_items, block)
    attended = (
        outs.transpose(1, 0, 2, 3, 4)
        .reshape(rows_dev, place_dev, length, per_group * HD)
        .transpose(0, 2, 1, 3)
    )
    returned = lax.all_to_all(attended, "seq", split_axis=1, concat_axis=2, tiled=True)
    mixed = returned[:, :, :KVG].reshape(count, QW)
    hidden = x_rows + times_rows(mixed, out_w)
    normed_two = norm_rows(hidden, gain_b).astype(jnp.bfloat16)
    d_result = cotangent.reshape(count, width).astype(jnp.float32)
    gate = jnp.dot(normed_two, gate_w, preferred_element_type=jnp.float32)
    upward = jnp.dot(normed_two, up_w, preferred_element_type=jnp.float32)
    active = (jax.nn.silu(gate) * upward).astype(jnp.bfloat16)
    layer_result = hidden + times_rows(active, down_w)
    d_branch = d_result.astype(jnp.bfloat16)
    d_active = jnp.dot(d_branch, down_w, preferred_element_type=jnp.float32)
    grad_down = token_sum(d_branch, active)
    swiglu_out, swiglu_back = jax.vjp(
        lambda gate_in, up_in: jax.nn.silu(gate_in) * up_in, gate, upward
    )
    d_gate, d_up = swiglu_back(d_active)
    d_gate = d_gate.astype(jnp.bfloat16)
    d_up = d_up.astype(jnp.bfloat16)
    grad_gate = token_sum(normed_two, d_gate)
    grad_up = token_sum(normed_two, d_up)
    d_normed_two = times_rows(d_gate, gate_w) + times_rows(d_up, up_w)
    activations = layer_result.astype(jnp.bfloat16).reshape(rows_dev, len_dev, width)
    second_out, second_back = jax.vjp(norm_rows, hidden, gain_b)
    d_hidden, grad_gain_b = second_back(d_normed_two)
    d_hidden = d_hidden + d_result
    d_attn = d_hidden.astype(jnp.bfloat16)
    grad_out = token_sum(d_attn, mixed)
    d_mixed = jnp.dot(d_attn, out_w, preferred_element_type=jnp.float32).astype(jnp.bfloat16)
    d_pack = jnp.pad(
        d_mixed.reshape(count, KVG, per_group * HD), ((0, 0), (0, places - KVG), (0, 0))
    )
    d_pack = d_pack.reshape(rows_dev, len_dev, places, -1)
    d_arrived = lax.all_to_all(d_pack, "seq", split_axis=2, concat_axis=1, tiled=True)
    d_items = d_arrived.transpose(0, 2, 1, 3).reshape(items, length, per_group, HD)
    d_query, d_key, d_value = attend_backward(
        q_heads, k_heads, v_heads, seg_items, d_items, lse, block
    )
    d_query = d_query.transpose(1, 0, 2, 3, 4).reshape(items, length, per_group * HD)
    d_heads = jnp.concatenate([d_query, d_key, d_value], axis=2).astype(jnp.bfloat16)
    d_heads = d_heads.reshape(rows_dev, place_dev, length, -1).transpose(0, 2, 1, 3)
    d_back = lax.all_to_all(d_heads, "seq", split_axis=1, concat_axis=2, tiled=True)
    d_back = d_back[:, :, :KVG].reshape(count, KVG, -1).astype(jnp.float32)
    d_q_rows = d_back[..., : per_group * HD].reshape(count, QH, HD)
    d_k_rows = d_back[..., per_group * HD : (per_group + 1) * HD]
    d_v_rows = d_back[..., (per_group + 1) * HD :]
    prep_out, prep_back = jax.vjp(
        lambda qkv_in, qs_in, ks_in: heads_prep(qkv_in, qs_in, ks_in, positions),
        qkv,
        q_scale,
        k_scale,
    )
    d_qkv, grad_q_scale, grad_k_scale = prep_back((d_q_rows, d_k_rows, d_v_rows))
    d_qkv = d_qkv.astype(jnp.bfloat16)
    grad_qkv = token_sum(normed, d_qkv)
    d_normed = times_rows(d_qkv, qkv_w)
    first_out, first_back = jax.vjp(norm_rows, x_rows, gain_a)
    d_tokens, grad_gain_a = first_back(d_normed)
    d_tokens = d_tokens + d_hidden
    head_sums = lax.psum((grad_q_scale, grad_k_scale), ("seq", "rep"))
    parts = (
        lax.psum_scatter(grad_gain_a, ("seq", "rep"), scatter_dimension=0, tiled=True),
        lax.psum_scatter(grad_qkv, ("seq", "rep"), scatter_dimension=0, tiled=True),
        lax.psum_scatter(grad_out, ("seq", "rep"), scatter_dimension=0, tiled=True),
        lax.psum_scatter(grad_gain_b, ("seq", "rep"), scatter_dimension=0, tiled=True),
        lax.psum_scatter(grad_gate, ("seq", "rep"), scatter_dimension=0, tiled=True),
        lax.psum_scatter(grad_up, ("seq", "rep"), scatter_dimension=0, tiled=True),
        lax.psum_scatter(grad_down, ("seq", "rep"), scatter_dimension=0, tiled=True),
    )
    return (
        activations,
        d_tokens.reshape(rows_dev, len_dev, width),
        parts[0],
        parts[1],
        parts[2],
        parts[3],
        parts[4],
        parts[5],
        parts[6],
        head_sums[0],
        head_sums[1],
    )


MESH = pl.DeviceIdType.MESH
BF = jnp.bfloat16
F32 = jnp.float32
NEG = -1e30
VMEM_BYTES = 63 * 2**20
QS = 5
DZ = 4
BLK = 128
LEN4 = 512
FFS = 896
BR = 64
HALF = 512
AW = 1024
QKV_W = 640
SCALE = HD ** (-0.5)
CHUNKS = ((0, 384), (384, 512))
QKV_M, OUT_M, F0_M, F1_M = range(4)


def place():
    s = lax.axis_index("seq")
    r = lax.axis_index("rep")
    return lax.div(s, 2), lax.rem(s, 2), lax.div(r, 2), lax.rem(r, 2)


def dev(x, c, z, y):
    return {"seq": 2 * x + c, "rep": 2 * z + y}


def flip(v, by):
    return v if by == 0 else 1 - v


def near(z):
    return z + 1 - 2 * lax.rem(z, 2)


def inner(z):
    return (z == 1) | (z == 2)


def send(src, dst, send_sem, recv_sem, target):
    pltpu.make_async_remote_copy(
        src_ref=src,
        dst_ref=dst,
        send_sem=send_sem,
        recv_sem=recv_sem,
        device_id=target,
        device_id_type=MESH,
    ).start()


def arrived(ref, sem):
    pltpu.make_async_copy(ref, ref, sem).wait()


def many(first, count):
    return pl.ds(pl.multiple_of(first, count), count)


def rows_of(ref, index, size):
    return ref.at[many(index * size, size)]


def greet(x, c, z, y):
    found = []
    for dz in range(DZ):
        for dx in range(2):
            for dy in range(2):
                for dc in range(2):
                    if (dx or dy or dc) if dz == 0 else dc == 0:
                        found.append(
                            dev(flip(x, dx), flip(c, dc), lax.rem(z + dz, DZ), flip(y, dy))
                        )
    barrier = pltpu.get_barrier_semaphore()
    for target in found:
        pl.semaphore_signal(barrier, inc=1, device_id=target, device_id_type=MESH)
    return lambda: pl.semaphore_wait(barrier, len(found))


def spread_small(src, spot, ss, rs):
    x, c, z, y = place()
    slot = 2 * x + c
    for k, (dx, dy) in enumerate(((1, 1), (1, 0), (0, 1))):
        send(src, spot, ss.at[k], rs.at[slot, 0], dev(flip(x, dx), y, z, flip(y, dy)))

    @pl.when(c == y)
    def _():
        pltpu.make_async_copy(src, spot, rs.at[slot, 0]).start()

    @pl.when(c != y)
    def _():
        send(src, spot, ss.at[3], rs.at[slot, 0], dev(x, y, z, y))


def spread_start(src, full, ss, rs):
    x, c, z, y = place()
    slot = 2 * x + c
    spot = rows_of(full, slot, BLK)
    send(src, spot, ss.at[0], rs.at[slot, 0], dev(1 - x, y, z, y))
    send(src, spot, ss.at[1], rs.at[slot, 0], dev(x, y, z, 1 - y))

    @pl.when(c == y)
    def _():
        pltpu.make_async_copy(src, spot, rs.at[slot, 0]).start()

    @pl.when(c != y)
    def _():
        send(src, spot, ss.at[2], rs.at[slot, 0], dev(x, y, z, y))


def spread_pass(full, ss, rs):
    x, c, z, y = place()
    for side in range(2):

        @pl.when((c == y) if side == 0 else (c != y))
        def _():
            for k in range(2):
                slot = 2 * ((1 - x) if side == 0 else x) + k
                arrived(rows_of(full, slot, BLK), rs.at[slot, 0])
                half = full.at[many(slot * BLK + side * (BLK // 2), BLK // 2)]
                target = dev(x, c, z, 1 - y) if side == 0 else dev(1 - x, c, z, y)
                send(half, half, ss.at[3 + k], rs.at[slot, side], target)


def spread_wait(full, rs):
    x, c, z, y = place()

    @pl.when(c == y)
    def _():
        for k in range(2):
            arrived(rows_of(full, 0, BLK), rs.at[2 * x + k, 0])

    @pl.when(c != y)
    def _():
        for k in range(2):
            for side in range(2):
                arrived(rows_of(full, 0, BLK // 2), rs.at[2 * (1 - x) + k, side])


def spread_sent(src, ss):
    x, c, z, y = place()
    for k in range(2):
        arrived(src, ss.at[k])
        arrived(src.at[pl.ds(0, BLK // 2)], ss.at[3 + k])

    @pl.when(c != y)
    def _():
        arrived(src, ss.at[2])


def small_wait(block, rs):
    for j in range(4):
        arrived(block, rs.at[j, 0])


def small_sent(src, ss):
    x, c, z, y = place()
    for k in range(3):
        arrived(src, ss.at[k])

    @pl.when(c != y)
    def _():
        arrived(src, ss.at[3])


BLOCK_ORDER = ((1, 1), (1, 0), (0, 1), (0, 0))


def block_at(order):
    x, c, z, y = place()
    dx, dc = BLOCK_ORDER[order]
    return 2 * flip(x, dx) + flip(c, dc)


def collect_halves(partial, helper, ss, hs):
    x, c, z, y = place()

    @pl.when(c != y)
    def _():
        for k in range(2):
            row = (2 * (1 - x) + k) * BLK
            for side, target in enumerate((dev(1 - x, c, z, y), dev(x, c, z, 1 - y))):
                half = partial.at[many(row + side * (BLK // 2), BLK // 2)]
                send(half, helper.at[k], ss.at[2 * k + side], hs.at[k], target)


def collect_near(partial, inbox, ss, rs):
    x, c, z, y = place()

    @pl.when(c == y)
    def _():
        own = rows_of(partial, 2 * x + c, BLK)
        other = rows_of(partial, 2 * x + 1 - c, BLK)
        pltpu.make_async_copy(own, inbox.at[0], rs.at[0]).start()
        send(other, inbox.at[0], ss.at[0], rs.at[0], dev(x, 1 - c, z, y))


def collect_far(partial, helper, inbox, ss, rs, hs):
    x, c, z, y = place()
    for k in range(2):
        arrived(helper.at[k], hs.at[k])
    for side in range(2):

        @pl.when((c != y) if side == 0 else (c == y))
        def _():
            tx = x if side == 0 else 1 - x
            slot = 2 if side == 0 else 1
            for k in range(2):
                row = (2 * tx + k) * BLK
                rows = many(row + side * (BLK // 2), BLK // 2)
                partial[rows, :] = (partial[rows, :].astype(F32) + helper[k].astype(F32)).astype(BF)
                send(
                    partial.at[many(row, BLK)], inbox.at[slot], ss.at[4 + k], rs.at[slot], dev(tx, k, z, c)
                )


def collect_wait(inbox, rs):
    for j in range(3):
        arrived(inbox.at[j], rs.at[j])


def collect_sent(inbox, helper, ss):
    x, c, z, y = place()
    for k in range(2):
        arrived(inbox.at[0], ss.at[4 + k])

    @pl.when(c == y)
    def _():
        arrived(inbox.at[0], ss.at[0])

    @pl.when(c != y)
    def _():
        for k in range(4):
            arrived(helper.at[0], ss.at[k])


def inbox_sum(inbox):
    return inbox[0].astype(F32) + inbox[1].astype(F32) + inbox[2].astype(F32)


def mm(left, right):
    return lax.dot_general(left, right, (((1,), (0,)), ((), ())), preferred_element_type=F32)


def mm_nt(left, right):
    return lax.dot_general(left, right, (((1,), (1,)), ((), ())), preferred_element_type=F32)


def mm_tn(left, right):
    return lax.dot_general(left, right, (((0,), (0,)), ((), ())), preferred_element_type=F32)


def group_of(local_head):
    x, c, z, y = place()
    return jnp.where(local_head + 2 * x + y >= 4, 1, 0)


def layer_body(
    tok, cot, small, wq, wo, wg, wu, wd,
    act_o, dtok_o, end_f, end_a, vr,
    wap, smallf, xf, n1, wav, w3, dyf, n2f, part, inbox, helper, active, dgu,
    qkvt, dqkvt, dqkv, qt, kt, kk, vt, vv, lse, att, cs, grow, hid, blk, dot_s, dkt, dvt,
    help_f, come_f, help_a, come_a, arecv, vec, vecr, gp2,
    sp_ss, sp_rs, co_ss, co_rs, co_hs, w_ss, w_rs, l_ss, l_rs, c_ss, c_rs, g_ss, g_rs, h_ss, h_rs, o_ss, o_rs, p_ss, p_rs, v_ss, v_rs,
    ready,
):
    x, c, z, y = place()
    shard = 2 * x + y
    me = (2 * x + c) * 2 * DZ + 2 * z + y
    mid = inner(z)
    sibling = dev(x, 1 - c, z, y)
    pair, across = near(z), DZ - 1 - z
    far = DZ - 1 - pair
    SMALL, TOK, COT, N2, DAB = range(5)
    OUT, DN, YY, DT = range(4)

    def own_pieces(m, to_shard):
        if m == QKV_M:
            return [wap.at[to_shard, :, pl.ds(0, QKV_W)]]
        if m == OUT_M:
            return [wap.at[to_shard, :, pl.ds(QKV_W, AW - QKV_W)]]
        lo, wide = CHUNKS[m - F0_M]
        lanes = pl.ds(pl.multiple_of(to_shard * FFS + lo, 128), wide)
        return [ref.at[:, lanes] for ref in (wg, wu, wd)]

    def spots(m, rows):
        if m < F0_M:
            return [held(m, rows, BR)]
        lo, wide = CHUNKS[m - F0_M]
        return [w3.at[many(rows, BR), pl.ds(3 * lo + j * wide, wide)] for j in range(3)]

    def held(m, first, count):
        rows = many(first, count)
        if m == QKV_M:
            return wav.at[rows, pl.ds(0, QKV_W)]
        if m == OUT_M:
            return wav.at[rows, pl.ds(QKV_W, AW - QKV_W)]
        lo, wide = CHUNKS[m - F0_M]
        return w3.at[rows, pl.ds(3 * lo, 3 * wide)]

    def weights_start(m):
        for dx, dy in ((1, 1), (1, 0), (0, 1), (0, 0)):
            tx, ty = flip(x, dx), flip(y, dy)
            for src, spot in zip(own_pieces(m, 2 * tx + ty), spots(m, me * BR)):
                if dx or dy:
                    send(src, spot, w_ss.at[m, 2 * dx + dy - 1], w_rs.at[m, shard], dev(tx, c, z, ty))
                else:
                    pltpu.make_async_copy(src, spot, w_rs.at[m, shard]).start()

    def line(m, from_plane, to_plane, k):
        for tx in range(2):
            slab = held(m, ((2 * tx + c) * DZ + from_plane) * 2 * BR, 2 * BR)
            send(slab, slab, l_ss.at[m, 2 * k + tx], l_rs.at[m, 2 * from_plane + tx], dev(x, c, to_plane, y))

    def line_wait(m, plane):
        for tx in range(2):
            arrived(held(m, 0, 2 * BR), l_rs.at[m, 2 * plane + tx])

    def weights_line(m):
        for k in range(4):
            arrived(held(m, 0, BR), w_rs.at[m, k])
        line(m, z, pair, 0)

        @pl.when(mid)
        def _():
            line(m, z, across, 1)

    def weights_pass_near(m):
        @pl.when(mid)
        def _():
            line_wait(m, pair)
            line(m, pair, across, 2)
            line_wait(m, across)
            line(m, across, pair, 3)

    def weights_pass_far(m):
        @pl.when(mid)
        def _():
            line_wait(m, far)
            line(m, far, pair, 4)

    def weights_swap(m):
        @pl.when(jnp.logical_not(mid))
        def _():
            for plane in (pair, far, across):
                line_wait(m, plane)

        for tx in range(2):
            half = held(m, (2 * tx + c) * HALF, HALF)
            send(half, half, c_ss.at[m, tx], c_rs.at[m, tx], sibling)

    def weights_wait(m):
        for tx in range(2):
            arrived(held(m, 0, HALF), c_rs.at[m, tx])

    def weights_sent(m):
        for k in range(3):
            arrived(held(m, 0, BR), w_ss.at[m, k])
        for k in range(2):
            arrived(held(m, 0, 2 * BR), l_ss.at[m, k])

        @pl.when(mid)
        def _():
            for k in range(2, 10):
                arrived(held(m, 0, 2 * BR), l_ss.at[m, k])

        for tx in range(2):
            arrived(held(m, 0, HALF), c_ss.at[m, tx])

    class Grad:
        pass

    def grad(kind, ref, first_row, lo, width, helped, come, final):
        g = Grad()
        lanes = pl.ds(lo, width)
        g.slab = lambda tx, plane: ref.at[many(first_row + (tx * DZ + plane) * 2 * BR, 2 * BR), lanes]
        g.helped, g.come, g.final, g.kind = helped, come, final, kind
        return g

    def start(g):
        k = g.kind

        @pl.when(jnp.logical_not(mid))
        def _():
            for i, plane in enumerate((far, across)):
                for tx in range(2):
                    send(
                        g.slab(tx, plane), g.helped(i, tx), h_ss.at[k, 2 * i + tx], h_rs.at[k, 2 * i + tx],
                        dev(x, c, pair, y),
                    )

        for tx in range(2):
            send(g.slab(tx, pair), g.come(0, tx), o_ss.at[k, tx], o_rs.at[k, tx], dev(x, c, pair, y))

    def join(g, i):
        k = g.kind
        plane = (across, far)[i]

        @pl.when(mid)
        def _():
            for _ in range(1):
                for tx in range(2):
                    rows, more = g.slab(tx, plane), g.helped(i, tx)
                    arrived(more, h_rs.at[k, 2 * i + tx])
                    rows[...] = (rows[...].astype(F32) + more[...].astype(F32)).astype(BF)
                    send(
                        rows, g.come(1, tx), o_ss.at[k, 2 + 2 * i + tx], o_rs.at[k, 2 + tx], dev(x, c, plane, y)
                    )

    def finish(g):
        k = g.kind
        for tx in range(2):
            rows = g.slab(tx, z)
            for i in range(2):
                arrived(rows, o_rs.at[k, 2 * i + tx])
            rows[...] = (
                rows[...].astype(F32) + g.come(0, tx)[...].astype(F32) + g.come(1, tx)[...].astype(F32)
            ).astype(BF)
        for dx, dy in ((1, 1), (1, 0), (0, 1), (0, 0)):
            tx, ty = flip(x, dx), flip(y, dy)
            src = g.slab(tx, z).at[many(ty * BR, BR)]
            if dx or dy:
                send(src, g.final(shard), p_ss.at[k, 2 * dx + dy - 1], p_rs.at[k, shard], dev(tx, c, z, ty))
            else:
                pltpu.make_async_copy(src, g.final(shard), p_rs.at[k, shard]).start()

    def final_wait(g):
        for t in range(4):
            arrived(g.final(0), p_rs.at[g.kind, t])

    def grad_sent(g):
        k = g.kind
        for i in range(3):
            arrived(g.final(0), p_ss.at[k, i])
        for i in range(2):
            arrived(g.slab(0, 0), o_ss.at[k, i])

        @pl.when(mid)
        def _():
            for i in range(2, 6):
                arrived(g.slab(0, 0), o_ss.at[k, i])

        @pl.when(jnp.logical_not(mid))
        def _():
            for i in range(4):
                arrived(g.slab(0, 0), h_ss.at[k, i])

    def ffn_grad(j):
        lo, wide = CHUNKS[j]
        lanes = pl.ds(3 * lo, 3 * wide)
        return grad(
            j, w3, 1024, 3 * lo, 3 * wide,
            lambda i, tx: help_f.at[i, pl.ds(tx * 2 * BR, 2 * BR), lanes],
            lambda i, tx: come_f.at[i, pl.ds(tx * 2 * BR, 2 * BR), lanes],
            lambda t: end_f.at[t, :, lanes],
        )

    GA = grad(
        2, arecv, 0, 0, FFS,
        lambda i, tx: help_a.at[i, pl.ds(tx * 2 * BR, 2 * BR)],
        lambda i, tx: come_a.at[i, pl.ds(tx * 2 * BR, 2 * BR)],
        lambda t: end_a.at[t],
    )
    F0, F1 = ffn_grad(0), ffn_grad(1)

    def collect_step(order, side, kind):
        if order == 1:
            collect_halves(part.at[side], helper.at[side], co_ss.at[kind], co_hs.at[kind])
        if order == 3:
            collect_near(part.at[side], inbox.at[side], co_ss.at[kind], co_rs.at[kind])

    def collect_last(side, kind):
        collect_far(
            part.at[side], helper.at[side], inbox.at[side], co_ss.at[kind], co_rs.at[kind], co_hs.at[kind]
        )

    everyone_here = greet(x, c, z, y)
    turned = jnp.transpose(small[...])
    lane = lax.broadcasted_iota(jnp.int32, (BR, 64), 1)
    gains = jnp.where(lane == 0, turned[0:64, 0:1], jnp.where(lane == 1, turned[0:64, 1:2], 0.0))
    gq, gk, fr = turned[0:64, 2:3], turned[0:64, 3:4], turned[0:32, 5:6]
    for t in range(4):
        wap[t, :, 0:320] = wq[:, 320 * t : 320 * t + 320]
        wap[t, :, 320:448] = wq[:, QW + 64 * t : QW + 64 * t + 128]
        wap[t, :, 448:576] = wq[:, QW + KW + 64 * t : QW + KW + 64 * t + 128]
        wap[t, :, 576:640] = gains.astype(BF)
        wap[t, :, 640:704] = jnp.zeros((BR, 64), BF)
        wap[t, :, 704:1024] = wo[:, 320 * t : 320 * t + 320]
    everyone_here()
    weights_start(QKV_M)
    spot = smallf.at[:, many((2 * x + c) * BLK, BLK)]
    spread_small(small, spot, sp_ss.at[SMALL], sp_rs.at[SMALL])
    weights_start(OUT_M)
    spread_start(tok, xf, sp_ss.at[TOK], sp_rs.at[TOK])
    weights_start(F0_M)
    weights_start(F1_M)
    weights_line(QKV_M)
    weights_line(OUT_M)
    small_wait(spot, sp_rs.at[SMALL])
    seg_row = smallf[4:5, :]
    seg_col = jnp.transpose(smallf[...])[:, 4:5]
    key_at = lax.broadcasted_iota(jnp.int32, (LEN4, LEN4), 0)
    query_at = lax.broadcasted_iota(jnp.int32, (LEN4, LEN4), 1)
    allowed = (key_at <= query_at) & (seg_col == seg_row)
    earlier = jnp.sum(jnp.where(seg_col < seg_row, 1.0, 0.0), axis=0, keepdims=True)
    index = lax.broadcasted_iota(jnp.int32, (1, LEN4), 1).astype(F32)
    angles = fr * (index - earlier)
    cs[0:32, :] = jnp.cos(angles)
    cs[32:64, :] = jnp.sin(angles)
    weights_pass_near(QKV_M)
    weights_pass_near(OUT_M)
    spread_pass(xf, sp_ss.at[TOK], sp_rs.at[TOK])
    weights_line(F0_M)
    weights_pass_far(QKV_M)
    weights_pass_far(OUT_M)
    weights_line(F1_M)
    weights_swap(QKV_M)
    spread_wait(xf, sp_rs.at[TOK])
    spread_start(cot, dyf, sp_ss.at[COT], sp_rs.at[COT])
    weights_wait(QKV_M)
    grow[...] = jnp.transpose(wav[:, 512:640].astype(F32))[64:72, :]

    @pl.loop(0, 4)
    def _(j):
        rows = many(j * BLK, BLK)
        v = xf[rows, :].astype(F32)
        n1[rows, :] = (
            v * lax.rsqrt(jnp.mean(v * v, axis=1, keepdims=True) + norm_eps) * grow[0:1, :]
        ).astype(BF)

    @pl.loop(0, 5)
    def _(j):
        wide = many(j * 128, 128)
        qkvt[wide, :] = jnp.transpose(mm(n1[...], wav[:, wide]))

    def rotated(v, gain):
        cos, sin = cs[0:32, :], cs[32:64, :]
        v = v * lax.rsqrt(jnp.mean(v * v, axis=0, keepdims=True) + norm_eps) * gain
        first, second = v[0:32, :], v[32:64, :]
        return first * cos - second * sin, second * cos + first * sin

    for h in range(QS):
        first, second = rotated(qkvt[h * 64 : h * 64 + 64, :], gq)
        qt[h, 0:32, :] = first.astype(BF)
        qt[h, 32:64, :] = second.astype(BF)
    for g in range(2):
        base = QS * 64 + g * 64
        first, second = rotated(qkvt[base : base + 64, :], gk)
        both = jnp.concatenate([first, second], axis=0)
        kt[g] = both.astype(BF)
        kk[g] = jnp.transpose(both).astype(BF)
        value = qkvt[base + 128 : base + 192, :]
        vt[g] = value.astype(BF)
        vv[g] = jnp.transpose(value).astype(BF)
    weights_swap(OUT_M)
    spread_pass(dyf, sp_ss.at[COT], sp_rs.at[COT])
    dqkvt[0:64, :] = jnp.zeros((64, LEN4), F32)
    for h in range(QS):
        g = group_of(h)
        scores = jnp.where(allowed, mm(kk[g], qt[h]) * SCALE, NEG)
        top = jnp.max(scores, axis=0, keepdims=True)
        weights = jnp.exp(scores - top)
        total = jnp.sum(weights, axis=0, keepdims=True)
        lse[h : h + 1, :] = top + jnp.log(total)
        dqkvt[h * 64 + 64 : h * 64 + 128, :] = mm(vt[g], (weights / total).astype(BF))
    att[...] = jnp.transpose(dqkvt[0:384, :]).astype(BF)
    weights_pass_near(F0_M)
    weights_wait(OUT_M)
    for order in range(4):
        rows = many(block_at(order) * BLK, BLK)
        part[0, rows, :] = mm_nt(att[rows, :], wav[:, QKV_W:AW]).astype(BF)
        collect_step(order, 0, OUT)
    collect_last(0, OUT)
    weights_pass_near(F1_M)
    weights_pass_far(F0_M)
    collect_wait(inbox.at[0], co_rs.at[OUT])
    spread_sent(tok, sp_ss.at[TOK])
    hidden = tok[...].astype(F32) + inbox_sum(inbox.at[0])
    hid[...] = hidden
    blk[0] = (
        hidden
        * lax.rsqrt(jnp.mean(hidden * hidden, axis=1, keepdims=True) + norm_eps)
        * grow[1:2, :]
    ).astype(BF)
    spread_start(blk.at[0], n2f, sp_ss.at[N2], sp_rs.at[N2])
    spread_pass(n2f, sp_ss.at[N2], sp_rs.at[N2])
    weights_pass_far(F1_M)
    weights_swap(F0_M)
    spread_wait(dyf, sp_rs.at[COT])
    spread_wait(n2f, sp_rs.at[N2])
    weights_wait(F0_M)

    def hidden_units(j):
        first, width = CHUNKS[j]
        base = 3 * first
        for lo in range(0, width, 256):
            wide = min(256, width - lo)
            gate = mm(n2f[...], w3[:, base + lo : base + lo + wide])
            upward = mm(n2f[...], w3[:, base + width + lo : base + width + lo + wide])
            grad_in = mm(dyf[...], w3[:, base + 2 * width + lo : base + 2 * width + lo + wide])
            sig = 1.0 / (1.0 + jnp.exp(-gate))
            silu = gate * sig
            active[:, first + lo : first + lo + wide] = (silu * upward).astype(BF)
            at = 2 * first + lo
            dgu[:, at : at + wide] = (grad_in * upward * (sig * (1.0 + gate * (1.0 - sig)))).astype(BF)
            at = at + width
            dgu[:, at : at + wide] = (grad_in * silu).astype(BF)

    def dn_part(j, rows, wide):
        first, width = CHUNKS[j]
        return mm_nt(dgu[rows, 2 * first : 2 * first + 2 * width], w3[wide, 3 * first : 3 * first + 2 * width])

    def y_part(j, rows, wide):
        first, width = CHUNKS[j]
        at = 3 * first + 2 * width
        return mm_nt(active[rows, first : first + width], w3[wide, at : at + width])

    def ffn_grads(j, core, row):
        first, width = CHUNKS[j]
        wide = many((2 * lax.div(row, 2) + core) * HALF + lax.rem(row, 2) * 256, 256)
        return (
            mm_tn(n2f[:, wide], dgu[:, 2 * first : 2 * first + 2 * width]),
            mm_tn(dyf[:, wide], active[:, first : first + width]),
        )

    def chunk_lanes(j):
        first, width = CHUNKS[j]
        return pl.ds(3 * first, 2 * width), pl.ds(3 * first + 2 * width, width), pl.ds(3 * first, 3 * width)

    def grads_swap(j):
        two, one, both = chunk_lanes(j)
        weights_sent(F0_M + j)
        pl.semaphore_signal(ready.at[j], inc=1, device_id=sibling, device_id_type=MESH)

        @pl.loop(0, 4)
        def _(row):
            rows = many(row * 256, 256)
            gu, down = ffn_grads(j, 1 - c, row)
            w3[rows, two] = gu.astype(BF)
            w3[rows, one] = down.astype(BF)

        pl.semaphore_wait(ready.at[j], 1)
        send(
            w3.at[pl.ds(0, 1024), both], w3.at[pl.ds(1024, 1024), both], g_ss.at[j], g_rs.at[j], sibling
        )

    def grads_own(j):
        two, one, both = chunk_lanes(j)
        arrived(w3.at[pl.ds(1024, 1024), both], g_rs.at[j])

        @pl.loop(0, 4)
        def _(row):
            rows = many(1024 + row * 256, 256)
            gu, down = ffn_grads(j, c, row)
            w3[rows, two] = (gu + w3[rows, two].astype(F32)).astype(BF)
            w3[rows, one] = (down + w3[rows, one].astype(F32)).astype(BF)

    every = slice(0, LEN4)
    hidden_units(0)
    collect_sent(inbox.at[0], helper.at[0], co_ss.at[OUT])
    spread_sent(cot, sp_ss.at[COT])

    @pl.loop(0, 8)
    def _(j):
        wide = many(j * 256, 256)
        part[1, :, wide] = dn_part(0, every, wide).astype(BF)
        part[0, :, wide] = y_part(0, every, wide).astype(BF)

    grads_swap(0)
    grads_own(0)
    start(F0)
    weights_swap(F1_M)
    weights_wait(F1_M)
    hidden_units(1)
    for order in range(4):
        rows = many(block_at(order) * BLK, BLK)

        @pl.loop(0, 4)
        def _(j):
            wide = many(j * 512, 512)
            part[1, rows, wide] = (part[1, rows, wide].astype(F32) + dn_part(1, rows, wide)).astype(BF)

        collect_step(order, 1, DN)

    collect_last(1, DN)

    @pl.loop(0, 8)
    def _(j):
        wide = many(j * 256, 256)
        part[0, :, wide] = (part[0, :, wide].astype(F32) + y_part(1, every, wide)).astype(BF)

    grads_swap(1)
    join(F0, 0)
    grads_own(1)
    start(F1)
    join(F0, 1)
    collect_wait(inbox.at[1], co_rs.at[DN])
    dn = inbox_sum(inbox.at[1])
    h = hid[...]
    r = lax.rsqrt(jnp.mean(h * h, axis=1, keepdims=True) + norm_eps)
    gp2[...] = jnp.broadcast_to(jnp.sum(dn * h * r, axis=0, keepdims=True), gp2.shape)
    a = dn * grow[1:2, :]
    dh = cot[...].astype(F32) + r * (a - h * (r * r * jnp.mean(a * h, axis=1, keepdims=True)))
    dtok_o[...] = dh
    blk[1] = dh.astype(BF)
    spread_start(blk.at[1], xf, sp_ss.at[DAB], sp_rs.at[DAB])
    spread_pass(xf, sp_ss.at[DAB], sp_rs.at[DAB])
    collect_step(1, 0, YY)
    collect_step(3, 0, YY)
    def att_grads(core, row):
        wide = many((2 * lax.div(row, 2) + core) * HALF + lax.rem(row, 2) * 256, 256)
        one, two = mm_tn(n1[:, wide], dqkv[...]), mm_tn(xf[:, wide], att[...])
        return one[:, 0:512], one[:, 512:640] + two[:, 0:128], two[:, 128:384]

    def att_grads_swap():
        @pl.loop(0, 4)
        def _(row):
            rows = many(lax.rem(row, 2) * 256, 256)
            side = lax.div(row, 2) * AW
            one, both, two = att_grads(1 - c, row)
            dyf[rows, pl.ds(pl.multiple_of(side, 128), 512)] = one.astype(BF)
            dyf[rows, pl.ds(pl.multiple_of(side + 512, 128), 128)] = both.astype(BF)
            dyf[rows, pl.ds(pl.multiple_of(side + 640, 128), 256)] = two.astype(BF)

        for side in range(2):
            send(
                dyf.at[:, pl.ds(side * AW, FFS)], arecv.at[pl.ds(side * HALF, HALF)],
                g_ss.at[2 + side], g_rs.at[2 + side], sibling,
            )

    def att_grads_own():
        for side in range(2):
            arrived(arecv.at[pl.ds(0, HALF)], g_rs.at[2 + side])

        @pl.loop(0, 4)
        def _(row):
            rows = many(row * 256, 256)
            one, both, two = att_grads(c, row)
            arecv[rows, 0:512] = (one + arecv[rows, 0:512].astype(F32)).astype(BF)
            arecv[rows, 512:640] = (both + arecv[rows, 512:640].astype(F32)).astype(BF)
            arecv[rows, 640:896] = (two + arecv[rows, 640:896].astype(F32)).astype(BF)

    spread_wait(xf, sp_rs.at[DAB])
    dot_s[...] = jnp.transpose(mm(xf[...], wav[:, QKV_W:AW]).astype(BF).astype(F32)).astype(BF)
    dkt[...] = jnp.zeros_like(dkt)
    dvt[...] = jnp.zeros_like(dvt)

    def unrotated(first, second, raw, gain):
        cos, sin = cs[0:32, :], cs[32:64, :]
        d_first = first * cos + second * sin
        d_second = second * cos - first * sin
        d = jnp.concatenate([d_first, d_second], axis=0)
        r = lax.rsqrt(jnp.mean(raw * raw, axis=0, keepdims=True) + norm_eps)
        d_gain = jnp.sum(d * raw * r, axis=1, keepdims=True)
        a = d * gain
        return r * (a - raw * (r * r * jnp.mean(a * raw, axis=0, keepdims=True))), d_gain

    dq_gain = jnp.zeros((64, 1), F32)
    for h in range(QS):
        g = group_of(h)
        scores = mm(kk[g], qt[h]) * SCALE
        p = jnp.where(allowed, jnp.exp(scores - lse[h : h + 1, :]), 0.0)
        d_out = dot_s[h * 64 + 64 : h * 64 + 128, :]
        dvt[g] += mm_nt(d_out, p.astype(BF))
        dp = mm(vv[g], d_out)
        ds = (p * (dp - jnp.sum(p * dp, axis=0, keepdims=True))).astype(BF)
        dkt[g] += mm_nt(qt[h], ds) * SCALE
        dq = (mm(kt[g], ds) * SCALE).astype(BF).astype(F32)
        d, more = unrotated(dq[0:32, :], dq[32:64, :], qkvt[h * 64 : h * 64 + 64, :], gq)
        dq_gain = dq_gain + more
        dqkvt[h * 64 : h * 64 + 64, :] = d
        for g_at, i in JOIN_AFTER.get(h, ()):
            join((F0, F1)[g_at], i)
    dk_gain = jnp.zeros((64, 1), F32)
    for g in range(2):
        base = QS * 64 + g * 64
        dk = dkt[g].astype(BF).astype(F32)
        d, more = unrotated(dk[0:32, :], dk[32:64, :], qkvt[base : base + 64, :], gk)
        dk_gain = dk_gain + more
        dqkvt[base : base + 64, :] = d
        dqkvt[base + 128 : base + 192, :] = dvt[g]
    dqkvt[576:640, :] = jnp.zeros((64, LEN4), F32)
    dqkv[...] = jnp.transpose(dqkvt[...]).astype(BF)
    att_grads_swap()
    collect_sent(inbox.at[1], helper.at[1], co_ss.at[DN])
    for order in range(4):
        rows = many(block_at(order) * BLK, BLK)
        part[1, rows, :] = mm_nt(dqkv[rows, :], wav[:, 0:QKV_W]).astype(BF)
        collect_step(order, 1, DT)

    join(F1, 1)
    att_grads_own()
    start(GA)
    finish(F0)
    collect_last(1, DT)
    collect_last(0, YY)
    finish(F1)
    collect_wait(inbox.at[0], co_rs.at[YY])
    act_o[...] = (hid[...] + inbox_sum(inbox.at[0])).astype(BF)
    join(GA, 0)
    join(GA, 1)
    collect_wait(inbox.at[1], co_rs.at[DT])
    dn = inbox_sum(inbox.at[1])
    xv = tok[...].astype(F32)
    r = lax.rsqrt(jnp.mean(xv * xv, axis=1, keepdims=True) + norm_eps)
    gain_a = jnp.sum(dn * xv * r, axis=0, keepdims=True)
    b = dn * grow[0:1, :]
    dtok_o[...] += r * (b - xv * (r * r * jnp.mean(b * xv, axis=1, keepdims=True)))
    qk = jnp.transpose(
        jnp.concatenate(
            [jnp.broadcast_to(dq_gain, (64, 128)), jnp.broadcast_to(dk_gain, (64, 128))], axis=0
        )
    )
    gain_b = gp2[0:1, :]
    vec[...] = jnp.zeros_like(vec)
    for i in range(4 * DZ):
        for half in range(2):
            at = (((i // (2 * DZ)) * 2 + half) * 2 * DZ + i % (2 * DZ)) * BR
            vec[half, i, 0:4, 0:64] = jnp.concatenate(
                [gain_a[:, at : at + BR], gain_b[:, at : at + BR], qk[0:1, 0:64], qk[0:1, 64:128]], axis=0
            )
    send(vec.at[1 - c], vecr, g_ss.at[6], g_rs.at[6], sibling)
    arrived(vecr, g_rs.at[6])
    vecr[...] += vec[c]
    source = shard * DZ + z
    for dz in range(DZ):
        for dx in range(2):
            for dy in range(2):
                tx, ty, tz = flip(x, dx), flip(y, dy), lax.rem(z + dz, DZ)
                src = vecr.at[(tx * DZ + tz) * 2 + ty]
                k = (dz * 2 + dx) * 2 + dy
                if k == 0:
                    pltpu.make_async_copy(src, vr.at[source], v_rs.at[source]).start()
                else:
                    send(src, vr.at[source], v_ss.at[k], v_rs.at[source], dev(tx, c, tz, ty))
    finish(GA)
    for i in range(4 * DZ):
        arrived(vr.at[0], v_rs.at[i])
    for g in (F0, F1, GA):
        final_wait(g)
    for g in (F0, F1, GA):
        grad_sent(g)
    weights_sent(QKV_M)
    weights_sent(OUT_M)
    for i in range(1, 4 * DZ):
        arrived(vr.at[0], v_ss.at[i])
    for j in range(2):
        arrived(w3.at[pl.ds(0, 1024), chunk_lanes(j)[2]], g_ss.at[j])
    for side in range(2):
        arrived(arecv.at[pl.ds(0, HALF)], g_ss.at[2 + side])
    arrived(vecr, g_ss.at[6])
    small_sent(small, sp_ss.at[SMALL])
    spread_sent(blk.at[0], sp_ss.at[N2])
    spread_sent(blk.at[1], sp_ss.at[DAB])
    collect_sent(inbox.at[0], helper.at[0], co_ss.at[YY])
    collect_sent(inbox.at[1], helper.at[1], co_ss.at[DT])


JOIN_AFTER = {1: ((1, 0),)}


def results_body(
    act, dtok, end_f, end_a, vr, act_o, dtok_o, ga_o, gqkv_o, go_o, gf_o, gate_o, up_o, down_o, gq_o, gk_o
):
    act_o[...] = act[...]
    dtok_o[...] = dtok[...]
    sums = jnp.sum(vr[...], axis=0)
    for i, out in enumerate((ga_o, gf_o, gq_o, gk_o)):
        out[...] = sums[i : i + 1, 0:64]
    for t in range(4):
        for j, out in enumerate((gate_o, up_o, down_o)):
            for first, width in CHUNKS:
                at = 3 * first + j * width
                out[:, t * FFS + first : t * FFS + first + width] = end_f[t, :, at : at + width].astype(F32)
        go_o[:, 320 * t : 320 * t + 320] = end_a[t, :, 576:896].astype(F32)
        gqkv_o[:, 320 * t : 320 * t + 320] = end_a[t, :, 0:320].astype(F32)
    for lo, to in ((320, QW), (448, QW + KW)):
        for g in range(5):
            parts = []
            if g < 4:
                parts.append(end_a[g, :, lo : lo + 64].astype(F32))
            if g > 0:
                parts.append(end_a[g - 1, :, lo + 64 : lo + 128].astype(F32))
            gqkv_o[:, to + 64 * g : to + 64 * g + 64] = sum(parts[1:], parts[0])


def plane_plan(
    tokens, segment_ids, cotangent, attn_gain, w_qkv, w_out, ffn_gain, w_gate, w_up, w_down, q_gain, k_gain
):
    width = tokens.shape[-1]
    freqs = rope_base ** (-jnp.arange(32, dtype=jnp.float32) * 2.0 / HD)

    def lanes(v):
        v = v.astype(F32).reshape(1, -1)
        return jnp.pad(v, ((0, 0), (0, BLK - v.shape[1])))

    small = jnp.concatenate(
        [lanes(v) for v in (attn_gain, ffn_gain, q_gain, k_gain, segment_ids, freqs)]
        + [jnp.zeros((2, BLK), F32)],
        axis=0,
    )
    dma = pltpu.SemaphoreType.DMA
    vm = pltpu.VMEM
    far, close = pl.BlockSpec(memory_space=pl.ANY), pl.BlockSpec(memory_space=pltpu.VMEM)
    halves = pl.pallas_call(
        layer_body,
        out_shape=[
            jax.ShapeDtypeStruct((BLK, width), BF),
            jax.ShapeDtypeStruct((BLK, width), F32),
            jax.ShapeDtypeStruct((4, BR, 3 * FFS), BF),
            jax.ShapeDtypeStruct((4, BR, FFS), BF),
            jax.ShapeDtypeStruct((4 * DZ, 8, BLK), F32),
        ],
        in_specs=[close] * 5 + [far] * 3,
        out_specs=[close] * 2 + [far] * 3,
        scratch_shapes=[
            vm((4, BR, AW), BF),
            vm((8, LEN4), F32),
            vm((LEN4, width), BF),
            vm((LEN4, width), BF),
            vm((2048, AW), BF),
            vm((2048, 3 * FFS), BF),
            vm((LEN4, width), BF),
            vm((LEN4, width), BF),
            vm((2, LEN4, width), BF),
            vm((2, 3, BLK, width), BF),
            vm((2, 2, BLK // 2, width), BF),
            vm((LEN4, FFS), BF),
            vm((LEN4, 2 * FFS), BF),
            vm((QKV_W, LEN4), F32),
            vm((QKV_W, LEN4), F32),
            vm((LEN4, QKV_W), BF),
            vm((QS, 64, LEN4), BF),
            vm((2, 64, LEN4), BF),
            vm((2, LEN4, 64), BF),
            vm((2, 64, LEN4), BF),
            vm((2, LEN4, 64), BF),
            vm((8, LEN4), F32),
            vm((LEN4, 384), BF),
            vm((64, LEN4), F32),
            vm((8, width), F32),
            vm((BLK, width), F32),
            vm((2, BLK, width), BF),
            vm((384, LEN4), BF),
            vm((2, 64, LEN4), F32),
            vm((2, 64, LEN4), F32),
            vm((2, 4 * BR, 3 * FFS), BF),
            vm((2, 4 * BR, 3 * FFS), BF),
            vm((2, 4 * BR, FFS), BF),
            vm((2, 4 * BR, FFS), BF),
            vm((1024, FFS), BF),
            vm((2, 4 * DZ, 8, BLK), F32),
            vm((4 * DZ, 8, BLK), F32),
            vm((8, width), F32),
            dma((5, 5)), dma((5, 4, 2)),
            dma((4, 6)), dma((4, 3)), dma((4, 2)),
            dma((5, 3)), dma((5, 4)), dma((5, 10)), dma((5, 8)),
            dma((5, 2)), dma((5, 2)),
            dma((8,)), dma((8,)),
            dma((5, 4)), dma((5, 4)),
            dma((5, 6)), dma((5, 4)), dma((5, 3)), dma((5, 4)),
            dma((16,)), dma((16,)),
            pltpu.SemaphoreType.REGULAR((2,)),
        ],
        compiler_params=pltpu.CompilerParams(
            collective_id=0, has_side_effects=True, vmem_limit_bytes=VMEM_BYTES
        ),
    )(
        tokens.reshape(BLK, width), cotangent.reshape(BLK, width), small, w_qkv, w_out, w_gate, w_up, w_down
    )
    outs = pl.pallas_call(
        results_body,
        out_shape=[
            jax.ShapeDtypeStruct((BLK, width), BF),
            jax.ShapeDtypeStruct((BLK, width), F32),
            jax.ShapeDtypeStruct((1, BR), F32),
            jax.ShapeDtypeStruct(w_qkv.shape, F32),
            jax.ShapeDtypeStruct(w_out.shape, F32),
            jax.ShapeDtypeStruct((1, BR), F32),
            jax.ShapeDtypeStruct(w_gate.shape, F32),
            jax.ShapeDtypeStruct(w_up.shape, F32),
            jax.ShapeDtypeStruct(w_down.shape, F32),
            jax.ShapeDtypeStruct((1, HD), F32),
            jax.ShapeDtypeStruct((1, HD), F32),
        ],
        in_specs=[close] * 5,
        out_specs=[close] * 11,
        compiler_params=pltpu.CompilerParams(vmem_limit_bytes=60 * 2**20),
    )(*halves)
    shapes = (
        tokens.shape, tokens.shape, (BR,), w_qkv.shape, w_out.shape, (BR,), w_gate.shape, w_up.shape, w_down.shape,
        (HD,), (HD,),
    )
    return tuple(out.reshape(shape) for out, shape in zip(outs, shapes))


def solution(mesh):
    in_specs = (
        P("rep", "seq", None),
        P("rep", "seq"),
        P("rep", "seq", None),
        P(("seq", "rep")),
        P(("seq", "rep"), None),
        P(("seq", "rep"), None),
        P(("seq", "rep")),
        P(("seq", "rep"), None),
        P(("seq", "rep"), None),
        P(("seq", "rep"), None),
        P(),
        P(),
    )
    out_specs = (
        P("rep", "seq", None),
        P("rep", "seq", None),
        P(("seq", "rep")),
        P(("seq", "rep"), None),
        P(("seq", "rep"), None),
        P(("seq", "rep")),
        P(("seq", "rep"), None),
        P(("seq", "rep"), None),
        P(("seq", "rep"), None),
        P(),
        P(),
    )
    planes = mesh.shape["seq"] == 4 and mesh.shape["rep"] == 8
    body = plane_plan if planes else shards
    return jax.shard_map(body, mesh=mesh, in_specs=in_specs, out_specs=out_specs, check_vma=False)
```

```python
import jax
import jax.numpy as jnp
from jax import lax
from jax.experimental import pallas as pl
from jax.experimental.pallas import tpu as pltpu
from jax.sharding import PartitionSpec as P

QH = 20
KVG = 5
HD = 64
QW = 1280
KW = 320


norm_eps = 1e-06
rope_base = 10000.0


def norm_rows(value_matrix, gain):
    return (
        value_matrix
        * lax.rsqrt(jnp.mean(value_matrix * value_matrix, axis=-1, keepdims=True) + norm_eps)
        * gain
    )


def rotate_heads(value_matrix, positions):
    half = value_matrix.shape[-1] // 2
    freqs = rope_base ** (-jnp.arange(half, dtype=jnp.float32) * 2.0 / value_matrix.shape[-1])
    angles = positions.astype(jnp.float32)[:, None] * freqs[None, :]
    cosine = jnp.cos(angles)[:, None, :]
    sine = jnp.sin(angles)[:, None, :]
    first = value_matrix[..., :half]
    second = value_matrix[..., half:]
    return jnp.concatenate(
        [first * cosine - second * sine, second * cosine + first * sine], axis=-1
    )


def heads_prep(qkv, q_scale, k_scale, positions):
    count = qkv.shape[0]
    query = qkv[:, :QW].reshape(count, QH, HD)
    key = qkv[:, QW : QW + KW].reshape(count, KVG, HD)
    value = qkv[:, QW + KW :].reshape(count, KVG, HD)
    query = rotate_heads(norm_rows(query, q_scale), positions)
    key = rotate_heads(norm_rows(key, k_scale), positions)
    return (query, key, value)


def times_rows(left, right):
    return lax.dot_general(
        left, right, (((1,), (1,)), ((), ())), preferred_element_type=jnp.float32
    )


def token_sum(left, right):
    return lax.dot_general(
        left, right, (((0,), (0,)), ((), ())), preferred_element_type=jnp.float32
    )


def block_scores(query_block, key_matrix, seg_row, start, score_scale):
    width = query_block.shape[1]
    length = key_matrix.shape[1]
    logit_scores = (
        jnp.einsum("zjfr,zyr->zfjy", query_block, key_matrix, preferred_element_type=jnp.float32)
        * score_scale
    )
    rows = start + jnp.arange(width, dtype=jnp.int32)
    cols = jnp.arange(length, dtype=jnp.int32)
    seg_blk = lax.dynamic_slice_in_dim(seg_row, start, width, 1)
    allowed = (cols[None, None, :] <= rows[None, :, None]) & (
        seg_row[:, None, :] == seg_blk[:, :, None]
    )
    return jnp.where(allowed[:, None], logit_scores, -1e30)


def attend_forward(query, key_matrix, value_matrix, seg_row, block):
    length = key_matrix.shape[1]
    score_scale = HD ** (-0.5)

    def one_block(start):
        query_block = lax.dynamic_slice_in_dim(query, start, block, 1)
        logit_scores = block_scores(query_block, key_matrix, seg_row, start, score_scale)
        top = jnp.max(logit_scores, axis=-1, keepdims=True)
        weights = jnp.exp(logit_scores - top)
        total = jnp.sum(weights, axis=-1, keepdims=True)
        attention_probabilities = (weights / total).astype(jnp.bfloat16)
        layer_result = jnp.einsum(
            "szjr,srn->sjzn",
            attention_probabilities,
            value_matrix,
            preferred_element_type=jnp.float32,
        )
        return (layer_result.astype(jnp.bfloat16), (top + jnp.log(total))[..., 0])

    starts = jnp.arange(0, length, block, dtype=jnp.int32)
    return lax.map(one_block, starts)


def attend_backward(query, key_matrix, value_matrix, seg_row, grads_out, lse, block):
    length = key_matrix.shape[1]
    score_scale = HD ** (-0.5)

    def one_block(carry, item):
        d_key, d_value = carry
        start, sums = item
        query_block = lax.dynamic_slice_in_dim(query, start, block, 1)
        gradient_block = lax.dynamic_slice_in_dim(grads_out, start, block, 1)
        logit_scores = block_scores(query_block, key_matrix, seg_row, start, score_scale)
        attention_probabilities = jnp.exp(logit_scores - sums[..., None])
        reduced_probabilities = attention_probabilities.astype(jnp.bfloat16)
        d_value = d_value + jnp.einsum(
            "syer,seyo->sro",
            reduced_probabilities,
            gradient_block,
            preferred_element_type=jnp.float32,
        )
        probability_gradient = jnp.einsum(
            "zjfr,zyr->zfjy", gradient_block, value_matrix, preferred_element_type=jnp.float32
        )
        inner = jnp.sum(attention_probabilities * probability_gradient, axis=-1, keepdims=True)
        score_gradient = (attention_probabilities * (probability_gradient - inner)).astype(
            jnp.bfloat16
        )
        d_query = (
            jnp.einsum(
                "szjr,srn->sjzn", score_gradient, key_matrix, preferred_element_type=jnp.float32
            )
            * score_scale
        )
        d_key = (
            d_key
            + jnp.einsum(
                "syer,seyo->sro", score_gradient, query_block, preferred_element_type=jnp.float32
            )
            * score_scale
        )
        return ((d_key, d_value), d_query)

    starts = jnp.arange(0, length, block, dtype=jnp.int32)
    zeros = jnp.zeros(key_matrix.shape, jnp.float32)
    carry, d_query = lax.scan(one_block, (zeros, zeros), (starts, lse))
    return (d_query, carry[0], carry[1])


def shards(
    tokens,
    segment_ids,
    cotangent,
    attn_gain,
    w_qkv,
    w_out,
    ffn_gain,
    w_gate,
    w_up,
    w_down,
    q_gain,
    k_gain,
):
    groups = lax.axis_size("seq")
    rows_dev, len_dev, width = tokens.shape
    count = rows_dev * len_dev
    per_group = QH // KVG
    places = (KVG + groups - 1) // groups * groups
    place_dev = places // groups
    length = len_dev * groups
    block = min(512, length)
    items = rows_dev * place_dev
    gain_one, qkv_w, out_w, gain_two, gate_w, up_w, down_w = (
        lax.all_gather(attn_gain, ("seq", "rep"), axis=0, tiled=True),
        lax.all_gather(w_qkv, ("seq", "rep"), axis=0, tiled=True),
        lax.all_gather(w_out, ("seq", "rep"), axis=0, tiled=True),
        lax.all_gather(ffn_gain, ("seq", "rep"), axis=0, tiled=True),
        lax.all_gather(w_gate, ("seq", "rep"), axis=0, tiled=True),
        lax.all_gather(w_up, ("seq", "rep"), axis=0, tiled=True),
        lax.all_gather(w_down, ("seq", "rep"), axis=0, tiled=True),
    )
    row_seg = lax.all_gather(segment_ids, "seq", axis=1, tiled=True)
    offset = lax.axis_index("seq") * len_dev
    earlier = jnp.sum((row_seg[:, None, :] < segment_ids[:, :, None]).astype(jnp.int32), axis=2)
    positions = (offset + jnp.arange(len_dev, dtype=jnp.int32)[None, :] - earlier).reshape(count)
    seg_items = jnp.repeat(row_seg, place_dev, axis=0)
    x_rows = tokens.reshape(count, width).astype(jnp.float32)
    gain_a = gain_one.astype(jnp.float32)
    gain_b = gain_two.astype(jnp.float32)
    q_scale = q_gain.astype(jnp.float32)
    k_scale = k_gain.astype(jnp.float32)
    normed = norm_rows(x_rows, gain_a).astype(jnp.bfloat16)
    qkv = jnp.dot(normed, qkv_w, preferred_element_type=jnp.float32)
    query, key, value = heads_prep(qkv, q_scale, k_scale, positions)
    packed = jnp.concatenate(
        [query.reshape(count, KVG, per_group * HD), key, value], axis=2
    ).astype(jnp.bfloat16)
    packed = jnp.pad(packed, ((0, 0), (0, places - KVG), (0, 0))).reshape(
        rows_dev, len_dev, places, -1
    )
    arrived = lax.all_to_all(packed, "seq", split_axis=2, concat_axis=1, tiled=True)
    arrived = arrived.transpose(0, 2, 1, 3).reshape(items, length, -1)
    q_heads = arrived[..., : per_group * HD].reshape(items, length, per_group, HD)
    k_heads = arrived[..., per_group * HD : (per_group + 1) * HD]
    v_heads = arrived[..., (per_group + 1) * HD :]
    outs, lse = attend_forward(q_heads, k_heads, v_heads, seg_items, block)
    attended = (
        outs.transpose(1, 0, 2, 3, 4)
        .reshape(rows_dev, place_dev, length, per_group * HD)
        .transpose(0, 2, 1, 3)
    )
    returned = lax.all_to_all(attended, "seq", split_axis=1, concat_axis=2, tiled=True)
    mixed = returned[:, :, :KVG].reshape(count, QW)
    hidden = x_rows + times_rows(mixed, out_w)
    normed_two = norm_rows(hidden, gain_b).astype(jnp.bfloat16)
    d_result = cotangent.reshape(count, width).astype(jnp.float32)
    gate = jnp.dot(normed_two, gate_w, preferred_element_type=jnp.float32)
    upward = jnp.dot(normed_two, up_w, preferred_element_type=jnp.float32)
    active = (jax.nn.silu(gate) * upward).astype(jnp.bfloat16)
    layer_result = hidden + times_rows(active, down_w)
    d_branch = d_result.astype(jnp.bfloat16)
    d_active = jnp.dot(d_branch, down_w, preferred_element_type=jnp.float32)
    grad_down = token_sum(d_branch, active)
    swiglu_out, swiglu_back = jax.vjp(
        lambda gate_in, up_in: jax.nn.silu(gate_in) * up_in, gate, upward
    )
    d_gate, d_up = swiglu_back(d_active)
    d_gate = d_gate.astype(jnp.bfloat16)
    d_up = d_up.astype(jnp.bfloat16)
    grad_gate = token_sum(normed_two, d_gate)
    grad_up = token_sum(normed_two, d_up)
    d_normed_two = times_rows(d_gate, gate_w) + times_rows(d_up, up_w)
    activations = layer_result.astype(jnp.bfloat16).reshape(rows_dev, len_dev, width)
    second_out, second_back = jax.vjp(norm_rows, hidden, gain_b)
    d_hidden, grad_gain_b = second_back(d_normed_two)
    d_hidden = d_hidden + d_result
    d_attn = d_hidden.astype(jnp.bfloat16)
    grad_out = token_sum(d_attn, mixed)
    d_mixed = jnp.dot(d_attn, out_w, preferred_element_type=jnp.float32).astype(jnp.bfloat16)
    d_pack = jnp.pad(
        d_mixed.reshape(count, KVG, per_group * HD), ((0, 0), (0, places - KVG), (0, 0))
    )
    d_pack = d_pack.reshape(rows_dev, len_dev, places, -1)
    d_arrived = lax.all_to_all(d_pack, "seq", split_axis=2, concat_axis=1, tiled=True)
    d_items = d_arrived.transpose(0, 2, 1, 3).reshape(items, length, per_group, HD)
    d_query, d_key, d_value = attend_backward(
        q_heads, k_heads, v_heads, seg_items, d_items, lse, block
    )
    d_query = d_query.transpose(1, 0, 2, 3, 4).reshape(items, length, per_group * HD)
    d_heads = jnp.concatenate([d_query, d_key, d_value], axis=2).astype(jnp.bfloat16)
    d_heads = d_heads.reshape(rows_dev, place_dev, length, -1).transpose(0, 2, 1, 3)
    d_back = lax.all_to_all(d_heads, "seq", split_axis=1, concat_axis=2, tiled=True)
    d_back = d_back[:, :, :KVG].reshape(count, KVG, -1).astype(jnp.float32)
    d_q_rows = d_back[..., : per_group * HD].reshape(count, QH, HD)
    d_k_rows = d_back[..., per_group * HD : (per_group + 1) * HD]
    d_v_rows = d_back[..., (per_group + 1) * HD :]
    prep_out, prep_back = jax.vjp(
        lambda qkv_in, qs_in, ks_in: heads_prep(qkv_in, qs_in, ks_in, positions),
        qkv,
        q_scale,
        k_scale,
    )
    d_qkv, grad_q_scale, grad_k_scale = prep_back((d_q_rows, d_k_rows, d_v_rows))
    d_qkv = d_qkv.astype(jnp.bfloat16)
    grad_qkv = token_sum(normed, d_qkv)
    d_normed = times_rows(d_qkv, qkv_w)
    first_out, first_back = jax.vjp(norm_rows, x_rows, gain_a)
    d_tokens, grad_gain_a = first_back(d_normed)
    d_tokens = d_tokens + d_hidden
    head_sums = lax.psum((grad_q_scale, grad_k_scale), ("seq", "rep"))
    parts = (
        lax.psum_scatter(grad_gain_a, ("seq", "rep"), scatter_dimension=0, tiled=True),
        lax.psum_scatter(grad_qkv, ("seq", "rep"), scatter_dimension=0, tiled=True),
        lax.psum_scatter(grad_out, ("seq", "rep"), scatter_dimension=0, tiled=True),
        lax.psum_scatter(grad_gain_b, ("seq", "rep"), scatter_dimension=0, tiled=True),
        lax.psum_scatter(grad_gate, ("seq", "rep"), scatter_dimension=0, tiled=True),
        lax.psum_scatter(grad_up, ("seq", "rep"), scatter_dimension=0, tiled=True),
        lax.psum_scatter(grad_down, ("seq", "rep"), scatter_dimension=0, tiled=True),
    )
    return (
        activations,
        d_tokens.reshape(rows_dev, len_dev, width),
        parts[0],
        parts[1],
        parts[2],
        parts[3],
        parts[4],
        parts[5],
        parts[6],
        head_sums[0],
        head_sums[1],
    )


MESH = pl.DeviceIdType.MESH
BF = jnp.bfloat16
F32 = jnp.float32
NEG = -1e30
VMEM_BYTES = 63 * 2**20
QS = 5
DZ = 4
BLK = 128
LEN4 = 512
FFS = 896
BR = 64
HALF = 512
AW = 1024
QKV_W = 640
SCALE = HD ** (-0.5)
CHUNKS = ((0, 384), (384, 512))
QKV_M, OUT_M, F0_M, F1_M = range(4)


def place():
    s = lax.axis_index("seq")
    r = lax.axis_index("rep")
    return lax.div(s, 2), lax.rem(s, 2), lax.div(r, 2), lax.rem(r, 2)


def dev(x, c, z, y):
    return {"seq": 2 * x + c, "rep": 2 * z + y}


def flip(v, by):
    return v if by == 0 else 1 - v


def near(z):
    return z + 1 - 2 * lax.rem(z, 2)


def inner(z):
    return (z == 1) | (z == 2)


def send(src, dst, send_sem, recv_sem, target):
    pltpu.make_async_remote_copy(
        src_ref=src,
        dst_ref=dst,
        send_sem=send_sem,
        recv_sem=recv_sem,
        device_id=target,
        device_id_type=MESH,
    ).start()


def arrived(ref, sem):
    pltpu.make_async_copy(ref, ref, sem).wait()


def many(first, count):
    return pl.ds(pl.multiple_of(first, count), count)


def rows_of(ref, index, size):
    return ref.at[many(index * size, size)]


def greet(x, c, z, y):
    found = []
    for dz in range(DZ):
        for dx in range(2):
            for dy in range(2):
                for dc in range(2):
                    if (dx or dy or dc) if dz == 0 else dc == 0:
                        found.append(
                            dev(flip(x, dx), flip(c, dc), lax.rem(z + dz, DZ), flip(y, dy))
                        )
    barrier = pltpu.get_barrier_semaphore()
    for target in found:
        pl.semaphore_signal(barrier, inc=1, device_id=target, device_id_type=MESH)
    return lambda: pl.semaphore_wait(barrier, len(found))


def spread_small(src, spot, ss, rs):
    x, c, z, y = place()
    slot = 2 * x + c
    for k, (dx, dy) in enumerate(((1, 1), (1, 0), (0, 1))):
        send(src, spot, ss.at[k], rs.at[slot, 0], dev(flip(x, dx), y, z, flip(y, dy)))

    @pl.when(c == y)
    def _():
        pltpu.make_async_copy(src, spot, rs.at[slot, 0]).start()

    @pl.when(c != y)
    def _():
        send(src, spot, ss.at[3], rs.at[slot, 0], dev(x, y, z, y))


def spread_start(src, full, ss, rs):
    x, c, z, y = place()
    slot = 2 * x + c
    spot = rows_of(full, slot, BLK)
    send(src, spot, ss.at[0], rs.at[slot, 0], dev(1 - x, y, z, y))
    send(src, spot, ss.at[1], rs.at[slot, 0], dev(x, y, z, 1 - y))

    @pl.when(c == y)
    def _():
        pltpu.make_async_copy(src, spot, rs.at[slot, 0]).start()

    @pl.when(c != y)
    def _():
        send(src, spot, ss.at[2], rs.at[slot, 0], dev(x, y, z, y))


def spread_pass(full, ss, rs):
    x, c, z, y = place()
    for side in range(2):

        @pl.when((c == y) if side == 0 else (c != y))
        def _():
            for k in range(2):
                slot = 2 * ((1 - x) if side == 0 else x) + k
                arrived(rows_of(full, slot, BLK), rs.at[slot, 0])
                half = full.at[many(slot * BLK + side * (BLK // 2), BLK // 2)]
                target = dev(x, c, z, 1 - y) if side == 0 else dev(1 - x, c, z, y)
                send(half, half, ss.at[3 + k], rs.at[slot, side], target)


def spread_wait(full, rs):
    x, c, z, y = place()

    @pl.when(c == y)
    def _():
        for k in range(2):
            arrived(rows_of(full, 0, BLK), rs.at[2 * x + k, 0])

    @pl.when(c != y)
    def _():
        for k in range(2):
            for side in range(2):
                arrived(rows_of(full, 0, BLK // 2), rs.at[2 * (1 - x) + k, side])


def spread_sent(src, ss):
    x, c, z, y = place()
    for k in range(2):
        arrived(src, ss.at[k])
        arrived(src.at[pl.ds(0, BLK // 2)], ss.at[3 + k])

    @pl.when(c != y)
    def _():
        arrived(src, ss.at[2])


def small_wait(block, rs):
    for j in range(4):
        arrived(block, rs.at[j, 0])


def small_sent(src, ss):
    x, c, z, y = place()
    for k in range(3):
        arrived(src, ss.at[k])

    @pl.when(c != y)
    def _():
        arrived(src, ss.at[3])


BLOCK_ORDER = ((1, 1), (1, 0), (0, 1), (0, 0))


def block_at(order):
    x, c, z, y = place()
    dx, dc = BLOCK_ORDER[order]
    return 2 * flip(x, dx) + flip(c, dc)


def collect_halves(partial, helper, ss, hs):
    x, c, z, y = place()

    @pl.when(c != y)
    def _():
        for k in range(2):
            row = (2 * (1 - x) + k) * BLK
            for side, target in enumerate((dev(1 - x, c, z, y), dev(x, c, z, 1 - y))):
                half = partial.at[many(row + side * (BLK // 2), BLK // 2)]
                send(half, helper.at[k], ss.at[2 * k + side], hs.at[k], target)


def collect_near(partial, inbox, ss, rs):
    x, c, z, y = place()

    @pl.when(c == y)
    def _():
        own = rows_of(partial, 2 * x + c, BLK)
        other = rows_of(partial, 2 * x + 1 - c, BLK)
        pltpu.make_async_copy(own, inbox.at[0], rs.at[0]).start()
        send(other, inbox.at[0], ss.at[0], rs.at[0], dev(x, 1 - c, z, y))


def collect_far(partial, helper, inbox, ss, rs, hs):
    x, c, z, y = place()
    for k in range(2):
        arrived(helper.at[k], hs.at[k])
    for side in range(2):

        @pl.when((c != y) if side == 0 else (c == y))
        def _():
            tx = x if side == 0 else 1 - x
            slot = 2 if side == 0 else 1
            for k in range(2):
                row = (2 * tx + k) * BLK
                rows = many(row + side * (BLK // 2), BLK // 2)
                partial[rows, :] = (partial[rows, :].astype(F32) + helper[k].astype(F32)).astype(BF)
                send(
                    partial.at[many(row, BLK)], inbox.at[slot], ss.at[4 + k], rs.at[slot], dev(tx, k, z, c)
                )


def collect_wait(inbox, rs):
    for j in range(3):
        arrived(inbox.at[j], rs.at[j])


def collect_sent(inbox, helper, ss):
    x, c, z, y = place()
    for k in range(2):
        arrived(inbox.at[0], ss.at[4 + k])

    @pl.when(c == y)
    def _():
        arrived(inbox.at[0], ss.at[0])

    @pl.when(c != y)
    def _():
        for k in range(4):
            arrived(helper.at[0], ss.at[k])


def inbox_sum(inbox):
    return inbox[0].astype(F32) + inbox[1].astype(F32) + inbox[2].astype(F32)


def mm(left, right):
    return lax.dot_general(left, right, (((1,), (0,)), ((), ())), preferred_element_type=F32)


def mm_nt(left, right):
    return lax.dot_general(left, right, (((1,), (1,)), ((), ())), preferred_element_type=F32)


def mm_tn(left, right):
    return lax.dot_general(left, right, (((0,), (0,)), ((), ())), preferred_element_type=F32)


def group_of(local_head):
    x, c, z, y = place()
    return jnp.where(local_head + 2 * x + y >= 4, 1, 0)


def layer_body(
    tok, cot, small, wq, wo, wg, wu, wd,
    act_o, dtok_o, end_f, end_a, vr,
    wap, smallf, xf, n1, wav, w3, dyf, n2f, part, inbox, helper, active, dgu,
    qkvt, dqkvt, dqkv, qt, kt, kk, vt, vv, lse, att, cs, grow, hid, blk, dot_s, dkt, dvt,
    help_f, come_f, help_a, come_a, arecv, vec, vecr, gp2,
    sp_ss, sp_rs, co_ss, co_rs, co_hs, w_ss, w_rs, l_ss, l_rs, c_ss, c_rs, g_ss, g_rs, h_ss, h_rs, o_ss, o_rs, p_ss, p_rs, v_ss, v_rs,
    ready,
):
    x, c, z, y = place()
    shard = 2 * x + y
    me = (2 * x + c) * 2 * DZ + 2 * z + y
    mid = inner(z)
    sibling = dev(x, 1 - c, z, y)
    pair, across = near(z), DZ - 1 - z
    far = DZ - 1 - pair
    SMALL, TOK, COT, N2, DAB = range(5)
    OUT, DN, YY, DT = range(4)

    def own_pieces(m, to_shard):
        if m == QKV_M:
            return [wap.at[to_shard, :, pl.ds(0, QKV_W)]]
        if m == OUT_M:
            return [wap.at[to_shard, :, pl.ds(QKV_W, AW - QKV_W)]]
        lo, wide = CHUNKS[m - F0_M]
        lanes = pl.ds(pl.multiple_of(to_shard * FFS + lo, 128), wide)
        return [ref.at[:, lanes] for ref in (wg, wu, wd)]

    def spots(m, rows):
        if m < F0_M:
            return [held(m, rows, BR)]
        lo, wide = CHUNKS[m - F0_M]
        return [w3.at[many(rows, BR), pl.ds(3 * lo + j * wide, wide)] for j in range(3)]

    def held(m, first, count):
        rows = many(first, count)
        if m == QKV_M:
            return wav.at[rows, pl.ds(0, QKV_W)]
        if m == OUT_M:
            return wav.at[rows, pl.ds(QKV_W, AW - QKV_W)]
        lo, wide = CHUNKS[m - F0_M]
        return w3.at[rows, pl.ds(3 * lo, 3 * wide)]

    def weights_start(m):
        for dx, dy in ((1, 1), (1, 0), (0, 1), (0, 0)):
            tx, ty = flip(x, dx), flip(y, dy)
            for src, spot in zip(own_pieces(m, 2 * tx + ty), spots(m, me * BR)):
                if dx or dy:
                    send(src, spot, w_ss.at[m, 2 * dx + dy - 1], w_rs.at[m, shard], dev(tx, c, z, ty))
                else:
                    pltpu.make_async_copy(src, spot, w_rs.at[m, shard]).start()

    def line(m, from_plane, to_plane, k):
        for tx in range(2):
            slab = held(m, ((2 * tx + c) * DZ + from_plane) * 2 * BR, 2 * BR)
            send(slab, slab, l_ss.at[m, 2 * k + tx], l_rs.at[m, 2 * from_plane + tx], dev(x, c, to_plane, y))

    def line_wait(m, plane):
        for tx in range(2):
            arrived(held(m, 0, 2 * BR), l_rs.at[m, 2 * plane + tx])

    def weights_line(m):
        for k in range(4):
            arrived(held(m, 0, BR), w_rs.at[m, k])
        line(m, z, pair, 0)

        @pl.when(mid)
        def _():
            line(m, z, across, 1)

    def weights_pass_near(m):
        @pl.when(mid)
        def _():
            line_wait(m, pair)
            line(m, pair, across, 2)
            line_wait(m, across)
            line(m, across, pair, 3)

    def weights_pass_far(m):
        @pl.when(mid)
        def _():
            line_wait(m, far)
            line(m, far, pair, 4)

    def weights_swap(m):
        @pl.when(jnp.logical_not(mid))
        def _():
            for plane in (pair, far, across):
                line_wait(m, plane)

        for tx in range(2):
            half = held(m, (2 * tx + c) * HALF, HALF)
            send(half, half, c_ss.at[m, tx], c_rs.at[m, tx], sibling)

    def weights_wait(m):
        for tx in range(2):
            arrived(held(m, 0, HALF), c_rs.at[m, tx])

    def weights_sent(m):
        for k in range(3):
            arrived(held(m, 0, BR), w_ss.at[m, k])
        for k in range(2):
            arrived(held(m, 0, 2 * BR), l_ss.at[m, k])

        @pl.when(mid)
        def _():
            for k in range(2, 10):
                arrived(held(m, 0, 2 * BR), l_ss.at[m, k])

        for tx in range(2):
            arrived(held(m, 0, HALF), c_ss.at[m, tx])

    class Grad:
        pass

    def grad(kind, ref, first_row, lo, width, helped, come, final):
        g = Grad()
        lanes = pl.ds(lo, width)
        g.slab = lambda tx, plane: ref.at[many(first_row + (tx * DZ + plane) * 2 * BR, 2 * BR), lanes]
        g.helped, g.come, g.final, g.kind = helped, come, final, kind
        return g

    def start(g):
        k = g.kind

        @pl.when(jnp.logical_not(mid))
        def _():
            for i, plane in enumerate((far, across)):
                for tx in range(2):
                    send(
                        g.slab(tx, plane), g.helped(i, tx), h_ss.at[k, 2 * i + tx], h_rs.at[k, 2 * i + tx],
                        dev(x, c, pair, y),
                    )

        for tx in range(2):
            send(g.slab(tx, pair), g.come(0, tx), o_ss.at[k, tx], o_rs.at[k, tx], dev(x, c, pair, y))

    def join(g, i):
        k = g.kind
        plane = (across, far)[i]

        @pl.when(mid)
        def _():
            for _ in range(1):
                for tx in range(2):
                    rows, more = g.slab(tx, plane), g.helped(i, tx)
                    arrived(more, h_rs.at[k, 2 * i + tx])
                    rows[...] = (rows[...].astype(F32) + more[...].astype(F32)).astype(BF)
                    send(
                        rows, g.come(1, tx), o_ss.at[k, 2 + 2 * i + tx], o_rs.at[k, 2 + tx], dev(x, c, plane, y)
                    )

    def finish(g):
        k = g.kind
        for tx in range(2):
            rows = g.slab(tx, z)
            for i in range(2):
                arrived(rows, o_rs.at[k, 2 * i + tx])
            rows[...] = (
                rows[...].astype(F32) + g.come(0, tx)[...].astype(F32) + g.come(1, tx)[...].astype(F32)
            ).astype(BF)
        for dx, dy in ((1, 1), (1, 0), (0, 1), (0, 0)):
            tx, ty = flip(x, dx), flip(y, dy)
            src = g.slab(tx, z).at[many(ty * BR, BR)]
            if dx or dy:
                send(src, g.final(shard), p_ss.at[k, 2 * dx + dy - 1], p_rs.at[k, shard], dev(tx, c, z, ty))
            else:
                pltpu.make_async_copy(src, g.final(shard), p_rs.at[k, shard]).start()

    def final_wait(g):
        for t in range(4):
            arrived(g.final(0), p_rs.at[g.kind, t])

    def grad_sent(g):
        k = g.kind
        for i in range(3):
            arrived(g.final(0), p_ss.at[k, i])
        for i in range(2):
            arrived(g.slab(0, 0), o_ss.at[k, i])

        @pl.when(mid)
        def _():
            for i in range(2, 6):
                arrived(g.slab(0, 0), o_ss.at[k, i])

        @pl.when(jnp.logical_not(mid))
        def _():
            for i in range(4):
                arrived(g.slab(0, 0), h_ss.at[k, i])

    def ffn_grad(j):
        lo, wide = CHUNKS[j]
        lanes = pl.ds(3 * lo, 3 * wide)
        return grad(
            j, w3, 1024, 3 * lo, 3 * wide,
            lambda i, tx: help_f.at[i, pl.ds(tx * 2 * BR, 2 * BR), lanes],
            lambda i, tx: come_f.at[i, pl.ds(tx * 2 * BR, 2 * BR), lanes],
            lambda t: end_f.at[t, :, lanes],
        )

    GA = grad(
        2, arecv, 0, 0, FFS,
        lambda i, tx: help_a.at[i, pl.ds(tx * 2 * BR, 2 * BR)],
        lambda i, tx: come_a.at[i, pl.ds(tx * 2 * BR, 2 * BR)],
        lambda t: end_a.at[t],
    )
    F0, F1 = ffn_grad(0), ffn_grad(1)

    def collect_step(order, side, kind):
        if order == 1:
            collect_halves(part.at[side], helper.at[side], co_ss.at[kind], co_hs.at[kind])
        if order == 3:
            collect_near(part.at[side], inbox.at[side], co_ss.at[kind], co_rs.at[kind])

    def collect_last(side, kind):
        collect_far(
            part.at[side], helper.at[side], inbox.at[side], co_ss.at[kind], co_rs.at[kind], co_hs.at[kind]
        )

    everyone_here = greet(x, c, z, y)
    turned = jnp.transpose(small[...])
    lane = lax.broadcasted_iota(jnp.int32, (BR, 64), 1)
    gains = jnp.where(lane == 0, turned[0:64, 0:1], jnp.where(lane == 1, turned[0:64, 1:2], 0.0))
    gq, gk, fr = turned[0:64, 2:3], turned[0:64, 3:4], turned[0:32, 5:6]
    for t in range(4):
        wap[t, :, 0:320] = wq[:, 320 * t : 320 * t + 320]
        wap[t, :, 320:448] = wq[:, QW + 64 * t : QW + 64 * t + 128]
        wap[t, :, 448:576] = wq[:, QW + KW + 64 * t : QW + KW + 64 * t + 128]
        wap[t, :, 576:640] = gains.astype(BF)
        wap[t, :, 640:704] = jnp.zeros((BR, 64), BF)
        wap[t, :, 704:1024] = wo[:, 320 * t : 320 * t + 320]
    everyone_here()
    weights_start(QKV_M)
    spot = smallf.at[:, many((2 * x + c) * BLK, BLK)]
    spread_small(small, spot, sp_ss.at[SMALL], sp_rs.at[SMALL])
    weights_start(OUT_M)
    spread_start(tok, xf, sp_ss.at[TOK], sp_rs.at[TOK])
    weights_start(F0_M)
    weights_start(F1_M)
    weights_line(QKV_M)
    weights_line(OUT_M)
    small_wait(spot, sp_rs.at[SMALL])
    seg_row = smallf[4:5, :]
    seg_col = jnp.transpose(smallf[...])[:, 4:5]
    key_at = lax.broadcasted_iota(jnp.int32, (LEN4, LEN4), 0)
    query_at = lax.broadcasted_iota(jnp.int32, (LEN4, LEN4), 1)
    allowed = (key_at <= query_at) & (seg_col == seg_row)
    earlier = jnp.sum(jnp.where(seg_col < seg_row, 1.0, 0.0), axis=0, keepdims=True)
    index = lax.broadcasted_iota(jnp.int32, (1, LEN4), 1).astype(F32)
    angles = fr * (index - earlier)
    cs[0:32, :] = jnp.cos(angles)
    cs[32:64, :] = jnp.sin(angles)
    weights_pass_near(QKV_M)
    weights_pass_near(OUT_M)
    spread_pass(xf, sp_ss.at[TOK], sp_rs.at[TOK])
    weights_line(F0_M)
    weights_pass_far(QKV_M)
    weights_pass_far(OUT_M)
    weights_line(F1_M)
    weights_swap(QKV_M)
    spread_wait(xf, sp_rs.at[TOK])
    spread_start(cot, dyf, sp_ss.at[COT], sp_rs.at[COT])
    weights_wait(QKV_M)
    grow[...] = jnp.transpose(wav[:, 512:640].astype(F32))[64:72, :]

    @pl.loop(0, 4)
    def _(j):
        rows = many(j * BLK, BLK)
        v = xf[rows, :].astype(F32)
        n1[rows, :] = (
            v * lax.rsqrt(jnp.mean(v * v, axis=1, keepdims=True) + norm_eps) * grow[0:1, :]
        ).astype(BF)

    @pl.loop(0, 5)
    def _(j):
        wide = many(j * 128, 128)
        qkvt[wide, :] = jnp.transpose(mm(n1[...], wav[:, wide]))

    def rotated(v, gain):
        cos, sin = cs[0:32, :], cs[32:64, :]
        v = v * lax.rsqrt(jnp.mean(v * v, axis=0, keepdims=True) + norm_eps) * gain
        first, second = v[0:32, :], v[32:64, :]
        return first * cos - second * sin, second * cos + first * sin

    for h in range(QS):
        first, second = rotated(qkvt[h * 64 : h * 64 + 64, :], gq)
        qt[h, 0:32, :] = first.astype(BF)
        qt[h, 32:64, :] = second.astype(BF)
    for g in range(2):
        base = QS * 64 + g * 64
        first, second = rotated(qkvt[base : base + 64, :], gk)
        both = jnp.concatenate([first, second], axis=0)
        kt[g] = both.astype(BF)
        kk[g] = jnp.transpose(both).astype(BF)
        value = qkvt[base + 128 : base + 192, :]
        vt[g] = value.astype(BF)
        vv[g] = jnp.transpose(value).astype(BF)
    weights_swap(OUT_M)
    spread_pass(dyf, sp_ss.at[COT], sp_rs.at[COT])
    dqkvt[0:64, :] = jnp.zeros((64, LEN4), F32)
    for h in range(QS):
        g = group_of(h)
        scores = jnp.where(allowed, mm(kk[g], qt[h]) * SCALE, NEG)
        top = jnp.max(scores, axis=0, keepdims=True)
        weights = jnp.exp(scores - top)
        total = jnp.sum(weights, axis=0, keepdims=True)
        lse[h : h + 1, :] = top + jnp.log(total)
        dqkvt[h * 64 + 64 : h * 64 + 128, :] = mm(vt[g], (weights / total).astype(BF))
    att[...] = jnp.transpose(dqkvt[0:384, :]).astype(BF)
    weights_pass_near(F0_M)
    weights_wait(OUT_M)
    for order in range(4):
        rows = many(block_at(order) * BLK, BLK)
        part[0, rows, :] = mm_nt(att[rows, :], wav[:, QKV_W:AW]).astype(BF)
        collect_step(order, 0, OUT)
    collect_last(0, OUT)
    weights_pass_near(F1_M)
    weights_pass_far(F0_M)
    collect_wait(inbox.at[0], co_rs.at[OUT])
    spread_sent(tok, sp_ss.at[TOK])
    hidden = tok[...].astype(F32) + inbox_sum(inbox.at[0])
    hid[...] = hidden
    blk[0] = (
        hidden
        * lax.rsqrt(jnp.mean(hidden * hidden, axis=1, keepdims=True) + norm_eps)
        * grow[1:2, :]
    ).astype(BF)
    spread_start(blk.at[0], n2f, sp_ss.at[N2], sp_rs.at[N2])
    spread_pass(n2f, sp_ss.at[N2], sp_rs.at[N2])
    weights_pass_far(F1_M)
    weights_swap(F0_M)
    spread_wait(dyf, sp_rs.at[COT])
    spread_wait(n2f, sp_rs.at[N2])
    weights_wait(F0_M)

    def hidden_units(j):
        first, width = CHUNKS[j]
        base = 3 * first
        for lo in range(0, width, 256):
            wide = min(256, width - lo)
            gate = mm(n2f[...], w3[:, base + lo : base + lo + wide])
            upward = mm(n2f[...], w3[:, base + width + lo : base + width + lo + wide])
            grad_in = mm(dyf[...], w3[:, base + 2 * width + lo : base + 2 * width + lo + wide])
            sig = 1.0 / (1.0 + jnp.exp(-gate))
            silu = gate * sig
            active[:, first + lo : first + lo + wide] = (silu * upward).astype(BF)
            at = 2 * first + lo
            dgu[:, at : at + wide] = (grad_in * upward * (sig * (1.0 + gate * (1.0 - sig)))).astype(BF)
            at = at + width
            dgu[:, at : at + wide] = (grad_in * silu).astype(BF)

    def dn_part(j, rows, wide):
        first, width = CHUNKS[j]
        return mm_nt(dgu[rows, 2 * first : 2 * first + 2 * width], w3[wide, 3 * first : 3 * first + 2 * width])

    def y_part(j, rows, wide):
        first, width = CHUNKS[j]
        at = 3 * first + 2 * width
        return mm_nt(active[rows, first : first + width], w3[wide, at : at + width])

    def ffn_grads(j, core, row):
        first, width = CHUNKS[j]
        wide = many((2 * lax.div(row, 2) + core) * HALF + lax.rem(row, 2) * 256, 256)
        return (
            mm_tn(n2f[:, wide], dgu[:, 2 * first : 2 * first + 2 * width]),
            mm_tn(dyf[:, wide], active[:, first : first + width]),
        )

    def chunk_lanes(j):
        first, width = CHUNKS[j]
        return pl.ds(3 * first, 2 * width), pl.ds(3 * first + 2 * width, width), pl.ds(3 * first, 3 * width)

    def grads_swap(j):
        two, one, both = chunk_lanes(j)
        weights_sent(F0_M + j)
        pl.semaphore_signal(ready.at[j], inc=1, device_id=sibling, device_id_type=MESH)

        @pl.loop(0, 4)
        def _(row):
            rows = many(row * 256, 256)
            gu, down = ffn_grads(j, 1 - c, row)
            w3[rows, two] = gu.astype(BF)
            w3[rows, one] = down.astype(BF)

        pl.semaphore_wait(ready.at[j], 1)
        send(
            w3.at[pl.ds(0, 1024), both], w3.at[pl.ds(1024, 1024), both], g_ss.at[j], g_rs.at[j], sibling
        )

    def grads_own(j):
        two, one, both = chunk_lanes(j)
        arrived(w3.at[pl.ds(1024, 1024), both], g_rs.at[j])

        @pl.loop(0, 4)
        def _(row):
            rows = many(1024 + row * 256, 256)
            gu, down = ffn_grads(j, c, row)
            w3[rows, two] = (gu + w3[rows, two].astype(F32)).astype(BF)
            w3[rows, one] = (down + w3[rows, one].astype(F32)).astype(BF)

    every = slice(0, LEN4)
    hidden_units(0)
    collect_sent(inbox.at[0], helper.at[0], co_ss.at[OUT])
    spread_sent(cot, sp_ss.at[COT])

    @pl.loop(0, 4)
    def _(j):
        wide = many(j * 512, 512)
        part[1, :, wide] = dn_part(0, every, wide).astype(BF)
        part[0, :, wide] = y_part(0, every, wide).astype(BF)

    grads_swap(0)
    grads_own(0)
    start(F0)
    weights_swap(F1_M)
    weights_wait(F1_M)
    hidden_units(1)
    for order in range(4):
        rows = many(block_at(order) * BLK, BLK)

        @pl.loop(0, 4)
        def _(j):
            wide = many(j * 512, 512)
            part[1, rows, wide] = (part[1, rows, wide].astype(F32) + dn_part(1, rows, wide)).astype(BF)

        collect_step(order, 1, DN)


    @pl.loop(0, 4)
    def _(j):
        wide = many(j * 512, 512)
        part[0, :, wide] = (part[0, :, wide].astype(F32) + y_part(1, every, wide)).astype(BF)

    collect_last(1, DN)

    grads_swap(1)
    grads_own(1)
    start(F1)
    collect_wait(inbox.at[1], co_rs.at[DN])
    dn = inbox_sum(inbox.at[1])
    h = hid[...]
    r = lax.rsqrt(jnp.mean(h * h, axis=1, keepdims=True) + norm_eps)
    gp2[...] = jnp.broadcast_to(jnp.sum(dn * h * r, axis=0, keepdims=True), gp2.shape)
    a = dn * grow[1:2, :]
    dh = cot[...].astype(F32) + r * (a - h * (r * r * jnp.mean(a * h, axis=1, keepdims=True)))
    dtok_o[...] = dh
    blk[1] = dh.astype(BF)
    spread_start(blk.at[1], xf, sp_ss.at[DAB], sp_rs.at[DAB])
    spread_pass(xf, sp_ss.at[DAB], sp_rs.at[DAB])
    collect_step(1, 0, YY)
    collect_step(3, 0, YY)
    join(F0, 0)
    join(F0, 1)
    def att_grads(core, row):
        wide = many((2 * lax.div(row, 2) + core) * HALF + lax.rem(row, 2) * 256, 256)
        one, two = mm_tn(n1[:, wide], dqkv[...]), mm_tn(xf[:, wide], att[...])
        return one[:, 0:512], one[:, 512:640] + two[:, 0:128], two[:, 128:384]

    def att_grads_swap():
        @pl.loop(0, 4)
        def _(row):
            rows = many(lax.rem(row, 2) * 256, 256)
            side = lax.div(row, 2) * AW
            one, both, two = att_grads(1 - c, row)
            dyf[rows, pl.ds(pl.multiple_of(side, 128), 512)] = one.astype(BF)
            dyf[rows, pl.ds(pl.multiple_of(side + 512, 128), 128)] = both.astype(BF)
            dyf[rows, pl.ds(pl.multiple_of(side + 640, 128), 256)] = two.astype(BF)

        for side in range(2):
            send(
                dyf.at[:, pl.ds(side * AW, FFS)], arecv.at[pl.ds(side * HALF, HALF)],
                g_ss.at[2 + side], g_rs.at[2 + side], sibling,
            )

    def att_grads_own():
        for side in range(2):
            arrived(arecv.at[pl.ds(0, HALF)], g_rs.at[2 + side])

        @pl.loop(0, 4)
        def _(row):
            rows = many(row * 256, 256)
            one, both, two = att_grads(c, row)
            arecv[rows, 0:512] = (one + arecv[rows, 0:512].astype(F32)).astype(BF)
            arecv[rows, 512:640] = (both + arecv[rows, 512:640].astype(F32)).astype(BF)
            arecv[rows, 640:896] = (two + arecv[rows, 640:896].astype(F32)).astype(BF)

    spread_wait(xf, sp_rs.at[DAB])
    dot_s[...] = jnp.transpose(mm(xf[...], wav[:, QKV_W:AW]).astype(BF).astype(F32)).astype(BF)
    dkt[...] = jnp.zeros_like(dkt)
    dvt[...] = jnp.zeros_like(dvt)

    def unrotated(first, second, raw, gain):
        cos, sin = cs[0:32, :], cs[32:64, :]
        d_first = first * cos + second * sin
        d_second = second * cos - first * sin
        d = jnp.concatenate([d_first, d_second], axis=0)
        r = lax.rsqrt(jnp.mean(raw * raw, axis=0, keepdims=True) + norm_eps)
        d_gain = jnp.sum(d * raw * r, axis=1, keepdims=True)
        a = d * gain
        return r * (a - raw * (r * r * jnp.mean(a * raw, axis=0, keepdims=True))), d_gain

    dq_gain = jnp.zeros((64, 1), F32)
    for h in range(QS):
        g = group_of(h)
        scores = mm(kk[g], qt[h]) * SCALE
        p = jnp.where(allowed, jnp.exp(scores - lse[h : h + 1, :]), 0.0)
        d_out = dot_s[h * 64 + 64 : h * 64 + 128, :]
        dvt[g] += mm_nt(d_out, p.astype(BF))
        dp = mm(vv[g], d_out)
        ds = (p * (dp - jnp.sum(p * dp, axis=0, keepdims=True))).astype(BF)
        dkt[g] += mm_nt(qt[h], ds) * SCALE
        dq = (mm(kt[g], ds) * SCALE).astype(BF).astype(F32)
        d, more = unrotated(dq[0:32, :], dq[32:64, :], qkvt[h * 64 : h * 64 + 64, :], gq)
        dq_gain = dq_gain + more
        dqkvt[h * 64 : h * 64 + 64, :] = d
        for g_at, i in JOIN_AFTER.get(h, ()):
            join((F0, F1)[g_at], i)
    dk_gain = jnp.zeros((64, 1), F32)
    for g in range(2):
        base = QS * 64 + g * 64
        dk = dkt[g].astype(BF).astype(F32)
        d, more = unrotated(dk[0:32, :], dk[32:64, :], qkvt[base : base + 64, :], gk)
        dk_gain = dk_gain + more
        dqkvt[base : base + 64, :] = d
        dqkvt[base + 128 : base + 192, :] = dvt[g]
    dqkvt[576:640, :] = jnp.zeros((64, LEN4), F32)
    dqkv[...] = jnp.transpose(dqkvt[...]).astype(BF)
    att_grads_swap()
    collect_sent(inbox.at[1], helper.at[1], co_ss.at[DN])
    for order in range(4):
        rows = many(block_at(order) * BLK, BLK)
        part[1, rows, :] = mm_nt(dqkv[rows, :], wav[:, 0:QKV_W]).astype(BF)
        collect_step(order, 1, DT)

    join(F1, 1)
    att_grads_own()
    start(GA)
    collect_last(1, DT)
    finish(F0)
    collect_last(0, YY)
    collect_wait(inbox.at[0], co_rs.at[YY])
    act_o[...] = (hid[...] + inbox_sum(inbox.at[0])).astype(BF)
    join(GA, 0)
    join(GA, 1)
    finish(F1)
    collect_wait(inbox.at[1], co_rs.at[DT])
    dn = inbox_sum(inbox.at[1])
    xv = tok[...].astype(F32)
    r = lax.rsqrt(jnp.mean(xv * xv, axis=1, keepdims=True) + norm_eps)
    gain_a = jnp.sum(dn * xv * r, axis=0, keepdims=True)
    b = dn * grow[0:1, :]
    dtok_o[...] += r * (b - xv * (r * r * jnp.mean(b * xv, axis=1, keepdims=True)))
    qk = jnp.transpose(
        jnp.concatenate(
            [jnp.broadcast_to(dq_gain, (64, 128)), jnp.broadcast_to(dk_gain, (64, 128))], axis=0
        )
    )
    gain_b = gp2[0:1, :]
    vec[...] = jnp.zeros_like(vec)
    for i in range(4 * DZ):
        for half in range(2):
            at = (((i // (2 * DZ)) * 2 + half) * 2 * DZ + i % (2 * DZ)) * BR
            vec[half, i, 0:4, 0:64] = jnp.concatenate(
                [gain_a[:, at : at + BR], gain_b[:, at : at + BR], qk[0:1, 0:64], qk[0:1, 64:128]], axis=0
            )
    send(vec.at[1 - c], vecr, g_ss.at[6], g_rs.at[6], sibling)
    arrived(vecr, g_rs.at[6])
    vecr[...] += vec[c]
    source = shard * DZ + z
    for dz in range(DZ):
        for dx in range(2):
            for dy in range(2):
                tx, ty, tz = flip(x, dx), flip(y, dy), lax.rem(z + dz, DZ)
                src = vecr.at[(tx * DZ + tz) * 2 + ty]
                k = (dz * 2 + dx) * 2 + dy
                if k == 0:
                    pltpu.make_async_copy(src, vr.at[source], v_rs.at[source]).start()
                else:
                    send(src, vr.at[source], v_ss.at[k], v_rs.at[source], dev(tx, c, tz, ty))
    finish(GA)
    for i in range(4 * DZ):
        arrived(vr.at[0], v_rs.at[i])
    for g in (F0, F1, GA):
        final_wait(g)
    for g in (F0, F1, GA):
        grad_sent(g)
    weights_sent(QKV_M)
    weights_sent(OUT_M)
    for i in range(1, 4 * DZ):
        arrived(vr.at[0], v_ss.at[i])
    for j in range(2):
        arrived(w3.at[pl.ds(0, 1024), chunk_lanes(j)[2]], g_ss.at[j])
    for side in range(2):
        arrived(arecv.at[pl.ds(0, HALF)], g_ss.at[2 + side])
    arrived(vecr, g_ss.at[6])
    small_sent(small, sp_ss.at[SMALL])
    spread_sent(blk.at[0], sp_ss.at[N2])
    spread_sent(blk.at[1], sp_ss.at[DAB])
    collect_sent(inbox.at[0], helper.at[0], co_ss.at[YY])
    collect_sent(inbox.at[1], helper.at[1], co_ss.at[DT])


JOIN_AFTER = {1: ((1, 0),)}


def results_body(
    act, dtok, end_f, end_a, vr, act_o, dtok_o, ga_o, gqkv_o, go_o, gf_o, gate_o, up_o, down_o, gq_o, gk_o
):
    act_o[...] = act[...]
    dtok_o[...] = dtok[...]
    sums = jnp.sum(vr[...], axis=0)
    for i, out in enumerate((ga_o, gf_o, gq_o, gk_o)):
        out[...] = sums[i : i + 1, 0:64]
    for t in range(4):
        for j, out in enumerate((gate_o, up_o, down_o)):
            for first, width in CHUNKS:
                at = 3 * first + j * width
                out[:, t * FFS + first : t * FFS + first + width] = end_f[t, :, at : at + width].astype(F32)
        go_o[:, 320 * t : 320 * t + 320] = end_a[t, :, 576:896].astype(F32)
        gqkv_o[:, 320 * t : 320 * t + 320] = end_a[t, :, 0:320].astype(F32)
    for lo, to in ((320, QW), (448, QW + KW)):
        for g in range(5):
            parts = []
            if g < 4:
                parts.append(end_a[g, :, lo : lo + 64].astype(F32))
            if g > 0:
                parts.append(end_a[g - 1, :, lo + 64 : lo + 128].astype(F32))
            gqkv_o[:, to + 64 * g : to + 64 * g + 64] = sum(parts[1:], parts[0])


def plane_plan(
    tokens, segment_ids, cotangent, attn_gain, w_qkv, w_out, ffn_gain, w_gate, w_up, w_down, q_gain, k_gain
):
    width = tokens.shape[-1]
    freqs = rope_base ** (-jnp.arange(32, dtype=jnp.float32) * 2.0 / HD)

    def lanes(v):
        v = v.astype(F32).reshape(1, -1)
        return jnp.pad(v, ((0, 0), (0, BLK - v.shape[1])))

    small = jnp.concatenate(
        [lanes(v) for v in (attn_gain, ffn_gain, q_gain, k_gain, segment_ids, freqs)]
        + [jnp.zeros((2, BLK), F32)],
        axis=0,
    )
    dma = pltpu.SemaphoreType.DMA
    vm = pltpu.VMEM
    far, close = pl.BlockSpec(memory_space=pl.ANY), pl.BlockSpec(memory_space=pltpu.VMEM)
    halves = pl.pallas_call(
        layer_body,
        out_shape=[
            jax.ShapeDtypeStruct((BLK, width), BF),
            jax.ShapeDtypeStruct((BLK, width), F32),
            jax.ShapeDtypeStruct((4, BR, 3 * FFS), BF),
            jax.ShapeDtypeStruct((4, BR, FFS), BF),
            jax.ShapeDtypeStruct((4 * DZ, 8, BLK), F32),
        ],
        in_specs=[close] * 5 + [far] * 3,
        out_specs=[close] * 2 + [far] * 3,
        scratch_shapes=[
            vm((4, BR, AW), BF),
            vm((8, LEN4), F32),
            vm((LEN4, width), BF),
            vm((LEN4, width), BF),
            vm((2048, AW), BF),
            vm((2048, 3 * FFS), BF),
            vm((LEN4, width), BF),
            vm((LEN4, width), BF),
            vm((2, LEN4, width), BF),
            vm((2, 3, BLK, width), BF),
            vm((2, 2, BLK // 2, width), BF),
            vm((LEN4, FFS), BF),
            vm((LEN4, 2 * FFS), BF),
            vm((QKV_W, LEN4), F32),
            vm((QKV_W, LEN4), F32),
            vm((LEN4, QKV_W), BF),
            vm((QS, 64, LEN4), BF),
            vm((2, 64, LEN4), BF),
            vm((2, LEN4, 64), BF),
            vm((2, 64, LEN4), BF),
            vm((2, LEN4, 64), BF),
            vm((8, LEN4), F32),
            vm((LEN4, 384), BF),
            vm((64, LEN4), F32),
            vm((8, width), F32),
            vm((BLK, width), F32),
            vm((2, BLK, width), BF),
            vm((384, LEN4), BF),
            vm((2, 64, LEN4), F32),
            vm((2, 64, LEN4), F32),
            vm((2, 4 * BR, 3 * FFS), BF),
            vm((2, 4 * BR, 3 * FFS), BF),
            vm((2, 4 * BR, FFS), BF),
            vm((2, 4 * BR, FFS), BF),
            vm((1024, FFS), BF),
            vm((2, 4 * DZ, 8, BLK), F32),
            vm((4 * DZ, 8, BLK), F32),
            vm((8, width), F32),
            dma((5, 5)), dma((5, 4, 2)),
            dma((4, 6)), dma((4, 3)), dma((4, 2)),
            dma((5, 3)), dma((5, 4)), dma((5, 10)), dma((5, 8)),
            dma((5, 2)), dma((5, 2)),
            dma((8,)), dma((8,)),
            dma((5, 4)), dma((5, 4)),
            dma((5, 6)), dma((5, 4)), dma((5, 3)), dma((5, 4)),
            dma((16,)), dma((16,)),
            pltpu.SemaphoreType.REGULAR((2,)),
        ],
        compiler_params=pltpu.CompilerParams(
            collective_id=0, has_side_effects=True, vmem_limit_bytes=VMEM_BYTES
        ),
    )(
        tokens.reshape(BLK, width), cotangent.reshape(BLK, width), small, w_qkv, w_out, w_gate, w_up, w_down
    )
    outs = pl.pallas_call(
        results_body,
        out_shape=[
            jax.ShapeDtypeStruct((BLK, width), BF),
            jax.ShapeDtypeStruct((BLK, width), F32),
            jax.ShapeDtypeStruct((1, BR), F32),
            jax.ShapeDtypeStruct(w_qkv.shape, F32),
            jax.ShapeDtypeStruct(w_out.shape, F32),
            jax.ShapeDtypeStruct((1, BR), F32),
            jax.ShapeDtypeStruct(w_gate.shape, F32),
            jax.ShapeDtypeStruct(w_up.shape, F32),
            jax.ShapeDtypeStruct(w_down.shape, F32),
            jax.ShapeDtypeStruct((1, HD), F32),
            jax.ShapeDtypeStruct((1, HD), F32),
        ],
        in_specs=[close] * 5,
        out_specs=[close] * 11,
        compiler_params=pltpu.CompilerParams(vmem_limit_bytes=60 * 2**20),
    )(*halves)
    shapes = (
        tokens.shape, tokens.shape, (BR,), w_qkv.shape, w_out.shape, (BR,), w_gate.shape, w_up.shape, w_down.shape,
        (HD,), (HD,),
    )
    return tuple(out.reshape(shape) for out, shape in zip(outs, shapes))


def solution(mesh):
    in_specs = (
        P("rep", "seq", None),
        P("rep", "seq"),
        P("rep", "seq", None),
        P(("seq", "rep")),
        P(("seq", "rep"), None),
        P(("seq", "rep"), None),
        P(("seq", "rep")),
        P(("seq", "rep"), None),
        P(("seq", "rep"), None),
        P(("seq", "rep"), None),
        P(),
        P(),
    )
    out_specs = (
        P("rep", "seq", None),
        P("rep", "seq", None),
        P(("seq", "rep")),
        P(("seq", "rep"), None),
        P(("seq", "rep"), None),
        P(("seq", "rep")),
        P(("seq", "rep"), None),
        P(("seq", "rep"), None),
        P(("seq", "rep"), None),
        P(),
        P(),
    )
    planes = mesh.shape["seq"] == 4 and mesh.shape["rep"] == 8
    body = plane_plan if planes else shards
    return jax.shard_map(body, mesh=mesh, in_specs=in_specs, out_specs=out_specs, check_vma=False)
```
